32 devices in a mesh: rep: 4 (over z), fsdp: 8 (over y, x, core).
Axes of the slice: x: 2, y: 2, z: 4, core: 2. Of those that a mesh axis runs over, the one named last changes fastest.
Arguments:
- tokens: bfloat16 [32768, 768], P(('rep', 'fsdp')), may hold values from -6 to 6
- bucket: int32 [32], P(('rep', 'fsdp')), may hold values from 0 to 1
- ln1_gain: bfloat16 [768], P('fsdp'), may hold values from 0.5 to 1.5
- ln1_bias: bfloat16 [768], P('fsdp'), may hold values from -3 to 3
- w_qkv: bfloat16 [768, 2304], P('fsdp'), may hold values from -0.21875 to 0.21875
- w_out: bfloat16 [768, 768], P('fsdp'), may hold values from -1.75 to 1.75
- ln2_gain: bfloat16 [768], P('fsdp'), may hold values from 0.5 to 1.5
- ln2_bias: bfloat16 [768], P('fsdp'), may hold values from -3 to 3
- w_up: bfloat16 [768, 3072], P('fsdp'), may hold values from -0.21875 to 0.21875
- w_down: bfloat16 [3072, 768], P('fsdp'), may hold values from -0.109375 to 0.109375
- cotangent: bfloat16 [32768, 768], P(('rep', 'fsdp')), may hold values from -6 to 6
Outputs:
- mixed: bfloat16 [32768, 768], P(('rep', 'fsdp'))
- tokens_grad: bfloat16 [32768, 768], P(('rep', 'fsdp'))
- ln1_gain_grad: float32 [768], P('fsdp')
- ln1_bias_grad: float32 [768], P('fsdp')
- w_qkv_grad: float32 [768, 2304], P('fsdp')
- w_out_grad: float32 [768, 768], P('fsdp')
- ln2_gain_grad: float32 [768], P('fsdp')
- ln2_bias_grad: float32 [768], P('fsdp')
- w_up_grad: float32 [768, 3072], P('fsdp')
- w_down_grad: float32 [3072, 768], P('fsdp')
The draws below stay inside these ranges and needn't reach their ends.
Inputs may be any that keep to these rules, and one draw needn't show every extreme that they name: bucket is 1 where the device's 1024 tokens are one image and 0 where they are images of 256 tokens in a row.
All inputs are finite; a program needn't handle non-finite values.
Results may differ from the reference program's by a relative error of at most 0.019.
Values may be sent and summed in bfloat16 or wider, within the bound.
No kernel may reach another device: no remote copies, remote signals or barrier semaphores. Data moves between devices by JAX's collectives and lax.ppermute only.
A program may use at most 256 MiB of HBM per device.

```python
import jax
import jax.numpy as jnp
from jax import lax

D = 768
HEADS = 12
HEAD_DIM = 64
FF = 3072
SHORT = 256
TOK_DEV = 1024
TOKENS = 32768
DEVICES = 32


def with_ends(result, rng, least, top_value):
    longest = result.shape.index(max(result.shape))
    spots = []
    for shift in (0, 1):
        where = [jax.random.randint(jax.random.fold_in(rng, axis), (), 0, length) for axis, length in enumerate(result.shape)]
        where[longest] = (where[longest] + shift) % result.shape[longest]
        spots.append(tuple(where))
    return result.at[spots[0]].set(least).at[spots[1]].set(top_value)


def levels(rng, dims, cuts, least, largest):
    def one(dim, shards_of):
        heights = jax.random.uniform(jax.random.fold_in(jax.random.fold_in(rng, 6), dim), (shards_of,), jnp.float32, least / len(cuts), largest / len(cuts))
        return jnp.repeat(jnp.exp(heights), dims[dim] // shards_of).reshape((-1,) + (1,) * (len(dims) - dim - 1))

    gain = one(*cuts[0])
    for cut in cuts[1:]:
        gain = gain * one(*cut)
    return gain


def noise(key, shape, width, most, pieces=(), kind=jnp.bfloat16):
    gain = levels(key, shape, pieces, -0.22, 0.18) if pieces else 1.0
    array = jax.random.normal(key, shape, jnp.float32) * width * gain
    return jnp.minimum(jnp.maximum(array, -most), most).astype(kind)


def setup_inputs(seed: int = 0) -> dict:
    splits = jax.random.split(jax.random.key(seed), 12)
    return {
        "tokens": noise(splits[0], (TOKENS, D), 1.0, 6.0, ((0, 32),)),
        "bucket": with_ends(jax.random.randint(splits[1], (DEVICES,), 0, 2), jax.random.fold_in(splits[1], 1), 0, 1).astype(jnp.int32),
        "ln1_gain": jnp.clip(1.0 + 0.1 * jax.random.normal(splits[2], (D,), jnp.float32), 0.5, 1.5).astype(jnp.bfloat16),
        "ln1_bias": noise(splits[3], (D,), 0.5, 3.0, ((0, 8),)),
        "w_qkv": noise(splits[4], (D, 3 * D), D ** -0.5, 0.21875, ((0, 8),)),
        "w_out": noise(splits[5], (D, D), (D // 64) ** -0.5, 1.75, ((0, 8),)),
        "ln2_gain": jnp.clip(1.0 + 0.1 * jax.random.normal(splits[6], (D,), jnp.float32), 0.5, 1.5).astype(jnp.bfloat16),
        "ln2_bias": noise(splits[7], (D,), 0.5, 3.0, ((0, 8),)),
        "w_up": noise(splits[8], (D, FF), D ** -0.5, 0.21875, ((0, 8),)),
        "w_down": noise(splits[9], (FF, D), FF ** -0.5, 0.109375, ((0, 8),)),
        "cotangent": noise(splits[10], (TOKENS, D), 1.0, 6.0, ((0, 32),)),
    }


@jax.custom_vjp
def low(v):
    return lax.optimization_barrier(v.astype(jnp.bfloat16)).astype(jnp.float32)

@jax.custom_vjp
def low_back(v):
    return v

def low_keep(v):
    return (low(v), None)

def low_pass(kept, grad):
    return (grad,)

def back_keep(v):
    return (v, None)

def back_low(kept, grad):
    return (low(grad),)
low.defvjp(low_keep, low_pass)
low_back.defvjp(back_keep, back_low)
norm_eps = 1e-06
highest = lax.Precision.HIGHEST
masked_score = -1e+30

def norm_rows(values, gain_vec, bias_vec):
    row_mean = lax.optimization_barrier(jnp.mean(values, axis=-1, keepdims=True))
    centred = values - row_mean
    row_var = lax.optimization_barrier(jnp.mean(centred * centred, axis=-1, keepdims=True))
    return centred * lax.rsqrt(row_var + norm_eps) * gain_vec + bias_vec

def layer_forward(inputs, gain_one, bias_one, full_qkv, full_out, gain_two, bias_two, full_up, full_down, allowed):
    row_count = inputs.shape[0]
    normed_one = low(norm_rows(inputs, gain_one, bias_one))
    qkv_value = low_back(low(jnp.dot(normed_one, full_qkv, precision=highest)))
    queries = qkv_value[:, :D].reshape(row_count, HEADS, HEAD_DIM)
    keys_all = qkv_value[:, D:2 * D].reshape(row_count, HEADS, HEAD_DIM)
    values_all = qkv_value[:, 2 * D:].reshape(row_count, HEADS, HEAD_DIM)
    scores = low_back(jnp.einsum('qhd,khd->hqk', queries, keys_all, precision=highest) * HEAD_DIM ** (-0.5))
    scores = jnp.where(allowed[None], scores, masked_score)
    att_probs = low(jax.nn.softmax(scores, axis=-1))
    attended = jnp.einsum('hqk,khd->qhd', att_probs, values_all, precision=highest).reshape(row_count, D)
    attended = low_back(low(attended))
    branch = low_back(jnp.dot(attended, full_out, precision=highest))
    middle = inputs + branch
    normed_two = low(norm_rows(middle, gain_two, bias_two))
    up_value = low_back(jnp.dot(normed_two, full_up, precision=highest))
    act_value = low(jax.nn.gelu(up_value, approximate=False))
    return middle + jnp.dot(act_value, full_down, precision=highest)

def reference(tokens, bucket, ln1_gain, ln1_bias, w_qkv, w_out, ln2_gain, ln2_bias, w_up, w_down, cotangent):
    params = tuple((item.astype(jnp.float32) for item in (ln1_gain, ln1_bias, w_qkv, w_out, ln2_gain, ln2_bias, w_up, w_down)))
    token_blocks = tokens.reshape(-1, TOK_DEV, D)
    cot_blocks = cotangent.reshape(-1, TOK_DEV, D)
    positions = jnp.arange(TOK_DEV, dtype=jnp.int32)

    def device_step(totals, block_item):
        block_tokens, block_cot, is_long = block_item
        segment = jnp.where(is_long == 1, jnp.zeros_like(positions), positions // SHORT).astype(jnp.int32)
        allowed = segment[:, None] == segment[None, :]

        def forward_fn(inputs, *weights):
            return layer_forward(inputs, *weights, allowed)
        mixed_blk, pullback = jax.vjp(forward_fn, block_tokens.astype(jnp.float32), *params)
        gradients = pullback(block_cot.astype(jnp.float32))
        totals = tuple((total + grad_item for total, grad_item in zip(totals, gradients[1:])))
        return (totals, (mixed_blk.astype(jnp.bfloat16), gradients[0].astype(jnp.bfloat16)))
    zero_totals = tuple((jnp.zeros_like(item) for item in params))
    totals, (mixed_all, grads_all) = lax.scan(device_step, zero_totals, (token_blocks, cot_blocks, bucket))
    return (mixed_all.reshape(-1, D), grads_all.reshape(-1, D), totals[0], totals[1], totals[2], totals[3], totals[4], totals[5], totals[6], totals[7])
```

```python
import functools

import jax
import jax.numpy as jnp
from jax import lax
from jax.experimental import pallas as pl
from jax.experimental.pallas import tpu as pltpu
from jax.sharding import PartitionSpec as P

HD=64; SHORT=256; LN_EPS=1e-6
f32=jnp.float32; bf16=jnp.bfloat16
def nt(a,b): return lax.dot_general(a,b,(((1,),(1,)),((),())),preferred_element_type=f32)
def nn(a,b): return lax.dot_general(a,b,(((1,),(0,)),((),())),preferred_element_type=f32)
def tn(a,b): return lax.dot_general(a,b,(((0,),(0,)),((),())),preferred_element_type=f32)

def ln_rows(x,g,b):
    mu=jnp.mean(x,axis=-1,keepdims=True); c=x-mu
    var=jnp.mean(c*c,axis=-1,keepdims=True)
    return c*lax.rsqrt(var+LN_EPS)*g+b

def terms(v):
    hi=v.astype(bf16).astype(f32); r=v-hi
    mid=r.astype(bf16).astype(f32)
    return hi,mid,r-mid

def ext(own,val,lane,base,v3):
    h,m,l=v3
    return jnp.where(own,val,jnp.where(lane==base,h,jnp.where(lane==base+1,m,jnp.where(lane==base+2,l,0.0)))).astype(bf16)

def fwd_kernel(QB,bucket_ref,x_ref,g_ref,b_ref,wq_ref,wk_ref,wv_ref,n1_ref,qe_ref,k_ref,v_ref,att_ref,vx_ref):
    T=x_ref.shape[0]; RB=128
    @pl.when(pl.program_id(0)==0)
    def _():
        def body(i,_):
            r=pl.ds(i*RB,RB)
            n1_ref[r,:]=ln_rows(x_ref[r,:].astype(f32),g_ref[...],b_ref[...]).astype(bf16)
            return 0
        lax.fori_loop(0,T//RB,body,0)
    n1=n1_ref[...]
    lane=lax.broadcasted_iota(jnp.int32,(T,128),1)
    low=lane<64
    q=nn(n1,wq_ref[...])
    for p in range(2):
        qp=q[:,128*p:128*p+128]*0.125
        qe_ref[2*p]=jnp.where(low,qp,0.0).astype(bf16)
        qe_ref[2*p+1]=jnp.where(low,0.0,qp).astype(bf16)
    k_ref[...]=nn(n1,wk_ref[...]).astype(bf16)
    v=nn(n1,wv_ref[...]); v_ref[...]=v.astype(bf16)
    for p in range(2):
        vp=v[:,128*p:128*p+128]
        vx_ref[2*p]=jnp.where(low,vp,1.0).astype(bf16)
        vx_ref[2*p+1]=jnp.where(low,1.0,vp).astype(bf16)
    def block(r,kr):
        laneq=lax.broadcasted_iota(jnp.int32,(r.size,128),1); lowq=laneq<64
        ss=[nt(qe_ref[h,r,:],k_ref[kr,128*(h//2):128*(h//2)+128]) for h in range(4)]
        for p in range(2):
            os=[]
            for j in range(2):
                h=2*p+j
                s=ss[h]
                m=jnp.max(s,axis=-1,keepdims=True)
                e=jnp.exp(s-m).astype(bf16)
                o=nn(e,vx_ref[h,kr,:])
                lse=m+jnp.log(o)
                own=lowq if j==0 else ~lowq
                base=64 if j==0 else 0
                h3=tuple(-t for t in terms(lse))
                qe_ref[h,r,:]=ext(own,qe_ref[h,r,:].astype(f32),laneq,base,h3)
                os.append(o)
            num=jnp.where(lowq,os[0],os[1])
            den=pltpu.roll(jnp.where(lowq,os[1],os[0]),64,1)
            att_ref[r,128*p:128*p+128]=(num/den).astype(bf16)
    long=bucket_ref[0]==1
    @pl.when(long)
    def _():
        def body(i,_):
            block(pl.ds(i*QB,QB),slice(None)); return 0
        lax.fori_loop(0,T//QB,body,0)
    @pl.when(jnp.logical_not(long))
    def _():
        def body(i,_):
            r=pl.ds(i*SHORT,SHORT)
            block(r,r); return 0
        lax.fori_loop(0,T//SHORT,body,0)

def attn_fwd(bucket,x,g,b,w,QB=256):
    T,D=x.shape; G=D//256
    return pl.pallas_call(
        functools.partial(fwd_kernel,QB),
        grid=(G,),
        in_specs=[pl.BlockSpec(memory_space=pltpu.SMEM),
          pl.BlockSpec((T,D),lambda i:(0,0)),pl.BlockSpec((1,D),lambda i:(0,0)),pl.BlockSpec((1,D),lambda i:(0,0)),
          pl.BlockSpec((D,256),lambda i:(0,i)),pl.BlockSpec((D,256),lambda i:(0,i+G)),pl.BlockSpec((D,256),lambda i:(0,i+2*G))],
        out_specs=[pl.BlockSpec((T,D),lambda i:(0,0)),pl.BlockSpec((4,T,128),lambda i:(i,0,0)),
          pl.BlockSpec((T,256),lambda i:(0,i)),pl.BlockSpec((T,256),lambda i:(0,i)),pl.BlockSpec((T,256),lambda i:(0,i))],
        out_shape=[jax.ShapeDtypeStruct((T,D),bf16),jax.ShapeDtypeStruct((D//64,T,128),bf16)]+[jax.ShapeDtypeStruct((T,D),bf16)]*3,
        scratch_shapes=[pltpu.VMEM((4,T,128),bf16)],
        compiler_params=pltpu.CompilerParams(vmem_limit_bytes=48<<20),
        name="attn_fwd",
    )(bucket,x,g,b,w,w,w)

def bwd_kernel(KB,bucket_ref,qe_ref,k_ref,v_ref,att_ref,do_ref,dq_ref,dk_ref,dv_ref,doe_ref,ke_ref,ve_ref,dqa_ref):
    T=k_ref.shape[0]
    lane=lax.broadcasted_iota(jnp.int32,(T,128),1); low=lane<64
    do=do_ref[...].astype(f32)
    prod=do*att_ref[...].astype(f32)
    k=k_ref[...].astype(f32); v=v_ref[...].astype(f32)
    one0=jnp.where(lane<67,1.0,0.0); one1=jnp.where(lane<3,1.0,0.0)
    for j in range(2):
        own=low if j==0 else ~low
        d=jnp.sum(jnp.where(own,prod,0.0),axis=-1,keepdims=True)
        doe_ref[j]=ext(own,do,lane,64 if j==0 else 0,tuple(-t for t in terms(d)))
        ke_ref[j]=jnp.where(own,k,one0 if j==0 else one1).astype(bf16)
        ve_ref[j]=jnp.where(own,v,one0 if j==0 else one1).astype(bf16)
    def block(kr,qr,first):
        lowk=lax.broadcasted_iota(jnp.int32,(kr.size,128),1)<64
        dks=[];dvs=[];dqs=[]
        sts=[nt(ke_ref[j,kr,:],qe_ref[j,qr,:]) for j in range(2)]
        dpts=[nt(ve_ref[j,kr,:],doe_ref[j,qr,:]) for j in range(2)]
        for j in range(2):
            pt=jnp.exp(sts[j])
            ds=(pt*dpts[j]).astype(bf16)
            dvs.append(nn(pt.astype(bf16),do_ref[qr,:]))
            dks.append(nn(ds,qe_ref[j,qr,:]))
            dqs.append(tn(ds,k_ref[kr,:]))
        dk_ref[kr,:]=jnp.where(lowk,dks[0],dks[1]).astype(bf16)
        dv_ref[kr,:]=jnp.where(lowk,dvs[0],dvs[1]).astype(bf16)
        return dqs
    long=bucket_ref[0]==1
    @pl.when(long)
    def _():
        dqa_ref[...]=jnp.zeros_like(dqa_ref)
        def body(i,_):
            dqs=block(pl.ds(i*KB,KB),slice(None),True)
            dqa_ref[...]+=jnp.where(low,dqs[0],dqs[1])
            return 0
        lax.fori_loop(0,T//KB,body,0)
        dq_ref[...]=(dqa_ref[...]*0.125).astype(bf16)
    @pl.when(jnp.logical_not(long))
    def _():
        lows=lax.broadcasted_iota(jnp.int32,(SHORT,128),1)<64
        def body(i,_):
            r=pl.ds(i*SHORT,SHORT)
            dqs=block(r,r,True)
            dq_ref[r,:]=(jnp.where(lows,dqs[0],dqs[1])*0.125).astype(bf16)
            return 0
        lax.fori_loop(0,T//SHORT,body,0)

def attn_bwd(bucket,qe,k,v,att,do,KB=256):
    T,D=k.shape
    col=pl.BlockSpec((T,128),lambda i:(0,i))
    return pl.pallas_call(
        functools.partial(bwd_kernel,KB),
        grid=(D//128,),
        in_specs=[pl.BlockSpec(memory_space=pltpu.SMEM),pl.BlockSpec((2,T,128),lambda i:(i,0,0)),col,col,col,col],
        out_specs=[col]*3,
        out_shape=[jax.ShapeDtypeStruct((T,D),bf16)]*3,
        scratch_shapes=[pltpu.VMEM((2,T,128),bf16)]*3+[pltpu.VMEM((T,128),f32)],
        compiler_params=pltpu.CompilerParams(vmem_limit_bytes=48<<20),
        name="attn_bwd",
    )(bucket,qe,k,v,att,do)

ERF_P=0.43999999999999995*2**-0.5
ERF_C=(0.24822094504462977,0.24887131426512357,0.21731271244932707,0.215814984889486,-0.020185789068163502,0.2966929213019595,-0.2779510917809505,0.07122418451404043)
RPI=(2*3.141592653589793)**-0.5
def gelu_pair(u):
    t=1.0/(1.0+ERF_P*jnp.abs(u))
    e=jnp.exp(-0.5*(u*u))
    q=ERF_C[7]
    for c in ERF_C[6::-1]: q=q*t+c
    tail=(0.5*t)*q*e
    cdf=jnp.where(u>=0,1.0-tail,tail)
    return u*cdf, cdf+u*(e*RPI)

def mlp_kernel(RB,x_ref,att_ref,dy_ref,wo_ref,g_ref,b_ref,wu_ref,wd_ref,
               mid_ref,n2t_ref,mix_ref,gn2_ref,gwu_ref,gwd_ref,n2_ref,macc_ref,act_ref,gup_ref):
    j=pl.program_id(0); T=x_ref.shape[0]
    @pl.when(j==0)
    def _():
        def body(i,_):
            r=pl.ds(i*RB,RB)
            mid=x_ref[r,:].astype(f32)+nn(att_ref[r,:],wo_ref[...])
            mid_ref[r,:]=mid; macc_ref[r,:]=mid
            n2_ref[r,:]=ln_rows(mid,g_ref[...],b_ref[...]).astype(bf16)
            return 0
        lax.fori_loop(0,T//RB,body,0)
        n2t_ref[...]=n2_ref[...].T
        gn2_ref[...]=jnp.zeros_like(gn2_ref)
    def body(i,_):
        r=pl.ds(i*RB,RB)
        up=nn(n2_ref[r,:],wu_ref[...])
        da=nt(dy_ref[r,:],wd_ref[...])
        act,gp=gelu_pair(up)
        act=act.astype(bf16); gup=(da*gp).astype(bf16)
        act_ref[r,:]=act; gup_ref[r,:]=gup
        macc_ref[r,:]+=nn(act,wd_ref[...])
        gn2_ref[r,:]+=nt(gup,wu_ref[...])
        return 0
    lax.fori_loop(0,T//RB,body,0)
    gwd_ref[...]=tn(act_ref[...],dy_ref[...]).astype(bf16)
    gwu_ref[...]=nn(n2t_ref[...],gup_ref[...]).astype(bf16)
    @pl.when(j==pl.num_programs(0)-1)
    def _():
        mix_ref[...]=macc_ref[...].astype(bf16)

def mlp(x,att,dy,wo,g,b,wu,wd,FB=512,RB=512):
    T,D=x.shape; F=wu.shape[1]
    full=lambda s: pl.BlockSpec(s,lambda i:(0,)*len(s))
    return pl.pallas_call(functools.partial(mlp_kernel,RB),grid=(F//FB,),
      in_specs=[full((T,D)),full((T,D)),full((T,D)),full((D,D)),full((1,D)),full((1,D)),pl.BlockSpec((D,FB),lambda i:(0,i)),pl.BlockSpec((FB,D),lambda i:(i,0))],
      out_specs=[full((T,D)),full((D,T)),full((T,D)),full((T,D)),pl.BlockSpec((D,FB),lambda i:(0,i)),pl.BlockSpec((FB,D),lambda i:(i,0))],
      out_shape=[jax.ShapeDtypeStruct((T,D),f32),jax.ShapeDtypeStruct((D,T),bf16),jax.ShapeDtypeStruct((T,D),bf16),jax.ShapeDtypeStruct((T,D),f32),
        jax.ShapeDtypeStruct((D,F),bf16),jax.ShapeDtypeStruct((F,D),bf16)],
      scratch_shapes=[pltpu.VMEM((T,D),bf16),pltpu.VMEM((T,D),f32),pltpu.VMEM((T,FB),bf16),pltpu.VMEM((T,FB),bf16)],
      compiler_params=pltpu.CompilerParams(vmem_limit_bytes=56<<20),name="mlp")(x,att,dy,wo,g,b,wu,wd)

def ln_back(gn,v,gain):
    mu=jnp.mean(v,axis=-1,keepdims=True); c=v-mu
    r=lax.rsqrt(jnp.mean(c*c,axis=-1,keepdims=True)+LN_EPS); xh=c*r
    gg=gn*gain
    dx=r*(gg-jnp.mean(gg,axis=-1,keepdims=True)-xh*jnp.mean(gg*xh,axis=-1,keepdims=True))
    return dx, jnp.sum(gn*xh,axis=0,keepdims=True), jnp.sum(gn,axis=0,keepdims=True)

def mid_kernel(gn2_ref,mid_ref,dy_ref,att_ref,wo_ref,g_ref,gmid_ref,gatt_ref,gwo_ref,gg_ref,gb_ref,gm_ref):
    T=dy_ref.shape[0]; RB=256
    gg_ref[...]=jnp.zeros_like(gg_ref); gb_ref[...]=jnp.zeros_like(gb_ref)
    def body(i,_):
        r=pl.ds(i*RB,RB)
        dx,dg,db=ln_back(gn2_ref[r,:],mid_ref[r,:],g_ref[...])
        gm=dy_ref[r,:].astype(f32)+dx
        gmid_ref[r,:]=gm; gmb=gm.astype(bf16); gm_ref[r,:]=gmb
        gg_ref[...]+=dg; gb_ref[...]+=db
        gatt_ref[r,:]=nt(gmb,wo_ref[...]).astype(bf16)
        return 0
    lax.fori_loop(0,T//RB,body,0)
    gwo_ref[...]=tn(att_ref[...],gm_ref[...]).astype(bf16)
def midk(gn2,mid,dy,att,wo,g):
    T,D=dy.shape
    return pl.pallas_call(mid_kernel,out_shape=[jax.ShapeDtypeStruct((T,D),f32),jax.ShapeDtypeStruct((T,D),bf16),jax.ShapeDtypeStruct((D,D),bf16),jax.ShapeDtypeStruct((1,D),f32),jax.ShapeDtypeStruct((1,D),f32)],
      scratch_shapes=[pltpu.VMEM((T,D),bf16)],compiler_params=pltpu.CompilerParams(vmem_limit_bytes=48<<20),name="midk")(gn2,mid,dy,att,wo,g)

def wq_kernel(n1_ref,dq_ref,dk_ref,dv_ref,gw_ref):
    n1t=n1_ref[...].T
    for i,d in enumerate((dq_ref,dk_ref,dv_ref)):
        gw_ref[i]=nn(n1t,d[...]).astype(bf16)
def wqk(n1,dq,dk,dv):
    T,D=n1.shape
    return pl.pallas_call(wq_kernel,out_shape=jax.ShapeDtypeStruct((3,D,D),bf16),compiler_params=pltpu.CompilerParams(vmem_limit_bytes=48<<20),name="wqk")(n1,dq,dk,dv)

def tail_kernel(x_ref,dq_ref,dk_ref,dv_ref,w_ref,gmid_ref,g_ref,tg_ref,gg_ref,gb_ref):
    T,D=x_ref.shape; RB=256
    gg_ref[...]=jnp.zeros_like(gg_ref); gb_ref[...]=jnp.zeros_like(gb_ref)
    def body(i,_):
        r=pl.ds(i*RB,RB)
        gn=nt(dq_ref[r,:],w_ref[:,:D])+nt(dk_ref[r,:],w_ref[:,D:2*D])+nt(dv_ref[r,:],w_ref[:,2*D:])
        dx,dg,db=ln_back(gn,x_ref[r,:].astype(f32),g_ref[...])
        tg_ref[r,:]=(gmid_ref[r,:]+dx).astype(bf16)
        gg_ref[...]+=dg; gb_ref[...]+=db
        return 0
    lax.fori_loop(0,T//RB,body,0)
def tailk(x,dq,dk,dv,w,gmid,g):
    T,D=x.shape
    return pl.pallas_call(tail_kernel,out_shape=[jax.ShapeDtypeStruct((T,D),bf16),jax.ShapeDtypeStruct((1,D),f32),jax.ShapeDtypeStruct((1,D),f32)],
      compiler_params=pltpu.CompilerParams(vmem_limit_bytes=48<<20),name="tailk")(x,dq,dk,dv,w,gmid,g)


def gather(v):
    return lax.all_gather(v, "fsdp", axis=0, tiled=True)


def scatter_sum(v):
    part = lax.psum_scatter(v.astype(bf16), "fsdp", scatter_dimension=0, tiled=True)
    return lax.psum(part, "rep").astype(f32)


def shards(tokens, bucket, ln1_gain, ln1_bias, w_qkv, w_out, ln2_gain, ln2_bias, w_up, w_down, cotangent):
    width = tokens.shape[1]
    norms = lax.all_gather(jnp.stack([ln1_gain, ln1_bias, ln2_gain, ln2_bias]), "fsdp", axis=1, tiled=True).astype(f32)
    gain_one, bias_one, gain_two, bias_two = (norms[i : i + 1] for i in range(4))
    full_qkv, full_out, full_up, full_down = (gather(w) for w in (w_qkv, w_out, w_up, w_down))
    normed_one, q_ext, keys, values, attended = attn_fwd(bucket, tokens, gain_one, bias_one, full_qkv)
    middle, _, mixed, grad_n2, gw_up, gw_down = mlp(
        tokens, attended, cotangent, full_out, gain_two, bias_two, full_up, full_down
    )
    grad_mid, grad_att, gw_out, g_gain2, g_bias2 = midk(grad_n2, middle, cotangent, attended, full_out, gain_two)
    gq, gk, gv = attn_bwd(bucket, q_ext, keys, values, attended, grad_att)
    gw_qkv = wqk(normed_one, gq, gk, gv)
    tokens_grad, g_gain1, g_bias1 = tailk(tokens, gq, gk, gv, full_qkv, grad_mid, gain_one)
    g_norms = jnp.concatenate([g_gain1, g_bias1, g_gain2, g_bias2], axis=0)
    g_norms = lax.psum(lax.psum_scatter(g_norms, "fsdp", scatter_dimension=1, tiled=True), "rep")
    return (
        mixed,
        tokens_grad,
        g_norms[0],
        g_norms[1],
        scatter_sum(gw_qkv.transpose(1, 0, 2).reshape(width, 3 * width)),
        scatter_sum(gw_out),
        g_norms[2],
        g_norms[3],
        scatter_sum(gw_up),
        scatter_sum(gw_down),
    )


def solution(mesh):
    return jax.shard_map(
        shards,
        mesh=mesh,
        in_specs=(
            P(("rep", "fsdp"), None),
            P(("rep", "fsdp")),
            P("fsdp"),
            P("fsdp"),
            P("fsdp", None),
            P("fsdp", None),
            P("fsdp"),
            P("fsdp"),
            P("fsdp", None),
            P("fsdp", None),
            P(("rep", "fsdp"), None),
        ),
        out_specs=(
            P(("rep", "fsdp"), None),
            P(("rep", "fsdp"), None),
            P("fsdp"),
            P("fsdp"),
            P("fsdp", None),
            P("fsdp", None),
            P("fsdp"),
            P("fsdp"),
            P("fsdp", None),
            P("fsdp", None),
        ),
        check_vma=False,
    )
```

```python
import functools

import jax
import jax.numpy as jnp
from jax import lax
from jax.experimental import pallas as pl
from jax.experimental.pallas import tpu as pltpu
from jax.sharding import PartitionSpec as P

HEAD_DIM = 64
SHORT = 256
LN_EPS = 1e-6
LANES = 128
CHUNKS = 3
f32 = jnp.float32
bf16 = jnp.bfloat16

ERF_P = 0.43999999999999995 * 2**-0.5
ERF_C = (
    0.24822094504462977,
    0.24887131426512357,
    0.21731271244932707,
    0.215814984889486,
    -0.020185789068163502,
    0.2966929213019595,
    -0.2779510917809505,
    0.07122418451404043,
)
ROOT_2PI = (2 * 3.141592653589793) ** -0.5


def nt(a, b):
    return lax.dot_general(a, b, (((1,), (1,)), ((), ())), preferred_element_type=f32)


def nn(a, b):
    return lax.dot_general(a, b, (((1,), (0,)), ((), ())), preferred_element_type=f32)


def tn(a, b):
    return lax.dot_general(a, b, (((0,), (0,)), ((), ())), preferred_element_type=f32)


def ln_rows(x, gain, bias):
    centred = x - jnp.mean(x, axis=-1, keepdims=True)
    var = jnp.mean(centred * centred, axis=-1, keepdims=True)
    return centred * lax.rsqrt(var + LN_EPS) * gain + bias


def ln_back(grad, v, gain):
    centred = v - jnp.mean(v, axis=-1, keepdims=True)
    r = lax.rsqrt(jnp.mean(centred * centred, axis=-1, keepdims=True) + LN_EPS)
    xh = centred * r
    gg = grad * gain
    dx = r * (gg - jnp.mean(gg, axis=-1, keepdims=True) - xh * jnp.mean(gg * xh, axis=-1, keepdims=True))
    return dx, jnp.sum(grad * xh, axis=0, keepdims=True), jnp.sum(grad, axis=0, keepdims=True)


def gelu_pair(u):
    t = 1.0 / (1.0 + ERF_P * jnp.abs(u))
    e = jnp.exp(-0.5 * (u * u))
    q = ERF_C[7]
    for c in ERF_C[6::-1]:
        q = q * t + c
    tail = (0.5 * t) * q * e
    cdf = jnp.where(u >= 0, 1.0 - tail, tail)
    return u * cdf, cdf + u * (e * ROOT_2PI)


def terms(v):
    hi = v.astype(bf16).astype(f32)
    r = v - hi
    mid = r.astype(bf16).astype(f32)
    return hi, mid, r - mid


def ext(own, val, lane, base, three):
    h, m, l = three
    rest = jnp.where(lane == base, h, jnp.where(lane == base + 1, m, jnp.where(lane == base + 2, l, 0.0)))
    return jnp.where(own, val, rest).astype(bf16)


def blocked(w):
    rows, cols = w.shape
    return w.reshape(rows, cols // LANES, LANES).transpose(1, 0, 2).reshape(-1, LANES)


def unblocked(p, rows):
    return p.reshape(-1, rows, LANES).transpose(1, 0, 2).reshape(rows, -1)


class Seg:
    def __init__(self, start, nb, rows, b0=0):
        self.start, self.nb, self.rows, self.b0 = start, nb, rows, b0

    def cut(self, lo, hi):
        a, b = max(lo, self.start), min(hi, self.start + self.nb * self.rows)
        if a >= b:
            return None
        return Seg(a - lo, (b - a) // self.rows, self.rows, self.b0 + (a - self.start) // self.rows)


def unpack(parts, me, jobs, sem):
    copies = []
    for ref, r, lo in parts:
        hi = lo + ref.shape[0]
        for seg, dst in jobs:
            s = seg.cut(lo, hi)
            if s is None:
                continue
            row = (me ^ r) * s.rows if r is not None else 0
            for b in range(s.nb):
                copies.append(
                    pltpu.make_async_copy(
                        ref.at[pl.ds(s.start + b * s.rows, s.rows), :],
                        dst.at[s.b0 + b, pl.ds(pl.multiple_of(row, 16), s.rows), :],
                        sem.at[len(copies)],
                    )
                )
    return copies


def pack(dsts, me, jobs, sem):
    copies = []
    for r, (ref, slot) in enumerate(dsts):
        for seg, src in jobs:
            row = (me ^ r) * seg.rows if len(dsts) > 1 else 0
            for b in range(seg.nb):
                copies.append(
                    pltpu.make_async_copy(
                        src.at[seg.b0 + b, pl.ds(pl.multiple_of(row, 16), seg.rows), :],
                        ref.at[slot, pl.ds(seg.start + b * seg.rows, seg.rows), :],
                        sem.at[len(copies)],
                    )
                )
    return copies


def run(copies):
    for c in copies:
        c.start()
    for c in copies:
        c.wait()


def blocks(ref, lo, n):
    return jnp.concatenate([ref[lo + i] for i in range(n)], axis=1)


def params(mib):
    return pltpu.CompilerParams(vmem_limit_bytes=mib << 20)


SMEM = pl.BlockSpec(memory_space=pltpu.SMEM)
VMEM = pl.BlockSpec(memory_space=pltpu.VMEM)
ANY = pl.BlockSpec(memory_space=pl.ANY)


def fwd_kernel(plan, qb, n_parts, *refs):
    bucket_ref, me_ref, x_ref = refs[:3]
    part_refs = refs[3 : 3 + n_parts]
    n1_ref, qe_ref, k_ref, v_ref, att_ref, norm_ref, w_ref, raw_ref, vx_ref, sem = refs[3 + n_parts :]
    rows, width = x_ref.shape
    groups = width // 256
    g = pl.program_id(0)

    @pl.when(g == 0)
    def _():
        parts = [(ref, r, lo) for ref, (r, lo) in zip(part_refs, plan["parts"])]
        run(unpack(parts, me_ref[0], [(plan["qkv"], w_ref), (plan["norm"], raw_ref)], sem))
        raw = raw_ref[...].astype(f32)
        total = raw[:, 0:16]
        for i in range(1, raw.shape[1] // 16):
            total = total + raw[:, 16 * i : 16 * i + 16]
        norm_ref[...] = jnp.concatenate([total[b] for b in range(width // LANES)], axis=1)

        def body(i, _):
            r = pl.ds(i * 128, 128)
            n1_ref[r, :] = ln_rows(x_ref[r, :].astype(f32), norm_ref[0:1, :], norm_ref[1:2, :]).astype(bf16)
            return 0

        lax.fori_loop(0, rows // 128, body, 0)

    n1 = n1_ref[...]
    low = lax.broadcasted_iota(jnp.int32, (rows, 128), 1) < 64
    q = nn(n1, blocks(w_ref, 2 * g, 2))
    k_ref[...] = nn(n1, blocks(w_ref, 2 * groups + 2 * g, 2)).astype(bf16)
    v = nn(n1, blocks(w_ref, 4 * groups + 2 * g, 2))
    v_ref[...] = v.astype(bf16)
    for p in range(2):
        qp = q[:, 128 * p : 128 * p + 128] * HEAD_DIM**-0.5
        vp = v[:, 128 * p : 128 * p + 128]
        qe_ref[2 * p] = jnp.where(low, qp, 0.0).astype(bf16)
        qe_ref[2 * p + 1] = jnp.where(low, 0.0, qp).astype(bf16)
        vx_ref[2 * p] = jnp.where(low, vp, 1.0).astype(bf16)
        vx_ref[2 * p + 1] = jnp.where(low, 1.0, vp).astype(bf16)

    def block(r, kr):
        lane = lax.broadcasted_iota(jnp.int32, (r.size, 128), 1)
        lowq = lane < 64
        ss = [nt(qe_ref[h, r, :], k_ref[kr, 128 * (h // 2) : 128 * (h // 2) + 128]) for h in range(4)]
        for p in range(2):
            os = []
            for j in range(2):
                h = 2 * p + j
                top = jnp.max(ss[h], axis=-1, keepdims=True)
                e = jnp.exp(ss[h] - top).astype(bf16)
                o = nn(e, vx_ref[h, kr, :])
                lse = top + jnp.log(o)
                own = lowq if j == 0 else ~lowq
                three = tuple(-t for t in terms(lse))
                qe_ref[h, r, :] = ext(own, qe_ref[h, r, :].astype(f32), lane, 64 - 64 * j, three)
                os.append(o)
            num = jnp.where(lowq, os[0], os[1])
            den = pltpu.roll(jnp.where(lowq, os[1], os[0]), 64, 1)
            att_ref[r, 128 * p : 128 * p + 128] = (num / den).astype(bf16)

    is_long = bucket_ref[0] == 1

    @pl.when(is_long)
    def _():
        def body(i, _):
            block(pl.ds(i * qb, qb), slice(None))
            return 0

        lax.fori_loop(0, rows // qb, body, 0)

    @pl.when(jnp.logical_not(is_long))
    def _():
        def body(i, _):
            r = pl.ds(i * SHORT, SHORT)
            block(r, r)
            return 0

        lax.fori_loop(0, rows // SHORT, body, 0)


def forward(bucket, me, x, parts, plan):
    rows, width = x.shape
    groups = width // 256
    nsh = plan["shards"]
    full = pl.BlockSpec((rows, width), lambda i: (0, 0))
    col = pl.BlockSpec((rows, 256), lambda i: (0, i))
    act = jax.ShapeDtypeStruct((rows, width), bf16)
    return pl.pallas_call(
        functools.partial(fwd_kernel, plan, 512, len(parts)),
        grid=(groups,),
        in_specs=[SMEM, SMEM, full] + [ANY] * len(parts),
        out_specs=[
            full,
            pl.BlockSpec((4, rows, 128), lambda i: (i, 0, 0)),
            col,
            col,
            col,
            pl.BlockSpec((16, width), lambda i: (0, 0)),
        ],
        out_shape=[
            act,
            jax.ShapeDtypeStruct((width // HEAD_DIM, rows, 128), bf16),
            act,
            act,
            act,
            jax.ShapeDtypeStruct((16, width), f32),
        ],
        scratch_shapes=[
            pltpu.VMEM((6 * groups, width, 128), bf16),
            pltpu.VMEM((width // 128, 16 * nsh, 128), bf16),
            pltpu.VMEM((4, rows, 128), bf16),
            pltpu.SemaphoreType.DMA((256,)),
        ],
        compiler_params=params(44),
        cost_estimate=pl.CostEstimate(flops=16 * 10**9, bytes_accessed=14 << 20, transcendentals=12 << 20),
        name="attn_fwd",
    )(bucket, me, x, *[p for p in parts])


def bwd_kernel(kb, bucket_ref, qe_ref, k_ref, v_ref, att_ref, do_ref, dq_ref, dk_ref, dv_ref, doe_ref, ke_ref, ve_ref, dqa_ref):
    rows = k_ref.shape[0]
    lane = lax.broadcasted_iota(jnp.int32, (rows, 128), 1)
    low = lane < 64
    do = do_ref[...].astype(f32)
    prod = do * att_ref[...].astype(f32)
    k = k_ref[...].astype(f32)
    v = v_ref[...].astype(f32)
    for j in range(2):
        own = low if j == 0 else ~low
        base = 64 - 64 * j
        ones = jnp.where((lane >= base) & (lane < base + 3), 1.0, 0.0)
        d = jnp.sum(jnp.where(own, prod, 0.0), axis=-1, keepdims=True)
        doe_ref[j] = ext(own, do, lane, base, tuple(-t for t in terms(d)))
        ke_ref[j] = jnp.where(own, k, ones).astype(bf16)
        ve_ref[j] = jnp.where(own, v, ones).astype(bf16)

    def block(kr, qr):
        lowk = lax.broadcasted_iota(jnp.int32, (kr.size, 128), 1) < 64
        dks, dvs, dqs = [], [], []
        sts = [nt(ke_ref[j, kr, :], qe_ref[j, qr, :]) for j in range(2)]
        dpts = [nt(ve_ref[j, kr, :], doe_ref[j, qr, :]) for j in range(2)]
        for j in range(2):
            pt = jnp.exp(sts[j])
            ds = (pt * dpts[j]).astype(bf16)
            dvs.append(nn(pt.astype(bf16), do_ref[qr, :]))
            dks.append(nn(ds, qe_ref[j, qr, :]))
            dqs.append(tn(ds, k_ref[kr, :]))
        dk_ref[kr, :] = jnp.where(lowk, dks[0], dks[1]).astype(bf16)
        dv_ref[kr, :] = jnp.where(lowk, dvs[0], dvs[1]).astype(bf16)
        return dqs

    is_long = bucket_ref[0] == 1

    @pl.when(is_long)
    def _():
        dqa_ref[...] = jnp.zeros_like(dqa_ref)

        def body(i, _):
            dqs = block(pl.ds(i * kb, kb), slice(None))
            dqa_ref[...] += jnp.where(low, dqs[0], dqs[1])
            return 0

        lax.fori_loop(0, rows // kb, body, 0)
        dq_ref[...] = (dqa_ref[...] * HEAD_DIM**-0.5).astype(bf16)

    @pl.when(jnp.logical_not(is_long))
    def _():
        lows = lax.broadcasted_iota(jnp.int32, (SHORT, 128), 1) < 64

        def body(i, _):
            r = pl.ds(i * SHORT, SHORT)
            dqs = block(r, r)
            dq_ref[r, :] = (jnp.where(lows, dqs[0], dqs[1]) * HEAD_DIM**-0.5).astype(bf16)
            return 0

        lax.fori_loop(0, rows // SHORT, body, 0)


def attn_bwd(bucket, qe, k, v, att, do):
    rows, width = k.shape
    col = pl.BlockSpec((rows, 128), lambda i: (0, i))
    return pl.pallas_call(
        functools.partial(bwd_kernel, 512),
        grid=(width // 128,),
        in_specs=[SMEM, pl.BlockSpec((2, rows, 128), lambda i: (i, 0, 0)), col, col, col, col],
        out_specs=[col] * 3,
        out_shape=[jax.ShapeDtypeStruct((rows, width), bf16)] * 3,
        scratch_shapes=[pltpu.VMEM((2, rows, 128), bf16)] * 3 + [pltpu.VMEM((rows, 128), f32)],
        compiler_params=params(44),
        cost_estimate=pl.CostEstimate(flops=30 * 10**9, bytes_accessed=14 << 20, transcendentals=12 << 20),
        name="attn_bwd",
    )(bucket, qe, k, v, att, do)


def packet_dsts(refs, nsh):
    if nsh == 1:
        return [(refs[0], 0)]
    keep, send = refs
    return [((send if r & 1 else keep), r >> 1) for r in range(nsh)]


def mlp_rows(r, n2_ref, dy_ref, wu, wd, macc_ref, gn2_ref, act_ref, gup_ref):
    n_up, n_dn = wu.shape[0], wd.shape[0]
    w_up = blocks(wu, 0, n_up)
    w_dn = blocks(wd, 0, n_dn)
    up = nn(n2_ref[r, :], w_up)
    da = nt(dy_ref[r, :], w_dn)
    act, gp = gelu_pair(up)
    act = act.astype(bf16)
    gup = (da * gp).astype(bf16)
    act_ref[r, :] = act
    gup_ref[r, :] = gup
    macc_ref[r, :] += nn(act, w_dn)
    gn2_ref[r, :] += nt(gup, w_up)


def mlp_grads(plan, me, n2t_ref, dy_ref, act_ref, gup_ref, gu_ref, gd_ref, outs, sem):
    for b in range(gu_ref.shape[0] // 2):
        g = nn(n2t_ref[...], gup_ref[:, 256 * b : 256 * b + 256]).astype(bf16)
        gu_ref[2 * b] = g[:, :128]
        gu_ref[2 * b + 1] = g[:, 128:]
    for b in range(gd_ref.shape[1] // 256):
        g = tn(act_ref[:, 256 * b : 256 * b + 256], dy_ref[...]).astype(bf16)
        for i in range(gd_ref.shape[0]):
            gd_ref[i, 256 * b : 256 * b + 256, :] = g[:, 128 * i : 128 * i + 128]
    run(pack(packet_dsts(outs, plan["shards"]), me, [(plan["g_up"], gu_ref), (plan["g_down"], gd_ref)], sem))


def mlp_kernel(plan, rb, n_parts, n_out, first, last, *refs):
    it = iter(refs)
    take = lambda n: [next(it) for _ in range(n)]
    (me_ref,) = take(1)
    if first:
        x_ref, att_ref, norm_ref = take(3)
    else:
        n2_ref, n2t_ref, macc_in, gn2_in = take(4)
    (dy_ref,) = take(1)
    part_refs = take(n_parts)
    if first:
        mid_ref, n2_ref, n2t_ref, wo_ref = take(4)
    (macc_ref, gn2_ref) = take(2)
    outs = take(n_out)
    wu, wd, act_ref, gup_ref, gu_ref, gd_ref = take(6)
    acc_ref = take(1)[0] if last else macc_ref
    (sem,) = take(1)
    rows = dy_ref.shape[0]
    me = me_ref[0]
    parts = [(ref, r, lo) for ref, (r, lo) in zip(part_refs, plan["parts"])]
    jobs = [(plan["up"], wu), (plan["down"], wd)] + ([(plan["out"], wo_ref)] if first else [])
    run(unpack(parts, me, jobs, sem))
    if not first:
        acc_ref[...] = macc_in[...]
        gn2_ref[...] = gn2_in[...]

    def body(i, _):
        r = pl.ds(i * rb, rb)
        if first:
            mid = x_ref[r, :].astype(f32) + nn(att_ref[r, :], blocks(wo_ref, 0, wo_ref.shape[0]))
            mid_ref[r, :] = mid
            acc_ref[r, :] = mid
            n2_ref[r, :] = ln_rows(mid, norm_ref[2:3, :], norm_ref[3:4, :]).astype(bf16)
            gn2_ref[r, :] = jnp.zeros_like(mid)
        mlp_rows(r, n2_ref, dy_ref, wu, wd, acc_ref, gn2_ref, act_ref, gup_ref)
        return 0

    lax.fori_loop(0, rows // rb, body, 0)
    if first:
        n2t_ref[...] = n2_ref[...].T
    if last:
        macc_ref[...] = acc_ref[...].astype(bf16)
    mlp_grads(plan, me, n2t_ref, dy_ref, act_ref, gup_ref, gu_ref, gd_ref, outs, sem)


def packet_outs(plan, extra=0):
    nsh = plan["shards"]
    shape = (1 if nsh == 1 else nsh // 2, plan["g_rows"] + extra, LANES)
    return [jax.ShapeDtypeStruct(shape, bf16)] * (1 if nsh == 1 else 2)


def mlp(plan, me, first, last, heads, dy, parts, extra=0):
    rows, width = dy.shape
    n_up, n_dn = plan["up"].nb, plan["down"].nb
    k_dn = plan["shards"] * plan["down"].rows
    outs = packet_outs(plan, extra)
    shape = jax.ShapeDtypeStruct
    out_shape = []
    if first:
        out_shape += [shape((rows, width), f32), shape((rows, width), bf16), shape((width, rows), bf16)]
        out_shape += [shape((width // LANES, width, LANES), bf16)]
    out_shape += [shape((rows, width), bf16 if last else f32), shape((rows, width), f32)]
    n_local = len(out_shape)
    scratch = [
        pltpu.VMEM((n_up, width, LANES), bf16),
        pltpu.VMEM((n_dn, k_dn, LANES), bf16),
        pltpu.VMEM((rows, k_dn), bf16),
        pltpu.VMEM((rows, k_dn), bf16),
        pltpu.VMEM((n_up, width, LANES), bf16),
        pltpu.VMEM((n_dn, k_dn, LANES), bf16),
    ]
    if last:
        scratch.append(pltpu.VMEM((rows, width), f32))
    scratch.append(pltpu.SemaphoreType.DMA((256,)))
    return pl.pallas_call(
        functools.partial(mlp_kernel, plan, 512, len(parts), len(outs), first, last),
        in_specs=[SMEM] + [VMEM] * (len(heads) + 1) + [ANY] * len(parts),
        out_specs=[VMEM] * n_local + [ANY] * len(outs),
        out_shape=out_shape + outs,
        scratch_shapes=scratch,
        compiler_params=params(52),
        cost_estimate=pl.CostEstimate(flops=12 * 10**9, bytes_accessed=18 << 20, transcendentals=2 << 20),
        name="mlp_first" if first else "mlp_last" if last else "mlp_mid",
    )(me, *heads, dy, *parts)


def mid_kernel(plan, n_pk, *refs):
    me_ref, gn2_ref, mid_ref, dy_ref, att_ref, wo_ref, norm_ref = refs[:7]
    gmid_ref, gatt_ref, gg_ref = refs[7 + n_pk : 10 + n_pk]
    outs = refs[10 + n_pk : 10 + 2 * n_pk]
    gm_ref, go_ref, sem = refs[10 + 2 * n_pk :]
    rows = dy_ref.shape[0]
    gg_ref[...] = jnp.zeros_like(gg_ref)
    w_out = blocks(wo_ref, 0, wo_ref.shape[0])

    def body(i, _):
        r = pl.ds(i * 256, 256)
        dx, dg, db = ln_back(gn2_ref[r, :], mid_ref[r, :], norm_ref[2:3, :])
        gm = dy_ref[r, :].astype(f32) + dx
        gmid_ref[r, :] = gm
        gmb = gm.astype(bf16)
        gm_ref[r, :] = gmb
        gg_ref[0:1, :] += dg
        gg_ref[1:2, :] += db
        gatt_ref[r, :] = nt(gmb, w_out).astype(bf16)
        return 0

    lax.fori_loop(0, rows // 256, body, 0)
    g = tn(att_ref[...], gm_ref[...]).astype(bf16)
    for b in range(go_ref.shape[0]):
        go_ref[b] = g[:, LANES * b : LANES * b + LANES]
    run(pack(packet_dsts(outs, plan["shards"]), me_ref[0], [(plan["g_out"], go_ref)], sem))


def mid_bwd(plan, me, gn2, mid, dy, att, wo, norms, packets):
    rows, width = dy.shape
    shape = jax.ShapeDtypeStruct
    n = len(packets)
    return pl.pallas_call(
        functools.partial(mid_kernel, plan, n),
        in_specs=[SMEM] + [VMEM] * 6 + [ANY] * n,
        out_specs=[VMEM] * 3 + [ANY] * n,
        out_shape=[shape((rows, width), f32), shape((rows, width), bf16), shape((8, width), f32)]
        + [shape(p.shape, p.dtype) for p in packets],
        input_output_aliases={7 + i: 3 + i for i in range(n)},
        scratch_shapes=[
            pltpu.VMEM((rows, width), bf16),
            pltpu.VMEM((width // LANES, width, LANES), bf16),
            pltpu.SemaphoreType.DMA((64,)),
        ],
        compiler_params=params(48),
        cost_estimate=pl.CostEstimate(flops=6 * 10**9, bytes_accessed=16 << 20, transcendentals=0),
        name="mid_bwd",
    )(me, gn2, mid, dy, att, wo, norms, *packets)


def wqkv_kernel(plan, n_out, *refs):
    me_ref, n1_ref = refs[:2]
    ds = refs[2:5]
    outs = refs[5 : 5 + n_out]
    gw_ref, sem = refs[5 + n_out :]
    n1t = n1_ref[...].T
    per = ds[0].shape[1] // LANES
    for i, d in enumerate(ds):
        g = nn(n1t, d[...]).astype(bf16)
        for b in range(per):
            gw_ref[i * per + b] = g[:, LANES * b : LANES * b + LANES]
    run(pack(packet_dsts(outs, plan["shards"]), me_ref[0], [(plan["g_qkv"], gw_ref)], sem))


def wqkv_grad(plan, me, n1, dq, dk, dv):
    width = n1.shape[1]
    outs = packet_outs(plan)
    return pl.pallas_call(
        functools.partial(wqkv_kernel, plan, len(outs)),
        in_specs=[SMEM] + [VMEM] * 4,
        out_specs=[ANY] * len(outs),
        out_shape=outs,
        scratch_shapes=[pltpu.VMEM((plan["g_qkv"].nb, width, LANES), bf16), pltpu.SemaphoreType.DMA((256,))],
        compiler_params=params(48),
        cost_estimate=pl.CostEstimate(flops=4 * 10**9, bytes_accessed=10 << 20, transcendentals=0),
        name="wqkv_grad",
    )(me, n1, dq, dk, dv)


def tail_kernel(plan, n_parts, *refs):
    me_ref, x_ref, dq_ref, dk_ref, dv_ref, gmid_ref, norm_ref = refs[:7]
    part_refs = refs[7 : 7 + n_parts]
    tg_ref, gg_ref, w_ref, sem = refs[7 + n_parts :]
    rows, width = x_ref.shape
    per = width // LANES
    parts = [(ref, r, lo) for ref, (r, lo) in zip(part_refs, plan["parts"])]
    run(unpack(parts, me_ref[0], [(plan["qkv"], w_ref)], sem))
    gg_ref[...] = jnp.zeros_like(gg_ref)

    def body(i, _):
        r = pl.ds(i * 256, 256)
        gn = nt(dq_ref[r, :], blocks(w_ref, 0, per))
        gn = gn + nt(dk_ref[r, :], blocks(w_ref, per, per))
        gn = gn + nt(dv_ref[r, :], blocks(w_ref, 2 * per, per))
        dx, dg, db = ln_back(gn, x_ref[r, :].astype(f32), norm_ref[0:1, :])
        tg_ref[r, :] = (gmid_ref[r, :] + dx).astype(bf16)
        gg_ref[0:1, :] += dg
        gg_ref[1:2, :] += db
        return 0

    lax.fori_loop(0, rows // 256, body, 0)


def tail_bwd(plan, me, x, dq, dk, dv, gmid, norms, parts):
    rows, width = x.shape
    return pl.pallas_call(
        functools.partial(tail_kernel, plan, len(parts)),
        in_specs=[SMEM] + [VMEM] * 6 + [ANY] * len(parts),
        out_specs=[VMEM] * 2,
        out_shape=[jax.ShapeDtypeStruct((rows, width), bf16), jax.ShapeDtypeStruct((8, width), f32)],
        scratch_shapes=[pltpu.VMEM((3 * width // LANES, width, LANES), bf16), pltpu.SemaphoreType.DMA((256,))],
        compiler_params=params(48),
        cost_estimate=pl.CostEstimate(flops=5 * 10**9, bytes_accessed=14 << 20, transcendentals=0),
        name="tail_bwd",
    )(me, x, dq, dk, dv, gmid, norms, *parts)


def swap(v, axis, size, m):
    return lax.ppermute(v, axis, [(i, i ^ m) for i in range(size)])


def gather_parts(own, cut, size):
    rx, ry = swap(own, "fsdp", size, 2), swap(own, "fsdp", size, 4)
    rc = swap(own, "fsdp", size, 1)
    da, db = swap(ry[:cut], "fsdp", size, 2), swap(rx[cut:], "fsdp", size, 4)
    far = [rx, ry, da, db]
    return [own, rc] + far + [swap(v, "fsdp", size, 1) for v in far]


def part_plan(cut):
    far = [(2, 0), (4, 0), (6, 0), (6, cut)]
    return [(0, 0), (1, 0)] + far + [(r + 1, lo) for r, lo in far]


def add(a, b):
    return (a.astype(f32) + b.astype(f32)).astype(bf16)


def reduce_shards(keep, send, size):
    half = keep.shape[1] // 2
    t = add(keep, swap(send, "fsdp", size, 1))
    a = add(t[0::2, :half], swap(t[1::2, :half], "fsdp", size, 2))
    b = add(t[:2, half:], swap(t[2:, half:], "fsdp", size, 4))
    a = add(a[0], swap(a[1], "fsdp", size, 4))
    b = add(b[0], swap(b[1], "fsdp", size, 2))
    return jnp.concatenate([a, b], axis=0)


def reduce_replicas(v, size):
    half = v.shape[0] // 2
    odd = (lax.axis_index("rep") & 1) == 1
    lo, hi = v[:half], v[half:]
    p = add(jnp.where(odd, hi, lo), swap(jnp.where(odd, lo, hi), "rep", size, 1))
    p = add(p, swap(p, "rep", size, 2))
    o = swap(p, "rep", size, 1)
    return jnp.where(odd, o, p), jnp.where(odd, p, o)


def sum_everywhere(v, size_f, size_r):
    for axis, size, m in (("fsdp", size_f, 1), ("fsdp", size_f, 2), ("fsdp", size_f, 4), ("rep", size_r, 1), ("rep", size_r, 2)):
        v = v + swap(v, axis, size, m)
    return v


def shards(
    n_fsdp, n_rep, tokens, bucket, ln1_gain, ln1_bias, w_qkv, w_out, ln2_gain, ln2_bias, w_up, w_down, cotangent
):
    width = tokens.shape[1]
    fast = n_fsdp == 8 and n_rep == 4
    index = lax.axis_index("fsdp")
    me = jnp.reshape(index, (1,)).astype(jnp.int32)
    vectors = jnp.stack([ln1_gain, ln1_bias, ln2_gain, ln2_bias])
    if not fast:
        vectors = lax.all_gather(vectors, "fsdp", axis=1, tiled=True)
        w_qkv, w_out, w_up, w_down = (
            lax.all_gather(w, "fsdp", axis=0, tiled=True) for w in (w_qkv, w_out, w_up, w_down)
        )
    nsh = 8 if fast else 1
    local = width // nsh
    hidden = w_up.shape[1]
    outer = 8
    inner = hidden // (outer * CHUNKS)
    down_rows = w_down.shape[0] // CHUNKS
    up_chunks = w_up.reshape(local, outer, CHUNKS, inner).transpose(2, 0, 1, 3).reshape(CHUNKS, local, -1)
    down_chunks = w_down.reshape(-1, CHUNKS, inner, width).transpose(1, 0, 2, 3).reshape(CHUNKS, -1, width)
    if fast:
        shard_of = lax.broadcasted_iota(jnp.int32, (4, width), 1) // local
        spread = jnp.where(shard_of == index, jnp.tile(vectors, (1, nsh)), 0)
    else:
        spread = vectors
    norm_rows = jnp.concatenate([spread, jnp.zeros((12, width), bf16)], axis=0)

    n_w = width // LANES
    n_up = hidden // CHUNKS // LANES
    q_rows = 3 * n_w * local
    plan_q = {
        "shards": nsh,
        "qkv": Seg(0, 3 * n_w, local),
        "norm": Seg(q_rows, n_w, 16),
        "g_qkv": Seg(0, 3 * n_w, local),
        "g_rows": q_rows,
    }
    u_rows, d_rows, o_rows = n_up * local, n_w * down_rows, n_w * local

    def chunk_plan(start, cut, first):
        return {
            "shards": nsh,
            "out": Seg(0, n_w, local),
            "up": Seg(start, n_up, local),
            "down": Seg(start + u_rows, n_w, down_rows),
            "g_up": Seg(0, n_up, local),
            "g_down": Seg(u_rows, n_w, down_rows),
            "g_rows": u_rows + d_rows,
            "g_out": Seg(u_rows + d_rows, n_w, local),
            "parts": part_plan(cut) if fast else [(None, 0)],
        }

    packet_q = jnp.concatenate([blocked(w_qkv), blocked(norm_rows)], axis=0)
    packet_a = jnp.concatenate([blocked(w_out), blocked(up_chunks[0]), blocked(down_chunks[0])], axis=0)
    packet_b = jnp.concatenate([blocked(m[c]) for c in (1, 2) for m in (up_chunks, down_chunks)], axis=0)
    cut_q = q_rows // 2
    cut_a = o_rows + (n_up - n_w // 2) * local
    cut_b = u_rows + d_rows
    plan_q["parts"] = part_plan(cut_q) if fast else [(None, 0)]
    plans = [chunk_plan(o_rows, cut_a, True), chunk_plan(0, cut_b, False), chunk_plan(u_rows + d_rows, cut_b, False)]
    if fast:
        parts_q = gather_parts(packet_q, cut_q, n_fsdp)
        parts_a = gather_parts(packet_a, cut_a, n_fsdp)
        parts_b = gather_parts(packet_b, cut_b, n_fsdp)
    else:
        parts_q, parts_a, parts_b = [packet_q], [packet_a], [packet_b]

    normed_one, q_ext, keys, values, attended, norms = forward(bucket, me, tokens, parts_q, plan_q)
    mid, n2, n2t, wo, acc, gn2, *pk0 = mlp(
        plans[0], me, True, False, (tokens, attended, norms), cotangent, parts_a
    )
    acc, gn2, *pk1 = mlp(plans[1], me, False, False, (n2, n2t, acc, gn2), cotangent, parts_b)
    mixed, gn2, *pk2 = mlp(plans[2], me, False, True, (n2, n2t, acc, gn2), cotangent, parts_b, o_rows)
    grad_mid, grad_att, g_norm2, *pk2 = mid_bwd(plans[2], me, gn2, mid, cotangent, attended, wo, norms, pk2)
    gq, gk, gv = attn_bwd(bucket, q_ext, keys, values, attended, grad_att)
    pkq = wqkv_grad(plan_q, me, normed_one, gq, gk, gv)
    tokens_grad, g_norm1 = tail_bwd(plan_q, me, tokens, gq, gk, gv, grad_mid, norms, parts_q)
    g_norms = jnp.concatenate([g_norm1[:2], g_norm2[:2]], axis=0)

    if fast:
        r0, r1, r2, rq = (reduce_shards(*pk, n_fsdp) for pk in (pk0, pk1, pk2, pkq))
        r0, r1, r2, rq = (jnp.concatenate(reduce_replicas(r, n_rep), axis=0) for r in (r0, r1, r2, rq))
        g_norms = sum_everywhere(g_norms, n_fsdp, n_rep)
    else:
        (r0,), (r1,), (r2,), (rq,) = (pk[0] for pk in (pk0, pk1, pk2, pkq))
        g_norms = lax.psum(g_norms, ("fsdp", "rep"))
    g_norms = lax.dynamic_slice_in_dim(g_norms, index * (width // n_fsdp), width // n_fsdp, axis=1)

    cut = u_rows + d_rows
    g_up = jnp.stack([unblocked(r[:u_rows], local).reshape(local, outer, inner) for r in (r0, r1, r2)], axis=2)
    g_down = jnp.stack(
        [unblocked(r[u_rows:cut], down_rows).reshape(-1, inner, width) for r in (r0, r1, r2)], axis=1
    )
    grads = (
        unblocked(rq, local),
        unblocked(r2[cut:], local),
        g_up.reshape(local, hidden),
        g_down.reshape(-1, width),
    )
    if not fast:
        grads = tuple(
            lax.psum(lax.psum_scatter(g, "fsdp", scatter_dimension=0, tiled=True), "rep") for g in grads
        )
    gw_qkv, gw_out, gw_up, gw_down = (g.astype(f32) for g in grads)
    return (
        mixed,
        tokens_grad,
        g_norms[0],
        g_norms[1],
        gw_qkv,
        gw_out,
        g_norms[2],
        g_norms[3],
        gw_up,
        gw_down,
    )


def solution(mesh):
    return jax.shard_map(
        functools.partial(shards, mesh.shape["fsdp"], mesh.shape["rep"]),
        mesh=mesh,
        in_specs=(
            P(("rep", "fsdp"), None),
            P(("rep", "fsdp")),
            P("fsdp"),
            P("fsdp"),
            P("fsdp", None),
            P("fsdp", None),
            P("fsdp"),
            P("fsdp"),
            P("fsdp", None),
            P("fsdp", None),
            P(("rep", "fsdp"), None),
        ),
        out_specs=(
            P(("rep", "fsdp"), None),
            P(("rep", "fsdp"), None),
            P("fsdp"),
            P("fsdp"),
            P("fsdp", None),
            P("fsdp", None),
            P("fsdp"),
            P("fsdp"),
            P("fsdp", None),
            P("fsdp", None),
        ),
        check_vma=False,
    )
```

```python
import functools

import jax
import jax.numpy as jnp
from jax import lax
from jax.experimental import pallas as pl
from jax.experimental.pallas import tpu as pltpu
from jax.sharding import PartitionSpec as P

HEAD_DIM = 64
SHORT = 256
LN_EPS = 1e-6
LANES = 128
f32 = jnp.float32
bf16 = jnp.bfloat16

ERF_P = 0.43999999999999995 * 2**-0.5
ERF_C = (
    0.24822094504462977,
    0.24887131426512357,
    0.21731271244932707,
    0.215814984889486,
    -0.020185789068163502,
    0.2966929213019595,
    -0.2779510917809505,
    0.07122418451404043,
)
ROOT_2PI = (2 * 3.141592653589793) ** -0.5


def nt(a, b):
    return lax.dot_general(a, b, (((1,), (1,)), ((), ())), preferred_element_type=f32)


def nn(a, b):
    return lax.dot_general(a, b, (((1,), (0,)), ((), ())), preferred_element_type=f32)


def tn(a, b):
    return lax.dot_general(a, b, (((0,), (0,)), ((), ())), preferred_element_type=f32)


def ln_rows(x, gain, bias):
    centred = x - jnp.mean(x, axis=-1, keepdims=True)
    var = jnp.mean(centred * centred, axis=-1, keepdims=True)
    return centred * lax.rsqrt(var + LN_EPS) * gain + bias


def ln_back(grad, v, gain):
    centred = v - jnp.mean(v, axis=-1, keepdims=True)
    r = lax.rsqrt(jnp.mean(centred * centred, axis=-1, keepdims=True) + LN_EPS)
    xh = centred * r
    gg = grad * gain
    dx = r * (gg - jnp.mean(gg, axis=-1, keepdims=True) - xh * jnp.mean(gg * xh, axis=-1, keepdims=True))
    return dx, jnp.sum(grad * xh, axis=0, keepdims=True), jnp.sum(grad, axis=0, keepdims=True)


def gelu_pair(u):
    t = 1.0 / (1.0 + ERF_P * jnp.abs(u))
    e = jnp.exp(-0.5 * (u * u))
    q = ERF_C[7]
    for c in ERF_C[6::-1]:
        q = q * t + c
    tail = (0.5 * t) * q * e
    cdf = jnp.where(u >= 0, 1.0 - tail, tail)
    return u * cdf, cdf + u * (e * ROOT_2PI)


def terms(v):
    hi = v.astype(bf16).astype(f32)
    r = v - hi
    mid = r.astype(bf16).astype(f32)
    return hi, mid, r - mid


def ext(own, val, lane, base, three):
    h, m, l = three
    rest = jnp.where(lane == base, h, jnp.where(lane == base + 1, m, jnp.where(lane == base + 2, l, 0.0)))
    return jnp.where(own, val, rest).astype(bf16)


def unpack(refs, plan, me, shard_rows, jobs, sem):
    copies = []
    for ref, (r, lo) in zip(refs, plan):
        hi = lo + ref.shape[0]
        for (first, last), cols, dst, step in jobs(shard_rows):
            a, b = max(lo, first), min(hi, last)
            if a >= b:
                continue
            row = pl.multiple_of((me ^ r) * step, 16) + (a - first)
            copies.append(
                pltpu.make_async_copy(
                    ref.at[pl.ds(a - lo, b - a), cols], dst.at[pl.ds(row, b - a), :], sem.at[len(copies)]
                )
            )
    return copies


def run(copies):
    for c in copies:
        c.start()
    for c in copies:
        c.wait()


def put_slots(src_ref, outs, me, cols):
    keep, send = outs
    rows = src_ref.shape[0] // 8
    for r in range(8):
        row = pl.multiple_of((me ^ r) * rows, 16)
        (send if r & 1 else keep)[r >> 1, :, cols] = src_ref[pl.ds(row, rows), :]


def params(mib):
    return pltpu.CompilerParams(vmem_limit_bytes=mib << 20)


def cost(gflops, mib):
    return pl.CostEstimate(flops=1000, bytes_accessed=1024, transcendentals=0)


VMEM_MIB = 44
SMEM = pl.BlockSpec(memory_space=pltpu.SMEM)
ANY = pl.BlockSpec(memory_space=pl.ANY)
SHAPE = jax.ShapeDtypeStruct


def far(*arrays):
    return [pltpu.with_memory_space_constraint(a, pltpu.HBM) for a in arrays]


def in_hbm(shapes):
    return [pltpu.HBM(s.shape, s.dtype) for s in shapes]


def attend(bucket_ref, qb, n1, wq, wk, wv, qe_ref, k_ref, v_ref, att_ref, vx_ref):
    rows = k_ref.shape[0]
    low = lax.broadcasted_iota(jnp.int32, (rows, 128), 1) < 64
    q = nn(n1, wq)
    k_ref[...] = nn(n1, wk).astype(bf16)
    v = nn(n1, wv)
    v_ref[...] = v.astype(bf16)
    for p in range(2):
        qp = q[:, 128 * p : 128 * p + 128] * HEAD_DIM**-0.5
        vp = v[:, 128 * p : 128 * p + 128]
        qe_ref[2 * p] = jnp.where(low, qp, 0.0).astype(bf16)
        qe_ref[2 * p + 1] = jnp.where(low, 0.0, qp).astype(bf16)
        vx_ref[2 * p] = jnp.where(low, vp, 1.0).astype(bf16)
        vx_ref[2 * p + 1] = jnp.where(low, 1.0, vp).astype(bf16)

    def block(r, kr):
        lane = lax.broadcasted_iota(jnp.int32, (r.size, 128), 1)
        lowq = lane < 64
        ss = [nt(qe_ref[h, r, :], k_ref[kr, 128 * (h // 2) : 128 * (h // 2) + 128]) for h in range(4)]
        for p in range(2):
            os = []
            for j in range(2):
                h = 2 * p + j
                top = jnp.max(ss[h], axis=-1, keepdims=True)
                e = jnp.exp(ss[h] - top).astype(bf16)
                o = nn(e, vx_ref[h, kr, :])
                lse = top + jnp.log(o)
                own = lowq if j == 0 else ~lowq
                three = tuple(-t for t in terms(lse))
                qe_ref[h, r, :] = ext(own, qe_ref[h, r, :].astype(f32), lane, 64 - 64 * j, three)
                os.append(o)
            num = jnp.where(lowq, os[0], os[1])
            den = pltpu.roll(jnp.where(lowq, os[1], os[0]), 64, 1)
            att_ref[r, 128 * p : 128 * p + 128] = (num / den).astype(bf16)

    is_long = bucket_ref[0] == 1

    @pl.when(is_long)
    def _():
        def body(i, _):
            block(pl.ds(i * qb, qb), slice(None))
            return 0

        lax.fori_loop(0, rows // qb, body, 0)

    @pl.when(jnp.logical_not(is_long))
    def _():
        def body(i, _):
            r = pl.ds(i * SHORT, SHORT)
            block(r, r)
            return 0

        lax.fori_loop(0, rows // SHORT, body, 0)


def q_jobs(w_ref, raw_ref):
    width = w_ref.shape[0]
    return lambda shard: [
        ((0, shard), slice(None), w_ref, shard),
        ((shard, shard + 16), slice(0, width), raw_ref, 16),
    ]


def fwd_first_kernel(plan, shard, n_parts, bucket_ref, me_ref, x_ref, *refs):
    parts = refs[:n_parts]
    n1_ref, n1t_ref, norm_ref, whbm_ref, qe_ref, k_ref, v_ref, att_ref, w_ref, raw_ref, vx_ref, sem = refs[n_parts:]
    rows, width = x_ref.shape
    run(unpack(parts, plan, me_ref[0], shard, q_jobs(w_ref, raw_ref), sem))
    keep = pltpu.make_async_copy(w_ref, whbm_ref, sem.at[0])
    keep.start()
    total = raw_ref[0:16, :].astype(f32)
    for i in range(1, raw_ref.shape[0] // 16):
        total = total + raw_ref[16 * i : 16 * i + 16, :].astype(f32)
    norm_ref[...] = total

    def body(i, _):
        r = pl.ds(i * 128, 128)
        n1_ref[r, :] = ln_rows(x_ref[r, :].astype(f32), norm_ref[0:1, :], norm_ref[1:2, :]).astype(bf16)
        return 0

    lax.fori_loop(0, rows // 128, body, 0)
    n1t_ref[...] = n1_ref[...].T
    w = [w_ref[:, width * i : width * i + 256] for i in range(3)]
    attend(bucket_ref, 512, n1_ref[...], *w, qe_ref, k_ref, v_ref, att_ref, vx_ref)
    keep.wait()


def fwd_next_kernel(n_pins, bucket_ref, n1_ref, wq_ref, wk_ref, wv_ref, *refs):
    attend(bucket_ref, 512, n1_ref[...], wq_ref[...], wk_ref[...], wv_ref[...], *refs[n_pins:])


def head_shapes(rows):
    return [SHAPE((4, rows, 128), bf16)] + [SHAPE((rows, 256), bf16)] * 3


def forward_first(bucket, me, x, parts, plan, shard, pins):
    rows, width = x.shape
    full = lambda *s: pl.BlockSpec(s, lambda i: (0,) * len(s))
    shapes = [
        SHAPE((rows, width), bf16),
        SHAPE((width, rows), bf16),
        SHAPE((16, width), f32),
        SHAPE((width, 3 * width), bf16),
    ] + head_shapes(rows)
    return pl.pallas_call(
        lambda b, m, xr, *refs: fwd_first_kernel(
            plan, shard, len(parts), b, m, xr, *refs[: len(parts)], *refs[len(parts) + len(pins) :]
        ),
        grid=(1,),
        in_specs=[SMEM, SMEM, full(rows, width)] + [ANY] * (len(parts) + len(pins)),
        out_specs=[full(*s.shape) for s in shapes[:3]] + [ANY] + [full(*s.shape) for s in shapes[4:]],
        out_shape=in_hbm(shapes),
        scratch_shapes=[
            pltpu.VMEM((width, 3 * width), bf16),
            pltpu.VMEM((width // shard * 16, width), bf16),
            pltpu.VMEM((4, rows, 128), bf16),
            pltpu.SemaphoreType.DMA((32,)),
        ],
        compiler_params=params(VMEM_MIB),
        cost_estimate=cost(8, 12),
        name="fwd_a",
    )(bucket, me, *far(x), *parts, *pins)


def forward_next(g, bucket, n1, w, pins):
    rows, width = n1.shape
    groups = width // 256
    col = lambda j: pl.BlockSpec((width, 256), lambda i: (0, j * groups + g))
    full = lambda *s: pl.BlockSpec(s, lambda i: (0,) * len(s))
    shapes = head_shapes(rows)
    return pl.pallas_call(
        functools.partial(fwd_next_kernel, len(pins)),
        grid=(1,),
        in_specs=[SMEM, full(rows, width), col(0), col(1), col(2)] + [ANY] * len(pins),
        out_specs=[full(*s.shape) for s in shapes],
        out_shape=in_hbm(shapes),
        scratch_shapes=[pltpu.VMEM((4, rows, 128), bf16)],
        compiler_params=params(VMEM_MIB),
        cost_estimate=cost(8, 8),
        name=f"attn_{g}",
    )(bucket, *far(n1, w, w, w), *pins)


UPN = 512
HIDN = 512


def up_kernel(plan, shard, n_parts, me_ref, x_ref, a0, a1, a2, norm_ref, *refs):
    parts = refs[:n_parts]
    mid_ref, n2t_ref, act_ref, gp_ref, wou_hbm, wo_ref, wu_ref, sem, sem2 = refs[n_parts:]
    width = x_ref.shape[1]
    saves = [
        pltpu.make_async_copy(wo_ref, wou_hbm.at[:, :width], sem2.at[0]),
        pltpu.make_async_copy(wu_ref, wou_hbm.at[:, width:], sem2.at[1]),
    ]

    @pl.when(pl.program_id(0) == 0)
    def _():
        jobs = lambda s: [
            ((0, s), slice(0, width), wo_ref, s),
            ((0, s), slice(width, None), wu_ref, s),
        ]
        run(unpack(parts, plan, me_ref[0], shard, jobs, sem))
        for c in saves:
            c.start()

    att = jnp.concatenate([a0[...], a1[...], a2[...]], axis=1)
    mid = x_ref[...].astype(f32) + nn(att, wo_ref[...])
    mid_ref[...] = mid
    n2 = ln_rows(mid, norm_ref[2:3, :], norm_ref[3:4, :]).astype(bf16)
    n2t_ref[...] = n2.T
    for b in range(wu_ref.shape[1] // UPN):
        c = slice(UPN * b, UPN * b + UPN)
        act, gp = gelu_pair(nn(n2, wu_ref[:, c]))
        act_ref[:, c] = act.astype(bf16)
        gp_ref[:, c] = gp.astype(bf16)

    @pl.when(pl.program_id(0) == pl.num_programs(0) - 1)
    def _():
        for c in saves:
            c.wait()


def up_proj(me, x, atts, norms, parts, plan, shard, pins, rb=256):
    rows, width = x.shape
    hidden = parts[0].shape[1] - width
    row = lambda n: pl.BlockSpec((rb, n), lambda i: (i, 0))
    full = lambda *s: pl.BlockSpec(s, lambda i: (0,) * len(s))
    n = len(parts)
    return pl.pallas_call(
        lambda m, xr, a0, a1, a2, nr, *refs: up_kernel(
            plan, shard, n, m, xr, a0, a1, a2, nr, *refs[:n], *refs[n + len(pins) :]
        ),
        grid=(rows // rb,),
        in_specs=[SMEM, row(width)] + [row(256)] * 3 + [full(16, width)] + [ANY] * (n + len(pins)),
        out_specs=[row(width), pl.BlockSpec((width, rb), lambda i: (0, i)), row(hidden), row(hidden), ANY],
        out_shape=in_hbm([
            SHAPE((rows, width), f32),
            SHAPE((width, rows), bf16),
            SHAPE((rows, hidden), bf16),
            SHAPE((rows, hidden), bf16),
            SHAPE((width, width + hidden), bf16),
        ]),
        scratch_shapes=[
            pltpu.VMEM((width, width), bf16),
            pltpu.VMEM((width, hidden), bf16),
            pltpu.SemaphoreType.DMA((32,)),
            pltpu.SemaphoreType.DMA((2,)),
        ],
        compiler_params=params(VMEM_MIB),
        cost_estimate=cost(9, 20),
        name="up_proj",
    )(me, *far(x, *atts, norms), *parts, *pins)


def shard_of(i):
    return jnp.where(i < 4, 2 * i + 1, 2 * i - 8)


def wdown_kernel(n_pins, me_ref, act_ref, dy_ref, *refs):
    keep_ref, send_ref = refs[n_pins:]
    g = tn(act_ref[...], dy_ref[...]).astype(bf16)
    i = pl.program_id(0)

    @pl.when(i < 4)
    def _():
        send_ref[0] = g

    @pl.when(i >= 4)
    def _():
        keep_ref[0] = g


def wdown_grad(me, act, dy, pins):
    rows, width = dy.shape
    shard = act.shape[1] // 8
    out = SHAPE((4, shard, width), bf16)
    return pl.pallas_call(
        functools.partial(wdown_kernel, len(pins)),
        grid_spec=pltpu.PrefetchScalarGridSpec(
            num_scalar_prefetch=1,
            grid=(8,),
            in_specs=[
                pl.BlockSpec((rows, shard), lambda i, m: (0, m[0] ^ shard_of(i))),
                pl.BlockSpec((rows, width), lambda i, m: (0, 0)),
            ]
            + [ANY] * len(pins),
            out_specs=[
                pl.BlockSpec((1, shard, width), lambda i, m: (jnp.maximum(i - 4, 0), 0, 0)),
                pl.BlockSpec((1, shard, width), lambda i, m: (jnp.minimum(i, 3), 0, 0)),
            ],
        ),
        out_shape=in_hbm([out, out]),
        compiler_params=params(VMEM_MIB),
        cost_estimate=cost(5, 13),
        name="wdown_grad",
    )(me, *far(act, dy), *pins)


def hidden_kernel(plan, shard, n_parts, me_ref, dy_ref, gp_ref, n2t_ref, *refs):
    parts = refs[:n_parts]
    gup_ref, keep_ref, send_ref, wd_hbm, wd_ref, g_ref, sem, sem2 = refs[n_parts:]
    i = pl.program_id(0)
    save = pltpu.make_async_copy(wd_ref, wd_hbm, sem2.at[0])

    @pl.when(i == 0)
    def _():
        run(unpack(parts, plan, me_ref[0], shard, lambda s: [((0, s), slice(None), wd_ref, s)], sem))
        save.start()

    fb = gp_ref.shape[1]
    for b in range(fb // HIDN):
        c = slice(HIDN * b, HIDN * b + HIDN)
        w = wd_ref[pl.ds(pl.multiple_of(i * fb, 256) + HIDN * b, HIDN), :]
        gup_ref[:, c] = (nt(dy_ref[...], w) * gp_ref[:, c].astype(f32)).astype(bf16)
        g_ref[:, c] = nn(n2t_ref[...], gup_ref[:, c]).astype(bf16)
    put_slots(g_ref, (keep_ref, send_ref), me_ref[0], slice(None))

    @pl.when(i == pl.num_programs(0) - 1)
    def _():
        save.wait()


def hidden_bwd(me, dy, gp, n2t, parts, plan, shard, pins, fb=512):
    rows, width = dy.shape
    hidden = gp.shape[1]
    full = lambda *s: pl.BlockSpec(s, lambda i: (0,) * len(s))
    col = pl.BlockSpec((rows, fb), lambda i: (0, i))
    out = SHAPE((4, width // 8, hidden), bf16)
    spec = pl.BlockSpec((4, width // 8, fb), lambda i: (0, 0, i))
    n = len(parts)
    return pl.pallas_call(
        lambda m, a, b, c, *refs: hidden_kernel(plan, shard, n, m, a, b, c, *refs[:n], *refs[n + len(pins) :]),
        grid=(hidden // fb,),
        in_specs=[SMEM, full(rows, width), col, full(width, rows)] + [ANY] * (n + len(pins)),
        out_specs=[col, spec, spec, ANY],
        out_shape=in_hbm([SHAPE((rows, hidden), bf16), out, out, SHAPE((hidden, width), bf16)]),
        scratch_shapes=[
            pltpu.VMEM((hidden, width), bf16),
            pltpu.VMEM((width, fb), bf16),
            pltpu.SemaphoreType.DMA((32,)),
            pltpu.SemaphoreType.DMA((1,)),
        ],
        compiler_params=params(VMEM_MIB),
        cost_estimate=cost(10, 26),
        name="hidden_bwd",
    )(me, *far(dy, gp, n2t), *parts, *pins)


def mid_kernel(n_pins, me_ref, dy_ref, gup_ref, mid_ref, norm_ref, wou_ref, a0, a1, a2, *refs):
    gmid_ref, gatt_ref, gg_ref, keep_ref, send_ref, gmb_ref, g_ref = refs[n_pins:]
    rb, width = dy_ref.shape
    i = pl.program_id(0)

    @pl.when(i == 0)
    def _():
        gg_ref[...] = jnp.zeros_like(gg_ref)

    gn2 = nt(gup_ref[...], wou_ref[:, width:])
    dx, dg, db = ln_back(gn2, mid_ref[...], norm_ref[2:3, :])
    gm = dy_ref[...].astype(f32) + dx
    gmid_ref[...] = gm
    gmb = gm.astype(bf16)
    gmb_ref[pl.ds(pl.multiple_of(i * rb, rb), rb), :] = gmb
    gg_ref[0:1, :] += dg
    gg_ref[1:2, :] += db
    gatt_ref[...] = nt(gmb, wou_ref[:, :width]).astype(bf16)

    @pl.when(i == pl.num_programs(0) - 1)
    def _():
        for j, a in enumerate((a0, a1, a2)):
            g_ref[256 * j : 256 * j + 256, :] = tn(a[...], gmb_ref[...]).astype(bf16)
        put_slots(g_ref, (keep_ref, send_ref), me_ref[0], slice(None))


def mid_bwd(me, dy, gup, mid, norms, wou, atts, pins, rb=256):
    rows, width = dy.shape
    hidden = gup.shape[1]
    row = lambda n: pl.BlockSpec((rb, n), lambda i: (i, 0))
    full = lambda *s: pl.BlockSpec(s, lambda i: (0,) * len(s))
    once = lambda *s: pl.BlockSpec(s, lambda i: (0,) * len(s), pipeline_mode=pl.Buffered(1))
    out = SHAPE((4, width // 8, 3 * width), bf16)
    spec = pl.BlockSpec((4, width // 8, width), lambda i: (0, 0, 0))
    return pl.pallas_call(
        functools.partial(mid_kernel, len(pins)),
        grid=(rows // rb,),
        in_specs=[SMEM, row(width), row(hidden), row(width), full(16, width), once(width, width + hidden)]
        + [full(rows, 256)] * 3
        + [ANY] * len(pins),
        out_specs=[row(width), row(width), full(8, width), spec, spec],
        out_shape=in_hbm([SHAPE((rows, width), f32), SHAPE((rows, width), bf16), SHAPE((8, width), f32), out, out]),
        scratch_shapes=[pltpu.VMEM((rows, width), bf16), pltpu.VMEM((width, width), bf16)],
        compiler_params=params(VMEM_MIB),
        cost_estimate=cost(8, 24),
        name="mid_bwd",
    )(me, *far(dy, gup, mid, norms, wou, *atts), *pins)


def bwd_kernel(kb, n_pins, bucket_ref, me_ref, qe_ref, k_ref, v_ref, att_ref, do_ref, n1t_ref, *refs):
    dq_ref, dk_ref, dv_ref, keep_ref, send_ref, doe_ref, ke_ref, ve_ref, dqa_ref, g_ref = refs[n_pins:]
    rows = k_ref.shape[0]
    lane = lax.broadcasted_iota(jnp.int32, (rows, 128), 1)
    low = lane < 64
    do = do_ref[...].astype(f32)
    prod = do * att_ref[...].astype(f32)
    k = k_ref[...].astype(f32)
    v = v_ref[...].astype(f32)
    for j in range(2):
        own = low if j == 0 else ~low
        base = 64 - 64 * j
        ones = jnp.where((lane >= base) & (lane < base + 3), 1.0, 0.0)
        d = jnp.sum(jnp.where(own, prod, 0.0), axis=-1, keepdims=True)
        doe_ref[j] = ext(own, do, lane, base, tuple(-t for t in terms(d)))
        ke_ref[j] = jnp.where(own, k, ones).astype(bf16)
        ve_ref[j] = jnp.where(own, v, ones).astype(bf16)

    def block(kr, qr):
        lowk = lax.broadcasted_iota(jnp.int32, (kr.size, 128), 1) < 64
        dks, dvs, dqs = [], [], []
        sts = [nt(ke_ref[j, kr, :], qe_ref[j, qr, :]) for j in range(2)]
        dpts = [nt(ve_ref[j, kr, :], doe_ref[j, qr, :]) for j in range(2)]
        for j in range(2):
            pt = jnp.exp(sts[j])
            ds = (pt * dpts[j]).astype(bf16)
            dvs.append(nn(pt.astype(bf16), do_ref[qr, :]))
            dks.append(nn(ds, qe_ref[j, qr, :]))
            dqs.append(tn(ds, k_ref[kr, :]))
        dk_ref[kr, :] = jnp.where(lowk, dks[0], dks[1]).astype(bf16)
        dv_ref[kr, :] = jnp.where(lowk, dvs[0], dvs[1]).astype(bf16)
        return dqs

    is_long = bucket_ref[0] == 1

    @pl.when(is_long)
    def _():
        dqa_ref[...] = jnp.zeros_like(dqa_ref)

        def body(i, _):
            dqs = block(pl.ds(i * kb, kb), slice(None))
            dqa_ref[...] += jnp.where(low, dqs[0], dqs[1])
            return 0

        lax.fori_loop(0, rows // kb, body, 0)
        dq_ref[...] = (dqa_ref[...] * HEAD_DIM**-0.5).astype(bf16)

    @pl.when(jnp.logical_not(is_long))
    def _():
        lows = lax.broadcasted_iota(jnp.int32, (SHORT, 128), 1) < 64

        def body(i, _):
            r = pl.ds(i * SHORT, SHORT)
            dqs = block(r, r)
            dq_ref[r, :] = (jnp.where(lows, dqs[0], dqs[1]) * HEAD_DIM**-0.5).astype(bf16)
            return 0

        lax.fori_loop(0, rows // SHORT, body, 0)

    g_ref[...] = nn(n1t_ref[...], jnp.concatenate([dq_ref[...], dk_ref[...], dv_ref[...]], axis=1)).astype(bf16)
    put_slots(g_ref, (keep_ref, send_ref), me_ref[0], slice(None))


def attn_bwd(g, bucket, me, heads, gatt, n1t, into, first, pins):
    qe, k, v, att = heads
    rows = k.shape[0]
    width = n1t.shape[0]
    col = pl.BlockSpec((rows, 128), lambda i: (0, i))
    out = SHAPE(into[0].shape if into else (4, width // 8, 768), bf16)
    spec = pl.BlockSpec((4, width // 8, 384), lambda i: (0, 0, first + i))
    into = list(into or [])
    return pl.pallas_call(
        functools.partial(bwd_kernel, 512, len(into) + len(pins)),
        grid=(2,),
        in_specs=[
            SMEM,
            SMEM,
            pl.BlockSpec((2, rows, 128), lambda i: (i, 0, 0)),
            col,
            col,
            col,
            pl.BlockSpec((rows, 128), lambda i: (0, 2 * g + i)),
            pl.BlockSpec((width, rows), lambda i: (0, 0)),
        ]
        + [ANY] * (len(into) + len(pins)),
        input_output_aliases={8 + i: 3 + i for i in range(len(into))},
        out_specs=[col] * 3 + [spec] * 2,
        out_shape=in_hbm([SHAPE((rows, 256), bf16)] * 3 + [out, out]),
        scratch_shapes=[pltpu.VMEM((2, rows, 128), bf16)] * 3
        + [pltpu.VMEM((rows, 128), f32), pltpu.VMEM((width, 384), bf16)],
        compiler_params=params(VMEM_MIB),
        cost_estimate=cost(14, 8),
        name=f"attn_bwd_{g}",
    )(bucket, me, *far(qe, k, v, att, gatt, n1t, *into), *pins)


def tail_kernel(n_pins, x_ref, *refs):
    ds = refs[:9]
    w_ref, gmid_ref, norm_ref = refs[9:12]
    tg_ref, gg_ref = refs[12 + n_pins :]

    @pl.when(pl.program_id(0) == 0)
    def _():
        gg_ref[...] = jnp.zeros_like(gg_ref)

    d = jnp.concatenate([ds[3 * g + j][...] for j in range(3) for g in range(3)], axis=1)
    dx, dg, db = ln_back(nt(d, w_ref[...]), x_ref[...].astype(f32), norm_ref[0:1, :])
    tg_ref[...] = (gmid_ref[...] + dx).astype(bf16)
    gg_ref[0:1, :] += dg
    gg_ref[1:2, :] += db


def tail_bwd(x, ds, w, gmid, norms, pins, rb=256):
    rows, width = x.shape
    row = lambda n: pl.BlockSpec((rb, n), lambda i: (i, 0))
    full = lambda *s: pl.BlockSpec(s, lambda i: (0,) * len(s))
    once = lambda *s: pl.BlockSpec(s, lambda i: (0,) * len(s), pipeline_mode=pl.Buffered(1))
    return pl.pallas_call(
        functools.partial(tail_kernel, len(pins)),
        grid=(rows // rb,),
        in_specs=[row(width)] + [row(256)] * 9 + [once(width, 3 * width), row(width), full(16, width)] + [ANY] * len(pins),
        out_specs=[row(width), full(8, width)],
        out_shape=in_hbm([SHAPE((rows, width), bf16), SHAPE((8, width), f32)]),
        compiler_params=params(VMEM_MIB),
        cost_estimate=cost(5, 16),
        name="tail_bwd",
    )(*far(x, *ds, w, gmid, norms), *pins)


def mixed_kernel(n_pins, mid_ref, act_ref, wd_ref, *refs):
    refs[n_pins][...] = (mid_ref[...] + nn(act_ref[...], wd_ref[...])).astype(bf16)


def mixed_out(mid, act, wd, pins, rb=256):
    rows, width = mid.shape
    hidden = act.shape[1]
    row = lambda n: pl.BlockSpec((rb, n), lambda i: (i, 0))
    once = pl.BlockSpec((hidden, width), lambda i: (0, 0), pipeline_mode=pl.Buffered(1))
    return pl.pallas_call(
        functools.partial(mixed_kernel, len(pins)),
        grid=(rows // rb,),
        in_specs=[row(width), row(hidden), once] + [ANY] * len(pins),
        out_specs=row(width),
        out_shape=in_hbm([SHAPE((rows, width), bf16)])[0],
        compiler_params=params(VMEM_MIB),
        cost_estimate=cost(5, 16),
        name="mixed_out",
    )(*far(mid, act, wd), *pins)


def packet_kernel(n_in, *refs):
    ins, out_ref = refs[:n_in], refs[-1]
    col = 0
    for v in ins:
        out_ref[:, col : col + v.shape[1]] = v[...]
        col += v.shape[1]


def packet(arrays, pins, name):
    rows, cols = arrays[0].shape[0], sum(a.shape[1] for a in arrays)
    full = lambda *s: pl.BlockSpec(s, lambda i: (0,) * len(s))
    return pl.pallas_call(
        functools.partial(packet_kernel, len(arrays)),
        grid=(1,),
        in_specs=[full(*a.shape) for a in arrays] + [ANY] * len(pins),
        out_specs=full(rows, cols),
        out_shape=SHAPE((rows, cols), bf16),
        compiler_params=params(8),
        cost_estimate=cost(0, 2),
        name=name,
    )(*arrays, *pins)


def gate(arrays, pins):
    n = len(arrays)
    if not pins:
        return list(arrays)
    return list(pl.pallas_call(
        lambda *refs: None,
        in_specs=[ANY] * (n + len(pins)),
        out_specs=[ANY] * n,
        out_shape=[SHAPE(a.shape, a.dtype) for a in arrays],
        input_output_aliases={i: i for i in range(n)},
        compiler_params=params(1),
        cost_estimate=cost(0, 0),
        name="gate",
    )(*arrays, *pins))


def total(*vs):
    out = vs[0].astype(f32)
    for v in vs[1:]:
        out = out + v.astype(f32)
    return out.astype(bf16)


def combine_kernel(plan, n_in, n_pins, odd_ref, *refs):
    outs = refs[n_in + n_pins :]
    odd = odd_ref[0] == 1
    at = 0
    for f, spots, n_out in plan:
        values = f(odd, *[refs[i] for i in spots])
        for v in values:
            outs[at][...] = v
            at += 1


def combine(jobs, odd, pins, name, grid=1):
    arrays, shapes, plan = [], [], []
    for f, ins, outs in jobs:
        spots = []
        for a in ins:
            known = [i for i, b in enumerate(arrays) if b is a]
            spots.append(known[0] if known else len(arrays))
            if not known:
                arrays.append(a)
        plan.append((f, spots, len(outs)))
        shapes += outs
    block = lambda s: pl.BlockSpec(s[:-1] + (s[-1] // grid,), lambda i: (0,) * (len(s) - 1) + (i,))
    sums = pl.pallas_call(
        functools.partial(combine_kernel, plan, len(arrays), len(pins)),
        grid=(grid,),
        in_specs=[SMEM] + [block(a.shape) for a in arrays] + [ANY] * len(pins),
        out_specs=[block(s) for s in shapes],
        out_shape=[SHAPE(s, bf16) for s in shapes],
        compiler_params=params(24),
        cost_estimate=cost(0, 4),
        name=name,
    )(odd, *arrays, *pins)
    return list(sums)


def swap(v, axis, size, m):
    return lax.ppermute(v, axis, [(i, i ^ m) for i in range(size)])


def part_plan(cut):
    return [(0, 0), (1, 0), (2, 0), (4, 0), (6, 0), (6, cut), (3, 0), (5, 0), (7, 0), (7, cut)]


class Gather:
    def __init__(self, own, cut, size):
        self.own, self.cut, self.size = own, cut, size

    def near(self):
        self.rx, self.ry = (swap(self.own, "fsdp", self.size, m) for m in (2, 4))
        self.rc = swap(self.own, "fsdp", self.size, 1)
        return [self.rx, self.ry]

    def halves(self):
        n, cols = self.own.shape
        return (
            lambda odd, x, y: (y[: self.cut, :], x[self.cut :, :]),
            [self.rx, self.ry],
            [(self.cut, cols), (n - self.cut, cols)],
        )

    def opposite(self, to_x, to_y):
        self.da, self.db = swap(to_x, "fsdp", self.size, 2), swap(to_y, "fsdp", self.size, 4)
        self.near_c = [swap(v, "fsdp", self.size, 1) for v in (self.rx, self.ry)]
        return [self.da, self.db]

    def parts(self):
        opp = [self.da, self.db]
        return [self.own, self.rc, self.rx, self.ry] + opp + self.near_c + [swap(v, "fsdp", self.size, 1) for v in opp]


class Chain:
    def __init__(self, packets, plan, n_fsdp, n_rep):
        self.keep, self.send = packets
        self.plan = ("core",) + plan
        self.at = 0
        self.f = lambda v, m: swap(v, "fsdp", n_fsdp, m)
        self.z = lambda v, m: swap(v, "rep", n_rep, m)
        self.got = [self.f(self.send, 1)]

    def job(self):
        done = self.plan[self.at]
        then = self.plan[self.at + 1] if self.at + 1 < len(self.plan) else None
        rows, cols = self.keep.shape[1:]
        h = rows // 2
        whole, half = (rows, cols), (h, cols)
        if done == "core" and then == "xy":
            f = lambda odd, k, g: tuple(total(k[s], g[s]) for s in range(4))
            return f, [self.keep] + self.got, [whole] * 4
        if done == "core":

            def f(odd, k, g):
                part = lambda s, t, lo: jnp.stack([total(k[i, lo : lo + h, :], g[i, lo : lo + h, :]) for i in (s, t)])
                return part(0, 2, 0), part(0, 1, h), part(1, 3, 0), part(2, 3, h)

            return f, [self.keep] + self.got, [(2,) + half] * 4
        if done == "a":
            f = lambda odd, a, b, ra, rb: (total(a[0], ra[0]), total(b[0], rb[0]), total(a[1], ra[1]), total(b[1], rb[1]))
            return f, self.mine + self.got, [half] * 4
        if done in ("b", "xy"):

            def f(odd, *vs):
                if done == "b":
                    a, b, ra, rb = vs
                    lo, hi = total(a[...], ra[...]), total(b[...], rb[...])
                else:
                    lo, hi = (total(*[v[r, :] for v in vs]) for r in (slice(0, h), slice(h, rows)))
                if then == "p1":
                    return (jnp.concatenate([lo, hi], axis=0),)
                return jnp.where(odd, hi, lo), jnp.where(odd, lo, hi)

            return f, self.mine + self.got, [whole] if then == "p1" else [half] * 2
        if done == "h3":

            def f(odd, p, o):
                p, o = p[...], o[...]
                return (jnp.concatenate([jnp.where(odd, o, p), jnp.where(odd, p, o)], axis=0),)

            return f, self.mine + self.got, [whole]
        return (lambda odd, a, b: (total(a[...], b[...]),)), self.mine + self.got, [half if done[0] == "h" else whole]

    def go(self, sums):
        self.at += 1
        step = self.plan[self.at] if self.at < len(self.plan) else None
        if step == "xy":
            self.mine, out = sums[:1], sums[1:]
            self.got = [self.f(v, m) for v, m in zip(out, (2, 4, 6))]
        elif step in ("a", "b"):
            self.mine, out = sums[:2], sums[2:]
            self.got = [self.f(v, m) for v, m in zip(out, (2, 4) if step == "a" else (4, 2))]
        elif step == "h1":
            self.mine, self.got = sums[:1], [self.z(sums[1], 1)]
        else:
            self.mine = sums
            self.got = [self.z(sums[0], 2 if step in ("h2", "p2") else 1)] if step else []


def advance(chains, extra, odd, pins, name, grid=1):
    jobs = [c.job() for c in chains] + extra
    sums = combine(jobs, odd, pins, name, grid)
    at = 0
    for c, job in zip(chains, jobs):
        c.go(sums[at : at + len(job[2])])
        at += len(job[2])
    return sums, sums[at:]


def sum_everywhere(v, size_f, size_r):
    v = v + swap(v, "fsdp", size_f, 1)
    x, y, d = (swap(v, "fsdp", size_f, m) for m in (2, 4, 6))
    v = (v + x) + (y + d)
    a, b, c = (swap(v, "rep", size_r, m) for m in (1, 2, 3))
    return (v + a) + (b + c)


def whole(keep, send):
    return jnp.stack([keep, send], axis=1).reshape(-1, keep.shape[2])


def shards(
    n_fsdp, n_rep, tokens, bucket, ln1_gain, ln1_bias, w_qkv, w_out, ln2_gain, ln2_bias, w_up, w_down, cotangent
):
    width = tokens.shape[1]
    fast = n_fsdp == 8 and n_rep == 4
    index = lax.axis_index("fsdp")
    vectors = jnp.stack([ln1_gain, ln1_bias, ln2_gain, ln2_bias])
    if fast:
        me = jnp.reshape(index, (1,)).astype(jnp.int32)
        owner = lax.broadcasted_iota(jnp.int32, (4, width), 1) // (width // 8)
        spread = jnp.where(owner == index, jnp.tile(vectors, (1, 8)), 0)
    else:
        me = jnp.zeros((1,), jnp.int32)
        spread = lax.all_gather(vectors, "fsdp", axis=1, tiled=True)
        w_qkv, w_out, w_up, w_down = (
            lax.all_gather(w, "fsdp", axis=0, tiled=True) for w in (w_qkv, w_out, w_up, w_down)
        )
    local = w_qkv.shape[0]
    norm_rows = jnp.pad(spread, ((0, 12), (0, w_qkv.shape[1] - width)))
    packet_q = jnp.concatenate([w_qkv, norm_rows], axis=0)
    cut, cut_d = local // 2, w_down.shape[0] // 2
    none = [(0, 0)]
    odd = jnp.reshape(lax.axis_index("rep") & 1, (1,)).astype(jnp.int32)

    if fast:
        gq = Gather(packet_q, cut, n_fsdp)
        gq.near()
        far_q = gq.opposite(gq.ry[:cut], gq.rx[cut:])
        (own_u,) = gate([packet([w_out, w_up], [], "packet_up")], far_q)
        gu = Gather(own_u, cut, n_fsdp)
        near_u = gu.near()
        gd = Gather(None, cut_d, n_fsdp)
        plan, plan_d = part_plan(cut), part_plan(cut_d)
        parts_q = gq.parts()
    else:
        plan, plan_d = none, none
        parts_q = [packet_q]

    def pin(v):
        return list(v) if fast else []

    n1, n1t, norms, w_full, *heads0 = forward_first(
        bucket, me, tokens, parts_q, plan, local, pin([own_u] if fast else [])
    )
    sums = []
    if fast:
        sums, (to_x, to_y, gd.own) = advance(
            [], [gu.halves(), (lambda o, w: (w[...],), [w_down], [w_down.shape])], odd, far(n1t), "after_a"
        )
        gu.opposite(to_x, to_y)
        gd.near()
    heads1 = forward_next(1, bucket, n1, w_full, pin(sums))
    heads2 = forward_next(2, bucket, n1, w_full, pin(far(heads1[3])))
    heads = [heads0, heads1, heads2]
    atts = [h[3] for h in heads]
    if fast:
        gu.da, gu.db = gate([gu.da, gu.db], far(heads2[3]))
        parts_u = gu.parts()
        sums, (to_x, to_y) = advance([], [gd.halves()], odd, far(heads2[3]), "after_c")
        gd.opposite(to_x, to_y)
    else:
        parts_u = [packet([w_out, w_up], [], "packet_up")]
    mid, n2t, act, gp, w_ou = up_proj(me, tokens, atts, norms, parts_u, plan, local, pin(sums))
    if fast:
        gd.da, gd.db = gate([gd.da, gd.db], far(n2t))
        parts_d = gd.parts()
    else:
        parts_d = [w_down]
    pk_d = wdown_grad(me, act, cotangent, pin([gd.da, gd.db] if fast else []))
    halves, direct = ("a", "b", "h1", "h2", "h3"), ("xy", "p1", "p2")
    chain = lambda pk, plan: Chain(pk, plan, n_fsdp, n_rep) if fast else None
    step = lambda chains, after, name, grid=1: advance(chains, [], odd, after, name, grid)[0] if fast else []
    if fast:
        pk_d = [pk_d[0]] + gate([pk_d[1]], parts_d)
    cd = chain(pk_d, halves)
    sums = step([cd], [], "after_wdown")
    gup, *pk_u, w_dn = hidden_bwd(me, cotangent, gp, n2t, parts_d, plan_d, w_down.shape[0], pin(sums))
    s0 = step([cd], far(gup), "after_hidden")
    if fast:
        pk_u = [pk_u[0]] + gate([pk_u[1]], s0)
    cu = chain(pk_u, halves)
    sums = step([cu], s0, "after_hidden_u")
    gmid, gatt, g_norm2, *pk_q = mid_bwd(me, cotangent, gup, mid, norms, w_ou, atts, pin(s0 + sums))
    sums = step([cd, cu], far(g_norm2), "after_mid")
    *d0, k, s = attn_bwd(0, bucket, me, heads[0], gatt, n1t, pk_q, 2, pin(sums))
    sums = step([cd, cu], far(d0[0]), "after_bwd0")
    *d1, k, s = attn_bwd(1, bucket, me, heads[1], gatt, n1t, (k, s), 4, pin(sums))
    s0 = step([cd, cu], far(d1[0]), "after_bwd1")
    pk_q = [k] + (gate([s], s0) if fast else [s])
    cq = chain(pk_q, ("xy", "h1", "h2", "h3"))
    sums = step([cq], s0, "after_bwd1_q")
    *d2, k, s = attn_bwd(2, bucket, me, heads[2], gatt, n1t, None, 0, pin(s0 + sums))
    s0 = step([cd, cu, cq], far(d2[0]), "after_bwd2")
    pk_r = [k] + (gate([s], s0) if fast else [s])
    cr = chain(pk_r, direct)
    sums = step([cr], s0, "after_bwd2_r")
    tokens_grad, g_norm1 = tail_bwd(tokens, d0 + d1 + d2, w_full, gmid, norms, pin(s0 + sums))
    sums = step([cu, cq, cr], far(g_norm1), "after_tail")
    mixed = mixed_out(mid, act, w_dn, pin(sums))
    sums = step([cq, cr], far(mixed), "after_mixed")
    step([cq, cr], sums, "last")
    g_norms = jnp.concatenate([g_norm1[:2], g_norm2[:2]], axis=0)

    if fast:
        g_norms = sum_everywhere(g_norms, n_fsdp, n_rep)
        (rows_d,), (rows_u,), (rows_q,), (rows_r,) = (c.mine for c in (cd, cu, cq, cr))
        gw_out = rows_q[:, :width]
        gw_q = jnp.concatenate([rows_q[:, width:], rows_r], axis=1)
    else:
        g_norms = lax.psum(g_norms, ("fsdp", "rep"))
        rows_q, rows_r, rows_u, rows_d = (whole(*pk) for pk in (pk_q, pk_r, pk_u, pk_d))
        gw_out = rows_q[:, :width]
        gw_q = jnp.concatenate([rows_q[:, width:], rows_r], axis=1)
    g_norms = lax.dynamic_slice_in_dim(g_norms, index * (width // n_fsdp), width // n_fsdp, axis=1)
    rows = gw_q.shape[0]
    gw_q = gw_q.reshape(rows, -1, 3, LANES).transpose(0, 2, 1, 3).reshape(rows, -1)
    grads = (gw_q, gw_out, rows_u, rows_d)
    if not fast:
        grads = tuple(
            lax.psum(lax.psum_scatter(g, "fsdp", scatter_dimension=0, tiled=True), "rep") for g in grads
        )
    gw_qkv, gw_out, gw_up, gw_down = (g.astype(f32) for g in grads)
    return (
        mixed,
        tokens_grad,
        g_norms[0],
        g_norms[1],
        gw_qkv,
        gw_out,
        g_norms[2],
        g_norms[3],
        gw_up,
        gw_down,
    )


def solution(mesh):
    return jax.shard_map(
        functools.partial(shards, mesh.shape["fsdp"], mesh.shape["rep"]),
        mesh=mesh,
        in_specs=(
            P(("rep", "fsdp"), None),
            P(("rep", "fsdp")),
            P("fsdp"),
            P("fsdp"),
            P("fsdp", None),
            P("fsdp", None),
            P("fsdp"),
            P("fsdp"),
            P("fsdp", None),
            P("fsdp", None),
            P(("rep", "fsdp"), None),
        ),
        out_specs=(
            P(("rep", "fsdp"), None),
            P(("rep", "fsdp"), None),
            P("fsdp"),
            P("fsdp"),
            P("fsdp", None),
            P("fsdp", None),
            P("fsdp"),
            P("fsdp"),
            P("fsdp", None),
            P("fsdp", None),
        ),
        check_vma=False,
    )
```

```python
import functools

import jax
import jax.numpy as jnp
from jax import lax
from jax.experimental import pallas as pl
from jax.experimental.pallas import tpu as pltpu
from jax.sharding import PartitionSpec as P

HEAD_DIM = 64
SHORT = 256
LN_EPS = 1e-6
LANES = 128
f32 = jnp.float32
bf16 = jnp.bfloat16

LOG2E = 1.4426950408889634
ROOT_2PI = (2 * 3.141592653589793) ** -0.5


def nt(a, b):
    return lax.dot_general(a, b, (((1,), (1,)), ((), ())), preferred_element_type=f32)


def nn(a, b):
    return lax.dot_general(a, b, (((1,), (0,)), ((), ())), preferred_element_type=f32)


def tn(a, b):
    return lax.dot_general(a, b, (((0,), (0,)), ((), ())), preferred_element_type=f32)


def ln_rows(x, gain, bias):
    centred = x - jnp.mean(x, axis=-1, keepdims=True)
    var = jnp.mean(centred * centred, axis=-1, keepdims=True)
    return centred * lax.rsqrt(var + LN_EPS) * gain + bias


def ln_back(grad, v, gain):
    centred = v - jnp.mean(v, axis=-1, keepdims=True)
    r = lax.rsqrt(jnp.mean(centred * centred, axis=-1, keepdims=True) + LN_EPS)
    xh = centred * r
    gg = grad * gain
    dx = r * (gg - jnp.mean(gg, axis=-1, keepdims=True) - xh * jnp.mean(gg * xh, axis=-1, keepdims=True))
    return dx, jnp.sum(grad * xh, axis=0, keepdims=True), jnp.sum(grad, axis=0, keepdims=True)


def gelu_pair(u):
    cdf = 0.5 + 0.5 * lax.erf(u * 2**-0.5)
    density = jnp.exp2((u * u) * (-0.5 * LOG2E))
    return u * cdf, cdf + (u * ROOT_2PI) * density


def terms(v):
    hi = v.astype(bf16).astype(f32)
    r = v - hi
    mid = r.astype(bf16).astype(f32)
    return hi, mid, r - mid


def spread(v, lane):
    hi, mid, lo = terms(-v)
    pos = lane & 63
    return jnp.where(pos == 0, hi, jnp.where(pos == 1, mid, jnp.where(pos == 2, lo, 0.0))).astype(bf16)


def unpack(refs, plan, me, shard_rows, jobs, sem):
    copies = []
    for ref, (r, lo) in zip(refs, plan):
        hi = lo + ref.shape[0]
        for (first, last), cols, dst, step in jobs(shard_rows):
            a, b = max(lo, first), min(hi, last)
            if a >= b:
                continue
            row = pl.multiple_of((me ^ r) * step, 16) + (a - first)
            copies.append(
                pltpu.make_async_copy(
                    ref.at[pl.ds(a - lo, b - a), cols], dst.at[pl.ds(row, b - a), :], sem.at[len(copies)]
                )
            )
    return copies


def run(copies):
    for c in copies:
        c.start()
    for c in copies:
        c.wait()


def put_slots(src_ref, outs, me, cols):
    keep, send = outs
    rows = src_ref.shape[0] // 8
    for r in range(8):
        row = pl.multiple_of((me ^ r) * rows, 16)
        (send if r & 1 else keep)[r >> 1, :, cols] = src_ref[pl.ds(row, rows), :]


def params(mib):
    return pltpu.CompilerParams(vmem_limit_bytes=mib << 20)


def cost(gflops, mib):
    return pl.CostEstimate(flops=1000, bytes_accessed=1024, transcendentals=0)


VMEM_MIB = 44
SMEM = pl.BlockSpec(memory_space=pltpu.SMEM)
ANY = pl.BlockSpec(memory_space=pl.ANY)
SHAPE = jax.ShapeDtypeStruct


def far(*arrays):
    return [pltpu.with_memory_space_constraint(a, pltpu.HBM) for a in arrays]


def in_hbm(shapes):
    return [pltpu.HBM(s.shape, s.dtype) for s in shapes]


def attend(bucket_ref, qb, n1, wq, wk, wv, qe_ref, k_ref, v_ref, att_ref, vx_ref):
    rows = k_ref.shape[0]
    low = lax.broadcasted_iota(jnp.int32, (rows, 128), 1) < 64
    q = nn(n1, wq)
    k_ref[...] = nn(n1, wk).astype(bf16)
    v = nn(n1, wv)
    v_ref[...] = v.astype(bf16)
    q = q * HEAD_DIM**-0.5
    for p in range(2):
        qp = q[:, 128 * p : 128 * p + 128]
        vp = v[:, 128 * p : 128 * p + 128]
        qe_ref[2 * p] = jnp.where(low, qp, 0.0).astype(bf16)
        qe_ref[2 * p + 1] = jnp.where(low, 0.0, qp).astype(bf16)
        vx_ref[2 * p] = jnp.where(low, vp, 1.0).astype(bf16)
        vx_ref[2 * p + 1] = jnp.where(low, 1.0, vp).astype(bf16)

    def block(r, kr):
        lane = lax.broadcasted_iota(jnp.int32, (r.size, 128), 1)
        lowq = lane < 64
        ss = [nt(qe_ref[h, r, :], k_ref[kr, 128 * (h // 2) : 128 * (h // 2) + 128]) for h in range(4)]
        for p in range(2):
            os, tops = [], []
            for h in (2 * p, 2 * p + 1):
                top = jnp.max(ss[h], axis=-1, keepdims=True)
                e = jnp.exp(ss[h] - top).astype(bf16)
                os.append(nn(e, vx_ref[h, kr, :]))
                tops.append(top)
            sums = jnp.where(lowq, os[1], os[0])
            lse = jnp.where(lowq, tops[1], tops[0]) + jnp.log(sums)
            rest = spread(lse, lane)
            q0, q1 = qe_ref[2 * p, r, :], qe_ref[2 * p + 1, r, :]
            qe_ref[2 * p, r, :] = jnp.where(lowq, q0, rest)
            qe_ref[2 * p + 1, r, :] = jnp.where(lowq, rest, q1)
            att = jnp.where(lowq, os[0], os[1]) / pltpu.roll(sums, 64, 1)
            att_ref[r, 128 * p : 128 * p + 128] = att.astype(bf16)

    is_long = bucket_ref[0] == 1

    @pl.when(is_long)
    def _():
        def body(i, _):
            block(pl.ds(i * qb, qb), slice(None))
            return 0

        lax.fori_loop(0, rows // qb, body, 0)

    @pl.when(jnp.logical_not(is_long))
    def _():
        def body(i, _):
            r = pl.ds(i * SHORT, SHORT)
            block(r, r)
            return 0

        lax.fori_loop(0, rows // SHORT, body, 0)


def q_jobs(w_ref, raw_ref):
    width = w_ref.shape[0]
    return lambda shard: [
        ((0, shard), slice(None), w_ref, shard),
        ((shard, shard + 16), slice(0, width), raw_ref, 16),
    ]


def fwd_first_kernel(plan, shard, n_parts, bucket_ref, me_ref, x_ref, *refs):
    parts = refs[:n_parts]
    n1_ref, n1t_ref, norm_ref, whbm_ref, qe_ref, k_ref, v_ref, att_ref, w_ref, raw_ref, vx_ref, sem = refs[n_parts:]
    rows, width = x_ref.shape
    run(unpack(parts, plan, me_ref[0], shard, q_jobs(w_ref, raw_ref), sem))
    keep = pltpu.make_async_copy(w_ref, whbm_ref, sem.at[0])
    keep.start()
    total = raw_ref[0:16, :].astype(f32)
    for i in range(1, raw_ref.shape[0] // 16):
        total = total + raw_ref[16 * i : 16 * i + 16, :].astype(f32)
    norm_ref[...] = total

    def body(i, _):
        r = pl.ds(i * 128, 128)
        n1_ref[r, :] = ln_rows(x_ref[r, :].astype(f32), norm_ref[0:1, :], norm_ref[1:2, :]).astype(bf16)
        return 0

    lax.fori_loop(0, rows // 128, body, 0)
    n1t_ref[...] = n1_ref[...].T
    w = [w_ref[:, width * i : width * i + 256] for i in range(3)]
    attend(bucket_ref, 512, n1_ref[...], *w, qe_ref, k_ref, v_ref, att_ref, vx_ref)
    keep.wait()


def fwd_next_kernel(n_pins, bucket_ref, n1_ref, wq_ref, wk_ref, wv_ref, *refs):
    attend(bucket_ref, 512, n1_ref[...], wq_ref[...], wk_ref[...], wv_ref[...], *refs[n_pins:])


def head_shapes(rows):
    return [SHAPE((4, rows, 128), bf16)] + [SHAPE((rows, 256), bf16)] * 3


def forward_first(bucket, me, x, parts, plan, shard, pins):
    rows, width = x.shape
    full = lambda *s: pl.BlockSpec(s, lambda i: (0,) * len(s))
    shapes = [
        SHAPE((rows, width), bf16),
        SHAPE((width, rows), bf16),
        SHAPE((16, width), f32),
        SHAPE((width, 3 * width), bf16),
    ] + head_shapes(rows)
    return pl.pallas_call(
        lambda b, m, xr, *refs: fwd_first_kernel(
            plan, shard, len(parts), b, m, xr, *refs[: len(parts)], *refs[len(parts) + len(pins) :]
        ),
        grid=(1,),
        in_specs=[SMEM, SMEM, full(rows, width)] + [ANY] * (len(parts) + len(pins)),
        out_specs=[full(*s.shape) for s in shapes[:3]] + [ANY] + [full(*s.shape) for s in shapes[4:]],
        out_shape=in_hbm(shapes),
        scratch_shapes=[
            pltpu.VMEM((width, 3 * width), bf16),
            pltpu.VMEM((width // shard * 16, width), bf16),
            pltpu.VMEM((4, rows, 128), bf16),
            pltpu.SemaphoreType.DMA((32,)),
        ],
        compiler_params=params(VMEM_MIB),
        cost_estimate=cost(8, 12),
        name="fwd_a",
    )(bucket, me, *far(x, *parts), *pins)


def forward_next(g, bucket, n1, w, pins):
    rows, width = n1.shape
    groups = width // 256
    col = lambda j: pl.BlockSpec((width, 256), lambda i: (0, j * groups + g))
    full = lambda *s: pl.BlockSpec(s, lambda i: (0,) * len(s))
    shapes = head_shapes(rows)
    return pl.pallas_call(
        functools.partial(fwd_next_kernel, len(pins)),
        grid=(1,),
        in_specs=[SMEM, full(rows, width), col(0), col(1), col(2)] + [ANY] * len(pins),
        out_specs=[full(*s.shape) for s in shapes],
        out_shape=in_hbm(shapes),
        scratch_shapes=[pltpu.VMEM((4, rows, 128), bf16)],
        compiler_params=params(VMEM_MIB),
        cost_estimate=cost(8, 8),
        name=f"attn_{g}",
    )(bucket, *far(n1, w, w, w), *pins)


UPN = 512
HIDN = 512


def up_kernel(plan, shard, n_parts, me_ref, x_ref, a0, a1, a2, norm_ref, *refs):
    parts = refs[:n_parts]
    mid_ref, n2t_ref, act_ref, gp_ref, wou_hbm, wo_ref, wu_ref, sem, sem2 = refs[n_parts:]
    width = x_ref.shape[1]
    saves = [
        pltpu.make_async_copy(wo_ref, wou_hbm.at[:, :width], sem2.at[0]),
        pltpu.make_async_copy(wu_ref, wou_hbm.at[:, width:], sem2.at[1]),
    ]

    @pl.when(pl.program_id(0) == 0)
    def _():
        jobs = lambda s: [
            ((0, s), slice(0, width), wo_ref, s),
            ((0, s), slice(width, None), wu_ref, s),
        ]
        run(unpack(parts, plan, me_ref[0], shard, jobs, sem))
        for c in saves:
            c.start()

    att = jnp.concatenate([a0[...], a1[...], a2[...]], axis=1)
    mid = x_ref[...].astype(f32) + nn(att, wo_ref[...])
    mid_ref[...] = mid
    n2 = ln_rows(mid, norm_ref[2:3, :], norm_ref[3:4, :]).astype(bf16)
    n2t_ref[...] = n2.T
    for b in range(wu_ref.shape[1] // UPN):
        c = slice(UPN * b, UPN * b + UPN)
        act, gp = gelu_pair(nn(n2, wu_ref[:, c]))
        act_ref[:, c] = act.astype(bf16)
        gp_ref[:, c] = gp.astype(bf16)

    @pl.when(pl.program_id(0) == pl.num_programs(0) - 1)
    def _():
        for c in saves:
            c.wait()


def up_proj(me, x, atts, norms, parts, plan, shard, pins, rb=256):
    rows, width = x.shape
    hidden = parts[0].shape[1] - width
    row = lambda n: pl.BlockSpec((rb, n), lambda i: (i, 0))
    full = lambda *s: pl.BlockSpec(s, lambda i: (0,) * len(s))
    n = len(parts)
    return pl.pallas_call(
        lambda m, xr, a0, a1, a2, nr, *refs: up_kernel(
            plan, shard, n, m, xr, a0, a1, a2, nr, *refs[:n], *refs[n + len(pins) :]
        ),
        grid=(rows // rb,),
        in_specs=[SMEM, row(width)] + [row(256)] * 3 + [full(16, width)] + [ANY] * (n + len(pins)),
        out_specs=[row(width), pl.BlockSpec((width, rb), lambda i: (0, i)), row(hidden), row(hidden), ANY],
        out_shape=in_hbm([
            SHAPE((rows, width), f32),
            SHAPE((width, rows), bf16),
            SHAPE((rows, hidden), bf16),
            SHAPE((rows, hidden), bf16),
            SHAPE((width, width + hidden), bf16),
        ]),
        scratch_shapes=[
            pltpu.VMEM((width, width), bf16),
            pltpu.VMEM((width, hidden), bf16),
            pltpu.SemaphoreType.DMA((32,)),
            pltpu.SemaphoreType.DMA((2,)),
        ],
        compiler_params=params(VMEM_MIB),
        cost_estimate=cost(9, 20),
        name="up_proj",
    )(me, *far(x, *atts, norms), *parts, *pins)


def shard_of(i):
    return jnp.where(i < 4, 2 * i + 1, 2 * i - 8)


def wdown_kernel(n_pins, me_ref, act_ref, dy_ref, *refs):
    keep_ref, send_ref = refs[n_pins:]
    g = tn(act_ref[...], dy_ref[...]).astype(bf16)
    i = pl.program_id(0)

    @pl.when(i < 4)
    def _():
        send_ref[0] = g

    @pl.when(i >= 4)
    def _():
        keep_ref[0] = g


def wdown_grad(me, act, dy, pins):
    rows, width = dy.shape
    shard = act.shape[1] // 8
    out = SHAPE((4, shard, width), bf16)
    return pl.pallas_call(
        functools.partial(wdown_kernel, len(pins)),
        grid_spec=pltpu.PrefetchScalarGridSpec(
            num_scalar_prefetch=1,
            grid=(8,),
            in_specs=[
                pl.BlockSpec((rows, shard), lambda i, m: (0, m[0] ^ shard_of(i))),
                pl.BlockSpec((rows, width), lambda i, m: (0, 0)),
            ]
            + [ANY] * len(pins),
            out_specs=[
                pl.BlockSpec((1, shard, width), lambda i, m: (jnp.maximum(i - 4, 0), 0, 0)),
                pl.BlockSpec((1, shard, width), lambda i, m: (jnp.minimum(i, 3), 0, 0)),
            ],
        ),
        out_shape=[out, out],
        compiler_params=params(VMEM_MIB),
        cost_estimate=cost(5, 13),
        name="wdown_grad",
    )(me, *far(act, dy), *pins)


def hidden_kernel(plan, shard, n_parts, me_ref, dy_ref, gp_ref, n2t_ref, *refs):
    parts = refs[:n_parts]
    gup_ref, keep_ref, send_ref, wd_hbm, wd_ref, g_ref, sem, sem2 = refs[n_parts:]
    i = pl.program_id(0)
    save = pltpu.make_async_copy(wd_ref, wd_hbm, sem2.at[0])

    @pl.when(i == 0)
    def _():
        run(unpack(parts, plan, me_ref[0], shard, lambda s: [((0, s), slice(None), wd_ref, s)], sem))
        save.start()

    fb = gp_ref.shape[1]
    for b in range(fb // HIDN):
        c = slice(HIDN * b, HIDN * b + HIDN)
        w = wd_ref[pl.ds(pl.multiple_of(i * fb, 256) + HIDN * b, HIDN), :]
        gup_ref[:, c] = (nt(dy_ref[...], w) * gp_ref[:, c].astype(f32)).astype(bf16)
        g_ref[:, c] = nn(n2t_ref[...], gup_ref[:, c]).astype(bf16)
    put_slots(g_ref, (keep_ref, send_ref), me_ref[0], slice(None))

    @pl.when(i == pl.num_programs(0) - 1)
    def _():
        save.wait()


def hidden_bwd(me, dy, gp, n2t, parts, plan, shard, pins, fb=512):
    rows, width = dy.shape
    hidden = gp.shape[1]
    full = lambda *s: pl.BlockSpec(s, lambda i: (0,) * len(s))
    col = pl.BlockSpec((rows, fb), lambda i: (0, i))
    out = SHAPE((4, width // 8, hidden), bf16)
    spec = pl.BlockSpec((4, width // 8, fb), lambda i: (0, 0, i))
    n = len(parts)
    return pl.pallas_call(
        lambda m, a, b, c, *refs: hidden_kernel(plan, shard, n, m, a, b, c, *refs[:n], *refs[n + len(pins) :]),
        grid=(hidden // fb,),
        in_specs=[SMEM, full(rows, width), col, full(width, rows)] + [ANY] * (n + len(pins)),
        out_specs=[col, spec, spec, ANY],
        out_shape=in_hbm([SHAPE((rows, hidden), bf16)]) + [out, out] + in_hbm([SHAPE((hidden, width), bf16)]),
        scratch_shapes=[
            pltpu.VMEM((hidden, width), bf16),
            pltpu.VMEM((width, fb), bf16),
            pltpu.SemaphoreType.DMA((32,)),
            pltpu.SemaphoreType.DMA((1,)),
        ],
        compiler_params=params(VMEM_MIB),
        cost_estimate=cost(10, 26),
        name="hidden_bwd",
    )(me, *far(dy, gp, n2t), *parts, *pins)


def mid_kernel(n_pins, me_ref, dy_ref, gup_ref, mid_ref, norm_ref, wou_ref, a0, a1, a2, *refs):
    gmid_ref, gatt_ref, gg_ref, keep_ref, send_ref, gmb_ref, g_ref = refs[n_pins:]
    rb, width = dy_ref.shape
    i = pl.program_id(0)

    @pl.when(i == 0)
    def _():
        gg_ref[...] = jnp.zeros_like(gg_ref)

    gn2 = nt(gup_ref[...], wou_ref[:, width:])
    dx, dg, db = ln_back(gn2, mid_ref[...], norm_ref[2:3, :])
    gm = dy_ref[...].astype(f32) + dx
    gmid_ref[...] = gm
    gmb = gm.astype(bf16)
    gmb_ref[pl.ds(pl.multiple_of(i * rb, rb), rb), :] = gmb
    gg_ref[0:1, :] += dg
    gg_ref[1:2, :] += db
    gatt_ref[...] = nt(gmb, wou_ref[:, :width]).astype(bf16)

    @pl.when(i == pl.num_programs(0) - 1)
    def _():
        for j, a in enumerate((a0, a1, a2)):
            g_ref[256 * j : 256 * j + 256, :] = tn(a[...], gmb_ref[...]).astype(bf16)
        put_slots(g_ref, (keep_ref, send_ref), me_ref[0], slice(None))


def mid_bwd(me, dy, gup, mid, norms, wou, atts, pins, rb=256):
    rows, width = dy.shape
    hidden = gup.shape[1]
    row = lambda n: pl.BlockSpec((rb, n), lambda i: (i, 0))
    full = lambda *s: pl.BlockSpec(s, lambda i: (0,) * len(s))
    once = lambda *s: pl.BlockSpec(s, lambda i: (0,) * len(s), pipeline_mode=pl.Buffered(1))
    out = SHAPE((4, width // 8, 2 * width), bf16)
    spec = pl.BlockSpec((4, width // 8, width), lambda i: (0, 0, 0))
    return pl.pallas_call(
        functools.partial(mid_kernel, len(pins)),
        grid=(rows // rb,),
        in_specs=[SMEM, row(width), row(hidden), row(width), full(16, width), once(width, width + hidden)]
        + [full(rows, 256)] * 3
        + [ANY] * len(pins),
        out_specs=[row(width), row(width), full(8, width), spec, spec],
        out_shape=in_hbm([SHAPE((rows, width), f32), SHAPE((rows, width), bf16), SHAPE((8, width), f32)]) + [out, out],
        scratch_shapes=[pltpu.VMEM((rows, width), bf16), pltpu.VMEM((width, width), bf16)],
        compiler_params=params(VMEM_MIB),
        cost_estimate=cost(8, 24),
        name="mid_bwd",
    )(me, *far(dy, gup, mid, norms, wou, *atts), *pins)


def bwd_kernel(kb, n_pins, bucket_ref, me_ref, qe_ref, k_ref, v_ref, att_ref, do_ref, n1t_hbm, *refs):
    dq_ref, dk_ref, dv_ref, keep_ref, send_ref, doe_ref, ke_ref, ve_ref, dqa_ref, g_ref, n1t_ref, sem = refs[n_pins:]
    rows = k_ref.shape[0]
    load = pltpu.make_async_copy(n1t_hbm, n1t_ref, sem.at[0])

    @pl.when(pl.program_id(0) == 0)
    def _():
        load.start()

    lane = lax.broadcasted_iota(jnp.int32, (rows, 128), 1)
    low = lane < 64
    do, k, v = do_ref[...], k_ref[...], v_ref[...]
    across = lambda i: lax.broadcasted_iota(jnp.int32, (128, 128), i) // 64
    other = jnp.where(across(0) + across(1) == 1, 1.0, 0.0).astype(bf16)
    d = sum(nn(t.astype(bf16), other) for t in terms(do.astype(f32) * att_ref[...].astype(f32)))
    rest = spread(d, lane)
    ones = jnp.where((lane & 63) < 3, 1.0, 0.0).astype(bf16)
    for j in range(2):
        own = low if j == 0 else ~low
        doe_ref[j] = jnp.where(own, do, rest)
        ke_ref[j] = jnp.where(own, k, ones)
        ve_ref[j] = jnp.where(own, v, ones)

    def block(kr, qr):
        lowk = lax.broadcasted_iota(jnp.int32, (kr.size, 128), 1) < 64
        dks, dvs, dqs = [], [], []
        sts = [nt(ke_ref[j, kr, :], qe_ref[j, qr, :]) for j in range(2)]
        dpts = [nt(ve_ref[j, kr, :], doe_ref[j, qr, :]) for j in range(2)]
        for j in range(2):
            pt = jnp.exp(sts[j])
            ds = (pt * dpts[j]).astype(bf16)
            dvs.append(nn(pt.astype(bf16), do_ref[qr, :]))
            dks.append(nn(ds, qe_ref[j, qr, :]))
            dqs.append(tn(k_ref[kr, :], ds).T)
        dk_ref[kr, :] = jnp.where(lowk, dks[0], dks[1]).astype(bf16)
        dv_ref[kr, :] = jnp.where(lowk, dvs[0], dvs[1]).astype(bf16)
        return dqs

    is_long = bucket_ref[0] == 1

    @pl.when(is_long)
    def _():
        if kb == rows:
            dqs = block(pl.ds(0, rows), slice(None))
            dq_ref[...] = (jnp.where(low, dqs[0], dqs[1]) * HEAD_DIM**-0.5).astype(bf16)
            return
        dqa_ref[...] = jnp.zeros_like(dqa_ref)

        def body(i, _):
            dqs = block(pl.ds(i * kb, kb), slice(None))
            dqa_ref[...] += jnp.where(low, dqs[0], dqs[1])
            return 0

        lax.fori_loop(0, rows // kb, body, 0)
        dq_ref[...] = (dqa_ref[...] * HEAD_DIM**-0.5).astype(bf16)

    @pl.when(jnp.logical_not(is_long))
    def _():
        lows = lax.broadcasted_iota(jnp.int32, (SHORT, 128), 1) < 64

        def body(i, _):
            r = pl.ds(i * SHORT, SHORT)
            dqs = block(r, r)
            dq_ref[r, :] = (jnp.where(lows, dqs[0], dqs[1]) * HEAD_DIM**-0.5).astype(bf16)
            return 0

        lax.fori_loop(0, rows // SHORT, body, 0)

    @pl.when(pl.program_id(0) == 0)
    def _():
        load.wait()

    g_ref[...] = nn(n1t_ref[...], jnp.concatenate([dq_ref[...], dk_ref[...], dv_ref[...]], axis=1)).astype(bf16)
    put_slots(g_ref, (keep_ref, send_ref), me_ref[0], slice(None))


def attn_bwd(g, bucket, me, heads, gatt, n1t, into, first, pins):
    qe, k, v, att = heads
    rows = k.shape[0]
    width = n1t.shape[0]
    col = pl.BlockSpec((rows, 128), lambda i: (0, i))
    out = SHAPE(into[0].shape if into else (4, width // 8, 768), bf16)
    spec = pl.BlockSpec((4, width // 8, 384), lambda i: (0, 0, first + i))
    into = list(into or [])
    return pl.pallas_call(
        functools.partial(bwd_kernel, 1024, len(into) + len(pins)),
        grid=(2,),
        in_specs=[
            SMEM,
            SMEM,
            pl.BlockSpec((2, rows, 128), lambda i: (i, 0, 0)),
            col,
            col,
            col,
            pl.BlockSpec((rows, 128), lambda i: (0, 2 * g + i)),
        ]
        + [ANY] * (1 + len(into) + len(pins)),
        input_output_aliases={8 + i: 3 + i for i in range(len(into))},
        out_specs=[col] * 3 + [spec] * 2,
        out_shape=in_hbm([SHAPE((rows, 256), bf16)] * 3) + [out, out],
        scratch_shapes=[pltpu.VMEM((2, rows, 128), bf16)] * 3
        + [
            pltpu.VMEM((rows, 128), f32),
            pltpu.VMEM((width, 384), bf16),
            pltpu.VMEM((width, rows), bf16),
            pltpu.SemaphoreType.DMA((1,)),
        ],
        compiler_params=params(VMEM_MIB),
        cost_estimate=cost(14, 8),
        name=f"attn_bwd_{g}",
    )(bucket, me, *far(qe, k, v, att, gatt, n1t), *into, *pins)


def tail_kernel(n_pins, x_ref, *refs):
    ds = refs[:9]
    w_ref, gmid_ref, norm_ref = refs[9:12]
    tg_ref, gg_ref = refs[12 + n_pins :]

    @pl.when(pl.program_id(0) == 0)
    def _():
        gg_ref[...] = jnp.zeros_like(gg_ref)

    d = jnp.concatenate([ds[3 * g + j][...] for j in range(3) for g in range(3)], axis=1)
    dx, dg, db = ln_back(nt(d, w_ref[...]), x_ref[...].astype(f32), norm_ref[0:1, :])
    tg_ref[...] = (gmid_ref[...] + dx).astype(bf16)
    gg_ref[0:1, :] += dg
    gg_ref[1:2, :] += db


def tail_bwd(x, ds, w, gmid, norms, pins, rb=256):
    rows, width = x.shape
    row = lambda n: pl.BlockSpec((rb, n), lambda i: (i, 0))
    full = lambda *s: pl.BlockSpec(s, lambda i: (0,) * len(s))
    once = lambda *s: pl.BlockSpec(s, lambda i: (0,) * len(s), pipeline_mode=pl.Buffered(1))
    return pl.pallas_call(
        functools.partial(tail_kernel, len(pins)),
        grid=(rows // rb,),
        in_specs=[row(width)] + [row(256)] * 9 + [once(width, 3 * width), row(width), full(16, width)] + [ANY] * len(pins),
        out_specs=[row(width), full(8, width)],
        out_shape=in_hbm([SHAPE((rows, width), bf16), SHAPE((8, width), f32)]),
        compiler_params=params(VMEM_MIB),
        cost_estimate=cost(5, 16),
        name="tail_bwd",
    )(*far(x, *ds, w, gmid, norms), *pins)


def mixed_kernel(n_pins, mid_ref, act_ref, wd_ref, *refs):
    refs[n_pins][...] = (mid_ref[...] + nn(act_ref[...], wd_ref[...])).astype(bf16)


def mixed_out(mid, act, wd, pins, rb=256):
    rows, width = mid.shape
    hidden = act.shape[1]
    row = lambda n: pl.BlockSpec((rb, n), lambda i: (i, 0))
    once = pl.BlockSpec((hidden, width), lambda i: (0, 0), pipeline_mode=pl.Buffered(1))
    return pl.pallas_call(
        functools.partial(mixed_kernel, len(pins)),
        grid=(rows // rb,),
        in_specs=[row(width), row(hidden), once] + [ANY] * len(pins),
        out_specs=row(width),
        out_shape=in_hbm([SHAPE((rows, width), bf16)])[0],
        compiler_params=params(VMEM_MIB),
        cost_estimate=cost(5, 16),
        name="mixed_out",
    )(*far(mid, act, wd), *pins)


def packet_kernel(n_in, *refs):
    ins, out_ref = refs[:n_in], refs[-1]
    col = 0
    for v in ins:
        out_ref[:, col : col + v.shape[1]] = v[...]
        col += v.shape[1]


def packet(arrays, pins, name):
    rows, cols = arrays[0].shape[0], sum(a.shape[1] for a in arrays)
    full = lambda *s: pl.BlockSpec(s, lambda i: (0,) * len(s))
    return pl.pallas_call(
        functools.partial(packet_kernel, len(arrays)),
        grid=(1,),
        in_specs=[full(*a.shape) for a in arrays] + [ANY] * len(pins),
        out_specs=full(rows, cols),
        out_shape=SHAPE((rows, cols), bf16),
        compiler_params=params(8),
        cost_estimate=cost(0, 2),
        name=name,
    )(*arrays, *pins)


def gate(arrays, pins):
    n = len(arrays)
    if not pins:
        return list(arrays)
    return list(pl.pallas_call(
        lambda *refs: None,
        in_specs=[ANY] * (n + len(pins)),
        out_specs=[ANY] * n,
        out_shape=[SHAPE(a.shape, a.dtype) for a in arrays],
        input_output_aliases={i: i for i in range(n)},
        compiler_params=params(1),
        cost_estimate=cost(0, 0),
        name="gate",
    )(*arrays, *pins))


def total(*vs):
    out = vs[0].astype(f32)
    for v in vs[1:]:
        out = out + v.astype(f32)
    return out.astype(bf16)


def combine_kernel(plan, n_in, n_pins, odd_ref, *refs):
    outs = refs[n_in + n_pins :]
    odd = odd_ref[0] == 1
    at = 0
    for f, spots, n_out in plan:
        values = f(odd, *[refs[i] for i in spots])
        for v in values:
            outs[at][...] = v.astype(outs[at].dtype)
            at += 1


def combine(jobs, odd, pins, name, grid=1):
    arrays, shapes, plan = [], [], []
    for f, ins, outs in jobs:
        spots = []
        for a in ins:
            known = [i for i, b in enumerate(arrays) if b is a]
            spots.append(known[0] if known else len(arrays))
            if not known:
                arrays.append(a)
        plan.append((f, spots, len(outs)))
        shapes += [o if isinstance(o, SHAPE) else SHAPE(o, bf16) for o in outs]
    block = lambda s: pl.BlockSpec(s[:-1] + (s[-1] // grid,), lambda i: (0,) * (len(s) - 1) + (i,))
    sums = pl.pallas_call(
        functools.partial(combine_kernel, plan, len(arrays), len(pins)),
        grid=(grid,),
        in_specs=[SMEM] + [block(a.shape) for a in arrays] + [ANY] * len(pins),
        out_specs=[block(s.shape) for s in shapes],
        out_shape=shapes,
        compiler_params=params(24),
        cost_estimate=cost(0, 4),
        name=name,
    )(odd, *arrays, *pins)
    return list(sums)


def swap(v, axis, size, m):
    return lax.ppermute(v, axis, [(i, i ^ m) for i in range(size)])


def part_plan(cut):
    return [(0, 0), (1, 0), (2, 0), (4, 0), (6, 0), (6, cut), (3, 0), (5, 0), (7, 0), (7, cut)]


class Gather:
    def __init__(self, own, cut, size):
        self.own, self.cut, self.size = own, cut, size

    def near(self):
        self.rx, self.ry = (swap(self.own, "fsdp", self.size, m) for m in (2, 4))
        return [self.rx, self.ry]

    def halves(self):
        n, cols = self.own.shape
        return (
            lambda odd, x, y: (y[: self.cut, :], x[self.cut :, :]),
            [self.rx, self.ry],
            [(self.cut, cols), (n - self.cut, cols)],
        )

    def opposite(self, to_x, to_y):
        self.da, self.db = swap(to_x, "fsdp", self.size, 2), swap(to_y, "fsdp", self.size, 4)
        return [self.da, self.db]

    def core_near(self):
        self.rc, *self.near_c = [swap(v, "fsdp", self.size, 1) for v in (self.own, self.rx, self.ry)]

    def parts(self):
        opp = [self.da, self.db]
        return [self.own, self.rc, self.rx, self.ry] + opp + self.near_c + [swap(v, "fsdp", self.size, 1) for v in opp]


class Chain:
    def __init__(self, packets, plan, n_fsdp, n_rep):
        self.mine, self.got = [], []
        self.plan = ("core",) + plan
        self.at = 0
        self.f = lambda v, m: swap(v, "fsdp", n_fsdp, m)
        self.z = lambda v, m: swap(v, "rep", n_rep, m)
        self.join(packets)

    def join(self, packets):
        keep, send = packets
        self.mine.append(keep)
        self.got.append(self.f(send, 1))
        self.shape = (keep.shape[1], sum(k.shape[2] for k in self.mine))

    def job(self):
        done = self.plan[self.at]
        then = self.plan[self.at + 1] if self.at + 1 < len(self.plan) else None
        rows, cols = self.shape
        h = rows // 2
        whole, half = (rows, cols), (h, cols)
        if done == "core" and then == "xy":

            def f(odd, *vs):
                n = len(vs) // 2
                pairs = list(zip(vs[:n], vs[n:]))
                return tuple(jnp.concatenate([total(k[s], g[s]) for k, g in pairs], axis=1) for s in range(4))

            return f, self.mine + self.got, [whole] * 4
        if done == "core":

            def f(odd, k, g):
                part = lambda s, t, lo: jnp.stack([total(k[i, lo : lo + h, :], g[i, lo : lo + h, :]) for i in (s, t)])
                return part(0, 2, 0), part(0, 1, h), part(1, 3, 0), part(2, 3, h)

            return f, self.mine + self.got, [(2,) + half] * 4
        if done == "a":
            f = lambda odd, a, b, ra, rb: (total(a[0], ra[0]), total(b[0], rb[0]), total(a[1], ra[1]), total(b[1], rb[1]))
            return f, self.mine + self.got, [half] * 4
        if done in ("b", "xy"):

            def f(odd, *vs):
                if done == "b":
                    a, b, ra, rb = vs
                    lo, hi = total(a[...], ra[...]), total(b[...], rb[...])
                else:
                    lo, hi = (total(*[v[r, :] for v in vs]) for r in (slice(0, h), slice(h, rows)))
                if then == "p1":
                    return (jnp.concatenate([lo, hi], axis=0),)
                return jnp.where(odd, hi, lo), jnp.where(odd, lo, hi)

            return f, self.mine + self.got, [whole] if then == "p1" else [half] * 2
        if done == "h3":

            def f(odd, p, o):
                p, o = p[...], o[...]
                return (jnp.concatenate([jnp.where(odd, o, p), jnp.where(odd, p, o)], axis=0),)

            return f, self.mine + self.got, [SHAPE(whole, f32)]
        out = half if done[0] == "h" else whole
        return (lambda odd, a, b: (total(a[...], b[...]),)), self.mine + self.got, [out if then else SHAPE(out, f32)]

    def go(self, sums):
        self.at += 1
        step = self.plan[self.at] if self.at < len(self.plan) else None
        if step == "xy":
            self.mine, out = sums[:1], sums[1:]
            self.got = [self.f(v, m) for v, m in zip(out, (2, 4, 6))]
        elif step in ("a", "b"):
            self.mine, out = sums[:2], sums[2:]
            self.got = [self.f(v, m) for v, m in zip(out, (2, 4) if step == "a" else (4, 2))]
        elif step == "h1":
            self.mine, self.got = sums[:1], [self.z(sums[1], 1)]
        else:
            self.mine = sums
            self.got = [self.z(sums[0], 2 if step in ("h2", "p2") else 1)] if step else []


def advance(chains, extra, odd, pins, name, grid=1):
    jobs = [c.job() for c in chains] + extra
    sums = combine(jobs, odd, pins, name, grid)
    at = 0
    for c, job in zip(chains, jobs):
        c.go(sums[at : at + len(job[2])])
        at += len(job[2])
    return sums, sums[at:]


def sum_chips(v, size):
    x, y, d = (swap(v, "fsdp", size, m) for m in (2, 4, 6))
    return (v + x) + (y + d)


def sum_replicas(v, size):
    a, b, c = (swap(v, "rep", size, m) for m in (1, 2, 3))
    return (v + a) + (b + c)


def whole(keep, send):
    return jnp.stack([keep, send], axis=1).reshape(-1, keep.shape[2])


def shards(
    n_fsdp, n_rep, tokens, bucket, ln1_gain, ln1_bias, w_qkv, w_out, ln2_gain, ln2_bias, w_up, w_down, cotangent
):
    width = tokens.shape[1]
    fast = n_fsdp == 8 and n_rep == 4
    index = lax.axis_index("fsdp")
    vectors = jnp.stack([ln1_gain, ln1_bias, ln2_gain, ln2_bias])
    if fast:
        me = jnp.reshape(index, (1,)).astype(jnp.int32)
        owner = lax.broadcasted_iota(jnp.int32, (4, width), 1) // (width // 8)
        spread = jnp.where(owner == index, jnp.tile(vectors, (1, 8)), 0)
    else:
        me = jnp.zeros((1,), jnp.int32)
        spread = lax.all_gather(vectors, "fsdp", axis=1, tiled=True)
        w_qkv, w_out, w_up, w_down = (
            lax.all_gather(w, "fsdp", axis=0, tiled=True) for w in (w_qkv, w_out, w_up, w_down)
        )
    local = w_qkv.shape[0]
    norm_rows = jnp.pad(spread, ((0, 12), (0, w_qkv.shape[1] - width)))
    packet_q = jnp.concatenate([w_qkv, norm_rows], axis=0)
    cut, cut_d = local // 2, w_down.shape[0] // 2
    none = [(0, 0)]
    odd = jnp.reshape(lax.axis_index("rep") & 1, (1,)).astype(jnp.int32)

    if fast:
        gq = Gather(packet_q, cut, n_fsdp)
        gq.near()
        far_q = gq.opposite(gq.ry[:cut], gq.rx[cut:])
        gq.core_near()
        (own_u,) = gate([packet([w_out, w_up], [], "packet_up")], far_q)
        gu = Gather(own_u, cut, n_fsdp)
        near_u = gu.near()
        gd = Gather(None, cut_d, n_fsdp)
        plan, plan_d = part_plan(cut), part_plan(cut_d)
        parts_q = gq.parts()
    else:
        plan, plan_d = none, none
        parts_q = [packet_q]

    def pin(v):
        return list(v) if fast else []

    n1, n1t, norms, w_full, *heads0 = forward_first(
        bucket, me, tokens, parts_q, plan, local, pin([own_u] if fast else [])
    )
    sums = []
    if fast:
        sums, (to_x, to_y, own_d) = advance(
            [], [gu.halves(), (lambda o, w: (w[...],), [w_down], [w_down.shape])], odd, far(n1t), "after_a"
        )
        gu.opposite(to_x, to_y)
        gu.rx, gu.ry = gate([gu.rx, gu.ry], far(n1t))
        (gu.own,) = gate([gu.own], far(n1t))
        gu.core_near()
    heads1 = forward_next(1, bucket, n1, w_full, pin(sums))
    sums = []
    if fast:
        gu.da, gu.db, gd.own, gu.rc, *gu.near_c = gate([gu.da, gu.db, own_d, gu.rc] + gu.near_c, far(heads1[3]))
        sums = [gd.own]
        gd.near()
        parts_u = gu.parts()
    heads2 = forward_next(2, bucket, n1, w_full, pin(sums))
    heads = [heads0, heads1, heads2]
    atts = [h[3] for h in heads]
    if fast:
        sums, (to_x, to_y) = advance([], [gd.halves()], odd, far(heads2[3]), "after_c")
        gd.opposite(to_x, to_y)
        gd.core_near()
    else:
        parts_u = [packet([w_out, w_up], [], "packet_up")]
    mid, n2t, act, gp, w_ou = up_proj(me, tokens, atts, norms, parts_u, plan, local, pin(sums))
    if fast:
        gd.da, gd.db = gate([gd.da, gd.db], far(n2t))
        parts_d = gd.parts()
    else:
        parts_d = [w_down]
    pk_d = wdown_grad(me, act, cotangent, pin([gd.da, gd.db] if fast else []))
    halves, direct = ("a", "b", "h1", "h2", "h3"), ("xy", "p1", "p2")
    chain = lambda pk, plan: Chain(pk, plan, n_fsdp, n_rep) if fast else None

    def step(chains, after, name):
        return advance(chains, [], odd, after, name)[0][-1:] if fast else []

    if fast:
        pk_d = [pk_d[0]] + gate([pk_d[1]], parts_d)
    cd = chain(pk_d, halves)
    sums = step([cd], [], "after_wdown")
    gup, *pk_u, w_dn = hidden_bwd(me, cotangent, gp, n2t, parts_d, plan_d, w_down.shape[0], pin(sums))
    sums = step([cd], far(gup), "after_hidden")
    if fast:
        pk_u = [pk_u[0]] + gate([pk_u[1]], sums)
    cu = chain(pk_u, halves)
    gmid, gatt, g_norm2, *pk_q = mid_bwd(me, cotangent, gup, mid, norms, w_ou, atts, pin(sums))
    sums = step([cd, cu], far(g_norm2), "after_mid")
    *d0, k, s = attn_bwd(0, bucket, me, heads[0], gatt, n1t, pk_q, 2, pin(sums))
    sums = step([cd, cu], far(d0[0]), "after_bwd0")
    pk_q = [k] + (gate([s], sums) if fast else [s])
    cq = chain(pk_q, ("xy", "h1", "h2", "h3"))
    *d1, k, s = attn_bwd(1, bucket, me, heads[1], gatt, n1t, None, 0, pin(sums))
    s0 = step([cd, cu], far(d1[0]), "after_bwd1")
    pk_1 = [k] + (gate([s], s0) if fast else [s])
    if fast:
        cq.join(pk_1)
    sums = step([cq], s0, "after_bwd1_q")
    *d2, k, s = attn_bwd(2, bucket, me, heads[2], gatt, n1t, None, 0, pin(s0 + sums))
    s0 = step([cd, cu, cq], far(d2[0]), "after_bwd2")
    pk_r = [k] + (gate([s], s0) if fast else [s])
    cr = chain(pk_r, direct)
    sums = step([cr], s0, "after_bwd2_r")
    tokens_grad, g_norm1 = tail_bwd(tokens, d0 + d1 + d2, w_full, gmid, norms, pin(s0 + sums))
    sums = step([cu, cq, cr], far(g_norm1), "after_tail")
    g_norms = jnp.concatenate([g_norm1[:2], g_norm2[:2]], axis=0)
    if fast:
        (g_norms,) = gate([g_norms], sums)
        g_norms_c = swap(g_norms, "fsdp", n_fsdp, 1)
    mixed = mixed_out(mid, act, w_dn, pin(sums))
    sums = step([cu, cq, cr], far(mixed), "after_mixed")
    if fast:
        (g_norms,) = gate([g_norms], sums)
        g_norms = sum_chips(g_norms + g_norms_c, n_fsdp)
    sums = step([cq], sums, "last_q")
    if fast:
        (g_norms,) = gate([g_norms], sums)
        g_norms = sum_replicas(g_norms, n_rep)
    step([cr], [], "last_r")

    if fast:
        (rows_d,), (rows_u,), (rows_q,), (rows_r,) = (c.mine for c in (cd, cu, cq, cr))
        gw_out = rows_q[:, :width]
        gw_q = jnp.concatenate([rows_q[:, width:], rows_r], axis=1)
    else:
        g_norms = lax.psum(g_norms, ("fsdp", "rep"))
        rows_q, rows_1, rows_r, rows_u, rows_d = (whole(*pk) for pk in (pk_q, pk_1, pk_r, pk_u, pk_d))
        rows_q = jnp.concatenate([rows_q, rows_1], axis=1)
        gw_out = rows_q[:, :width]
        gw_q = jnp.concatenate([rows_q[:, width:], rows_r], axis=1)
    g_norms = lax.dynamic_slice_in_dim(g_norms, index * (width // n_fsdp), width // n_fsdp, axis=1)
    rows = gw_q.shape[0]
    gw_q = gw_q.reshape(rows, -1, 3, LANES).transpose(0, 2, 1, 3).reshape(rows, -1)
    grads = (gw_q, gw_out, rows_u, rows_d)
    if not fast:
        grads = tuple(
            lax.psum(lax.psum_scatter(g, "fsdp", scatter_dimension=0, tiled=True), "rep") for g in grads
        )
    gw_qkv, gw_out, gw_up, gw_down = (g.astype(f32) for g in grads)
    return (
        mixed,
        tokens_grad,
        g_norms[0],
        g_norms[1],
        gw_qkv,
        gw_out,
        g_norms[2],
        g_norms[3],
        gw_up,
        gw_down,
    )


def solution(mesh):
    return jax.shard_map(
        functools.partial(shards, mesh.shape["fsdp"], mesh.shape["rep"]),
        mesh=mesh,
        in_specs=(
            P(("rep", "fsdp"), None),
            P(("rep", "fsdp")),
            P("fsdp"),
            P("fsdp"),
            P("fsdp", None),
            P("fsdp", None),
            P("fsdp"),
            P("fsdp"),
            P("fsdp", None),
            P("fsdp", None),
            P(("rep", "fsdp"), None),
        ),
        out_specs=(
            P(("rep", "fsdp"), None),
            P(("rep", "fsdp"), None),
            P("fsdp"),
            P("fsdp"),
            P("fsdp", None),
            P("fsdp", None),
            P("fsdp"),
            P("fsdp"),
            P("fsdp", None),
            P("fsdp", None),
        ),
        check_vma=False,
    )
```

```python
import functools

import jax
import jax.numpy as jnp
from jax import lax
from jax.experimental import pallas as pl
from jax.experimental.pallas import tpu as pltpu
from jax.sharding import PartitionSpec as P

HEAD_DIM = 64
SHORT = 256
LN_EPS = 1e-6
LANES = 128
f32 = jnp.float32
bf16 = jnp.bfloat16

LOG2E = 1.4426950408889634
ROOT_2PI = (2 * 3.141592653589793) ** -0.5


def nt(a, b):
    return lax.dot_general(a, b, (((1,), (1,)), ((), ())), preferred_element_type=f32)


def nn(a, b):
    return lax.dot_general(a, b, (((1,), (0,)), ((), ())), preferred_element_type=f32)


def tn(a, b):
    return lax.dot_general(a, b, (((0,), (0,)), ((), ())), preferred_element_type=f32)


def ln_rows(x, gain, bias):
    centred = x - jnp.mean(x, axis=-1, keepdims=True)
    var = jnp.mean(centred * centred, axis=-1, keepdims=True)
    return centred * lax.rsqrt(var + LN_EPS) * gain + bias


def ln_back(grad, v, gain):
    centred = v - jnp.mean(v, axis=-1, keepdims=True)
    r = lax.rsqrt(jnp.mean(centred * centred, axis=-1, keepdims=True) + LN_EPS)
    xh = centred * r
    gg = grad * gain
    dx = r * (gg - jnp.mean(gg, axis=-1, keepdims=True) - xh * jnp.mean(gg * xh, axis=-1, keepdims=True))
    return dx, jnp.sum(grad * xh, axis=0, keepdims=True), jnp.sum(grad, axis=0, keepdims=True)


def gelu_pair(u):
    cdf = 0.5 + 0.5 * lax.erf(u * 2**-0.5)
    density = jnp.exp2((u * u) * (-0.5 * LOG2E))
    return u * cdf, cdf + (u * ROOT_2PI) * density


def terms(v):
    hi = v.astype(bf16).astype(f32)
    r = v - hi
    mid = r.astype(bf16).astype(f32)
    return hi, mid, r - mid


def spread(v, lane):
    hi, mid, lo = terms(-v)
    pos = lane & 63
    return jnp.where(pos == 0, hi, jnp.where(pos == 1, mid, jnp.where(pos == 2, lo, 0.0))).astype(bf16)


def unpack(refs, plan, me, shard_rows, jobs, sem):
    copies = []
    for ref, (r, lo) in zip(refs, plan):
        hi = lo + ref.shape[0]
        for (first, last), cols, dst, step in jobs(shard_rows):
            a, b = max(lo, first), min(hi, last)
            if a >= b:
                continue
            row = pl.multiple_of((me ^ r) * step, 16) + (a - first)
            copies.append(
                pltpu.make_async_copy(
                    ref.at[pl.ds(a - lo, b - a), cols], dst.at[pl.ds(row, b - a), :], sem.at[len(copies)]
                )
            )
    return copies


def run(copies):
    for c in copies:
        c.start()
    for c in copies:
        c.wait()


def put_slots(src_ref, outs, me, cols):
    keep, send = outs
    rows = src_ref.shape[0] // 8
    for r in range(8):
        row = pl.multiple_of((me ^ r) * rows, 16)
        (send if r & 1 else keep)[r >> 1, :, cols] = src_ref[pl.ds(row, rows), :]


def params(mib):
    return pltpu.CompilerParams(vmem_limit_bytes=mib << 20)


def cost(gflops, mib):
    return pl.CostEstimate(flops=1000, bytes_accessed=1024, transcendentals=0)


VMEM_MIB = 44
SMEM = pl.BlockSpec(memory_space=pltpu.SMEM)
VMEM = pl.BlockSpec(memory_space=pltpu.VMEM)
ANY = pl.BlockSpec(memory_space=pl.ANY)
SHAPE = jax.ShapeDtypeStruct


def far(*arrays):
    return [pltpu.with_memory_space_constraint(a, pltpu.HBM) for a in arrays]


def in_hbm(shapes):
    return [pltpu.HBM(s.shape, s.dtype) for s in shapes]


def attend(bucket_ref, qb, n1, wq, wk, wv, qe_ref, k_ref, v_ref, att_ref, vx_ref):
    rows = k_ref.shape[0]
    low = lax.broadcasted_iota(jnp.int32, (rows, 128), 1) < 64
    q = nn(n1, wq)
    k_ref[...] = nn(n1, wk).astype(bf16)
    v = nn(n1, wv)
    v_ref[...] = v.astype(bf16)
    q = q * HEAD_DIM**-0.5
    for p in range(2):
        qp = q[:, 128 * p : 128 * p + 128]
        vp = v[:, 128 * p : 128 * p + 128]
        qe_ref[2 * p] = jnp.where(low, qp, 0.0).astype(bf16)
        qe_ref[2 * p + 1] = jnp.where(low, 0.0, qp).astype(bf16)
        vx_ref[2 * p] = jnp.where(low, vp, 1.0).astype(bf16)
        vx_ref[2 * p + 1] = jnp.where(low, 1.0, vp).astype(bf16)

    def block(r, kr):
        lane = lax.broadcasted_iota(jnp.int32, (r.size, 128), 1)
        lowq = lane < 64
        ss = [nt(qe_ref[h, r, :], k_ref[kr, 128 * (h // 2) : 128 * (h // 2) + 128]) for h in range(4)]
        for p in range(2):
            os, tops = [], []
            for h in (2 * p, 2 * p + 1):
                top = jnp.max(ss[h], axis=-1, keepdims=True)
                e = jnp.exp(ss[h] - top).astype(bf16)
                os.append(nn(e, vx_ref[h, kr, :]))
                tops.append(top)
            sums = jnp.where(lowq, os[1], os[0])
            lse = jnp.where(lowq, tops[1], tops[0]) + jnp.log(sums)
            rest = spread(lse, lane)
            q0, q1 = qe_ref[2 * p, r, :], qe_ref[2 * p + 1, r, :]
            qe_ref[2 * p, r, :] = jnp.where(lowq, q0, rest)
            qe_ref[2 * p + 1, r, :] = jnp.where(lowq, rest, q1)
            att = jnp.where(lowq, os[0], os[1]) / pltpu.roll(sums, 64, 1)
            att_ref[r, 128 * p : 128 * p + 128] = att.astype(bf16)

    is_long = bucket_ref[0] == 1

    @pl.when(is_long)
    def _():
        def body(i, _):
            block(pl.ds(i * qb, qb), slice(None))
            return 0

        lax.fori_loop(0, rows // qb, body, 0)

    @pl.when(jnp.logical_not(is_long))
    def _():
        def body(i, _):
            r = pl.ds(i * SHORT, SHORT)
            block(r, r)
            return 0

        lax.fori_loop(0, rows // SHORT, body, 0)


def q_jobs(w_ref, raw_ref):
    width = w_ref.shape[0]
    return lambda shard: [
        ((0, shard), slice(None), w_ref, shard),
        ((shard, shard + 16), slice(0, width), raw_ref, 16),
    ]


def fwd_first_kernel(plan, shard, n_parts, bucket_ref, me_ref, x_ref, *refs):
    parts = refs[:n_parts]
    n1_ref, n1t_ref, norm_ref, whbm_ref, qe_ref, k_ref, v_ref, att_ref, w_ref, raw_ref, vx_ref, sem = refs[n_parts:]
    rows, width = x_ref.shape
    run(unpack(parts, plan, me_ref[0], shard, q_jobs(w_ref, raw_ref), sem))
    keep = pltpu.make_async_copy(w_ref, whbm_ref, sem.at[0])
    keep.start()
    total = raw_ref[0:16, :].astype(f32)
    for i in range(1, raw_ref.shape[0] // 16):
        total = total + raw_ref[16 * i : 16 * i + 16, :].astype(f32)
    norm_ref[...] = total

    def body(i, _):
        r = pl.ds(i * 128, 128)
        n1_ref[r, :] = ln_rows(x_ref[r, :].astype(f32), norm_ref[0:1, :], norm_ref[1:2, :]).astype(bf16)
        return 0

    lax.fori_loop(0, rows // 128, body, 0)
    n1t_ref[...] = n1_ref[...].T
    w = [w_ref[:, width * i : width * i + 256] for i in range(3)]
    attend(bucket_ref, 256, n1_ref[...], *w, qe_ref, k_ref, v_ref, att_ref, vx_ref)
    keep.wait()


def fwd_next_kernel(n_pins, bucket_ref, n1_ref, wq_ref, wk_ref, wv_ref, *refs):
    attend(bucket_ref, 256, n1_ref[...], wq_ref[...], wk_ref[...], wv_ref[...], *refs[n_pins:])


def head_shapes(rows):
    return [SHAPE((4, rows, 128), bf16)] + [SHAPE((rows, 256), bf16)] * 3


def forward_first(bucket, me, x, parts, plan, shard, pins):
    rows, width = x.shape
    full = lambda *s: pl.BlockSpec(s, lambda i: (0,) * len(s))
    shapes = [
        SHAPE((rows, width), bf16),
        SHAPE((width, rows), bf16),
        SHAPE((16, width), f32),
        SHAPE((width, 3 * width), bf16),
    ] + head_shapes(rows)
    return pl.pallas_call(
        lambda b, m, xr, *refs: fwd_first_kernel(
            plan, shard, len(parts), b, m, xr, *refs[: len(parts)], *refs[len(parts) + len(pins) :]
        ),
        grid=(1,),
        in_specs=[SMEM, SMEM, full(rows, width)] + [ANY] * (len(parts) + len(pins)),
        out_specs=[full(*s.shape) for s in shapes[:3]] + [ANY] + [full(*s.shape) for s in shapes[4:]],
        out_shape=in_hbm(shapes),
        scratch_shapes=[
            pltpu.VMEM((width, 3 * width), bf16),
            pltpu.VMEM((width // shard * 16, width), bf16),
            pltpu.VMEM((4, rows, 128), bf16),
            pltpu.SemaphoreType.DMA((32,)),
        ],
        compiler_params=params(VMEM_MIB),
        cost_estimate=cost(8, 12),
        name="fwd_a",
    )(bucket, me, *far(x, *parts), *pins)


def forward_next(g, bucket, n1, w, pins):
    rows, width = n1.shape
    groups = width // 256
    col = lambda j: pl.BlockSpec((width, 256), lambda i: (0, j * groups + g))
    full = lambda *s: pl.BlockSpec(s, lambda i: (0,) * len(s))
    shapes = head_shapes(rows)
    return pl.pallas_call(
        functools.partial(fwd_next_kernel, len(pins)),
        grid=(1,),
        in_specs=[SMEM, full(rows, width), col(0), col(1), col(2)] + [ANY] * len(pins),
        out_specs=[full(*s.shape) for s in shapes],
        out_shape=in_hbm(shapes),
        scratch_shapes=[pltpu.VMEM((4, rows, 128), bf16)],
        compiler_params=params(VMEM_MIB),
        cost_estimate=cost(8, 8),
        name=f"attn_{g}",
    )(bucket, *far(n1, w, w, w), *pins)


UPN = 512
HIDN = 512


def up_kernel(plan, shard, n_parts, me_ref, x_ref, a0, a1, a2, norm_ref, *refs):
    parts = refs[:n_parts]
    mid_ref, n2t_ref, act_ref, gp_ref, wou_hbm, wo_ref, wu_ref, sem, sem2 = refs[n_parts:]
    width = x_ref.shape[1]
    saves = [
        pltpu.make_async_copy(wo_ref, wou_hbm.at[:, :width], sem2.at[0]),
        pltpu.make_async_copy(wu_ref, wou_hbm.at[:, width:], sem2.at[1]),
    ]

    @pl.when(pl.program_id(0) == 0)
    def _():
        jobs = lambda s: [
            ((0, s), slice(0, width), wo_ref, s),
            ((0, s), slice(width, None), wu_ref, s),
        ]
        run(unpack(parts, plan, me_ref[0], shard, jobs, sem))
        for c in saves:
            c.start()

    att = jnp.concatenate([a0[...], a1[...], a2[...]], axis=1)
    mid = x_ref[...].astype(f32) + nn(att, wo_ref[...])
    mid_ref[...] = mid
    n2 = ln_rows(mid, norm_ref[2:3, :], norm_ref[3:4, :]).astype(bf16)
    n2t_ref[...] = n2.T
    for b in range(wu_ref.shape[1] // UPN):
        c = slice(UPN * b, UPN * b + UPN)
        act, gp = gelu_pair(nn(n2, wu_ref[:, c]))
        act_ref[:, c] = act.astype(bf16)
        gp_ref[:, c] = gp.astype(bf16)

    @pl.when(pl.program_id(0) == pl.num_programs(0) - 1)
    def _():
        for c in saves:
            c.wait()


def up_proj(me, x, atts, norms, parts, plan, shard, pins, rb=256):
    rows, width = x.shape
    hidden = parts[0].shape[1] - width
    row = lambda n: pl.BlockSpec((rb, n), lambda i: (i, 0))
    full = lambda *s: pl.BlockSpec(s, lambda i: (0,) * len(s))
    n = len(parts)
    return pl.pallas_call(
        lambda m, xr, a0, a1, a2, nr, *refs: up_kernel(
            plan, shard, n, m, xr, a0, a1, a2, nr, *refs[:n], *refs[n + len(pins) :]
        ),
        grid=(rows // rb,),
        in_specs=[SMEM, row(width)] + [row(256)] * 3 + [full(16, width)] + [ANY] * (n + len(pins)),
        out_specs=[row(width), pl.BlockSpec((width, rb), lambda i: (0, i)), row(hidden), row(hidden), ANY],
        out_shape=in_hbm([
            SHAPE((rows, width), f32),
            SHAPE((width, rows), bf16),
            SHAPE((rows, hidden), bf16),
            SHAPE((rows, hidden), bf16),
            SHAPE((width, width + hidden), bf16),
        ]),
        scratch_shapes=[
            pltpu.VMEM((width, width), bf16),
            pltpu.VMEM((width, hidden), bf16),
            pltpu.SemaphoreType.DMA((32,)),
            pltpu.SemaphoreType.DMA((2,)),
        ],
        compiler_params=params(VMEM_MIB),
        cost_estimate=cost(9, 20),
        name="up_proj",
    )(me, *far(x, *atts, norms), *parts, *pins)


def shard_of(i):
    return jnp.where(i < 4, 2 * i + 1, 2 * i - 8)


def wdown_kernel(n_pins, me_ref, act_ref, dy_ref, *refs):
    keep_ref, send_ref = refs[n_pins:]
    g = tn(act_ref[...], dy_ref[...]).astype(bf16)
    i = pl.program_id(0)

    @pl.when(i < 4)
    def _():
        send_ref[0] = g

    @pl.when(i >= 4)
    def _():
        keep_ref[0] = g


def wdown_grad(me, act, dy, pins):
    rows, width = dy.shape
    shard = act.shape[1] // 8
    out = SHAPE((4, shard, width), bf16)
    return pl.pallas_call(
        functools.partial(wdown_kernel, len(pins)),
        grid_spec=pltpu.PrefetchScalarGridSpec(
            num_scalar_prefetch=1,
            grid=(8,),
            in_specs=[
                pl.BlockSpec((rows, shard), lambda i, m: (0, m[0] ^ shard_of(i))),
                pl.BlockSpec((rows, width), lambda i, m: (0, 0)),
            ]
            + [ANY] * len(pins),
            out_specs=[
                pl.BlockSpec((1, shard, width), lambda i, m: (jnp.maximum(i - 4, 0), 0, 0)),
                pl.BlockSpec((1, shard, width), lambda i, m: (jnp.minimum(i, 3), 0, 0)),
            ],
        ),
        out_shape=[out, out],
        compiler_params=params(VMEM_MIB),
        cost_estimate=cost(5, 13),
        name="wdown_grad",
    )(me, *far(act, dy), *pins)


def hidden_kernel(plan, shard, n_parts, me_ref, dy_ref, gp_ref, n2t_ref, *refs):
    parts = refs[:n_parts]
    gup_ref, keep_ref, send_ref, wd_hbm, wd_ref, g_ref, sem, sem2 = refs[n_parts:]
    i = pl.program_id(0)
    save = pltpu.make_async_copy(wd_ref, wd_hbm, sem2.at[0])

    @pl.when(i == 0)
    def _():
        run(unpack(parts, plan, me_ref[0], shard, lambda s: [((0, s), slice(None), wd_ref, s)], sem))
        save.start()

    fb = gp_ref.shape[1]
    for b in range(fb // HIDN):
        c = slice(HIDN * b, HIDN * b + HIDN)
        w = wd_ref[pl.ds(pl.multiple_of(i * fb, 256) + HIDN * b, HIDN), :]
        gup_ref[:, c] = (nt(dy_ref[...], w) * gp_ref[:, c].astype(f32)).astype(bf16)
        g_ref[:, c] = nn(n2t_ref[...], gup_ref[:, c]).astype(bf16)
    put_slots(g_ref, (keep_ref, send_ref), me_ref[0], slice(None))

    @pl.when(i == pl.num_programs(0) - 1)
    def _():
        save.wait()


def hidden_bwd(me, dy, gp, n2t, parts, plan, shard, pins, fb=512):
    rows, width = dy.shape
    hidden = gp.shape[1]
    full = lambda *s: pl.BlockSpec(s, lambda i: (0,) * len(s))
    col = pl.BlockSpec((rows, fb), lambda i: (0, i))
    out = SHAPE((4, width // 8, hidden), bf16)
    spec = pl.BlockSpec((4, width // 8, fb), lambda i: (0, 0, i))
    n = len(parts)
    return pl.pallas_call(
        lambda m, a, b, c, *refs: hidden_kernel(plan, shard, n, m, a, b, c, *refs[:n], *refs[n + len(pins) :]),
        grid=(hidden // fb,),
        in_specs=[SMEM, full(rows, width), col, full(width, rows)] + [ANY] * (n + len(pins)),
        out_specs=[col, spec, spec, ANY],
        out_shape=in_hbm([SHAPE((rows, hidden), bf16)]) + [out, out] + in_hbm([SHAPE((hidden, width), bf16)]),
        scratch_shapes=[
            pltpu.VMEM((hidden, width), bf16),
            pltpu.VMEM((width, fb), bf16),
            pltpu.SemaphoreType.DMA((32,)),
            pltpu.SemaphoreType.DMA((1,)),
        ],
        compiler_params=params(VMEM_MIB),
        cost_estimate=cost(10, 26),
        name="hidden_bwd",
    )(me, *far(dy, gp, n2t), *parts, *pins)


def mid_kernel(n_pins, me_ref, dy_ref, gup_ref, mid_ref, norm_ref, wou_ref, a0, a1, a2, *refs):
    gmid_ref, gatt_ref, gg_ref, keep_ref, send_ref, gmb_ref, g_ref = refs[n_pins:]
    rb, width = dy_ref.shape
    i = pl.program_id(0)

    @pl.when(i == 0)
    def _():
        gg_ref[...] = jnp.zeros_like(gg_ref)

    gn2 = nt(gup_ref[...], wou_ref[:, width:])
    dx, dg, db = ln_back(gn2, mid_ref[...], norm_ref[2:3, :])
    gm = dy_ref[...].astype(f32) + dx
    gmid_ref[...] = gm
    gmb = gm.astype(bf16)
    gmb_ref[pl.ds(pl.multiple_of(i * rb, rb), rb), :] = gmb
    gg_ref[0:1, :] += dg
    gg_ref[1:2, :] += db
    gatt_ref[...] = nt(gmb, wou_ref[:, :width]).astype(bf16)

    @pl.when(i == pl.num_programs(0) - 1)
    def _():
        for j, a in enumerate((a0, a1, a2)):
            g_ref[256 * j : 256 * j + 256, :] = tn(a[...], gmb_ref[...]).astype(bf16)
        put_slots(g_ref, (keep_ref, send_ref), me_ref[0], slice(None))


def mid_bwd(me, dy, gup, mid, norms, wou, atts, pins, rb=256):
    rows, width = dy.shape
    hidden = gup.shape[1]
    row = lambda n: pl.BlockSpec((rb, n), lambda i: (i, 0))
    full = lambda *s: pl.BlockSpec(s, lambda i: (0,) * len(s))
    once = lambda *s: pl.BlockSpec(s, lambda i: (0,) * len(s), pipeline_mode=pl.Buffered(1))
    out = SHAPE((4, width // 8, 2 * width), bf16)
    spec = pl.BlockSpec((4, width // 8, width), lambda i: (0, 0, 0))
    return pl.pallas_call(
        functools.partial(mid_kernel, len(pins)),
        grid=(rows // rb,),
        in_specs=[SMEM, row(width), row(hidden), row(width), full(16, width), VMEM]
        + [full(rows, 256)] * 3
        + [ANY] * len(pins),
        out_specs=[row(width), row(width), full(8, width), spec, spec],
        out_shape=in_hbm([SHAPE((rows, width), f32), SHAPE((rows, width), bf16), SHAPE((8, width), f32)]) + [out, out],
        scratch_shapes=[pltpu.VMEM((rows, width), bf16), pltpu.VMEM((width, width), bf16)],
        compiler_params=params(VMEM_MIB),
        cost_estimate=cost(8, 24),
        name="mid_bwd",
    )(me, *far(dy, gup, mid, norms), wou, *far(*atts), *pins)


def bwd_kernel(kb, n_pins, bucket_ref, me_ref, qe_ref, k_ref, v_ref, att_ref, do_ref, n1t_hbm, *refs):
    dq_ref, dk_ref, dv_ref, keep_ref, send_ref, doe_ref, ke_ref, ve_ref, dqa_ref, g_ref, n1t_ref, sem = refs[n_pins:]
    rows = k_ref.shape[0]
    load = pltpu.make_async_copy(n1t_hbm, n1t_ref, sem.at[0])

    @pl.when(pl.program_id(0) == 0)
    def _():
        load.start()

    lane = lax.broadcasted_iota(jnp.int32, (rows, 128), 1)
    low = lane < 64
    do, k, v = do_ref[...], k_ref[...], v_ref[...]
    across = lambda i: lax.broadcasted_iota(jnp.int32, (128, 128), i) // 64
    other = jnp.where(across(0) + across(1) == 1, 1.0, 0.0).astype(bf16)
    d = sum(nn(t.astype(bf16), other) for t in terms(do.astype(f32) * att_ref[...].astype(f32)))
    rest = spread(d, lane)
    ones = jnp.where((lane & 63) < 3, 1.0, 0.0).astype(bf16)
    for j in range(2):
        own = low if j == 0 else ~low
        doe_ref[j] = jnp.where(own, do, rest)
        ke_ref[j] = jnp.where(own, k, ones)
        ve_ref[j] = jnp.where(own, v, ones)

    def block(kr, qr):
        lowk = lax.broadcasted_iota(jnp.int32, (kr.size, 128), 1) < 64
        dks, dvs, dqs = [], [], []
        sts = [nt(ke_ref[j, kr, :], qe_ref[j, qr, :]) for j in range(2)]
        dpts = [nt(ve_ref[j, kr, :], doe_ref[j, qr, :]) for j in range(2)]
        for j in range(2):
            pt = jnp.exp(sts[j])
            ds = (pt * dpts[j]).astype(bf16)
            dvs.append(nn(pt.astype(bf16), do_ref[qr, :]))
            dks.append(nn(ds, qe_ref[j, qr, :]))
            dqs.append(tn(k_ref[kr, :], ds).T)
        dk_ref[kr, :] = jnp.where(lowk, dks[0], dks[1]).astype(bf16)
        dv_ref[kr, :] = jnp.where(lowk, dvs[0], dvs[1]).astype(bf16)
        return dqs

    is_long = bucket_ref[0] == 1

    @pl.when(is_long)
    def _():
        if kb == rows:
            dqs = block(pl.ds(0, rows), slice(None))
            dq_ref[...] = (jnp.where(low, dqs[0], dqs[1]) * HEAD_DIM**-0.5).astype(bf16)
            return
        dqa_ref[...] = jnp.zeros_like(dqa_ref)

        def body(i, _):
            dqs = block(pl.ds(i * kb, kb), slice(None))
            dqa_ref[...] += jnp.where(low, dqs[0], dqs[1])
            return 0

        lax.fori_loop(0, rows // kb, body, 0)
        dq_ref[...] = (dqa_ref[...] * HEAD_DIM**-0.5).astype(bf16)

    @pl.when(jnp.logical_not(is_long))
    def _():
        lows = lax.broadcasted_iota(jnp.int32, (SHORT, 128), 1) < 64

        def body(i, _):
            r = pl.ds(i * SHORT, SHORT)
            dqs = block(r, r)
            dq_ref[r, :] = (jnp.where(lows, dqs[0], dqs[1]) * HEAD_DIM**-0.5).astype(bf16)
            return 0

        lax.fori_loop(0, rows // SHORT, body, 0)

    @pl.when(pl.program_id(0) == 0)
    def _():
        load.wait()

    g_ref[...] = nn(n1t_ref[...], jnp.concatenate([dq_ref[...], dk_ref[...], dv_ref[...]], axis=1)).astype(bf16)
    put_slots(g_ref, (keep_ref, send_ref), me_ref[0], slice(None))


def attn_bwd(g, bucket, me, heads, gatt, n1t, into, first, pins):
    qe, k, v, att = heads
    rows = k.shape[0]
    width = n1t.shape[0]
    col = pl.BlockSpec((rows, 128), lambda i: (0, i))
    out = SHAPE(into[0].shape if into else (4, width // 8, 768), bf16)
    spec = pl.BlockSpec((4, width // 8, 384), lambda i: (0, 0, first + i))
    into = list(into or [])
    return pl.pallas_call(
        functools.partial(bwd_kernel, 512, len(into) + len(pins)),
        grid=(2,),
        in_specs=[
            SMEM,
            SMEM,
            pl.BlockSpec((2, rows, 128), lambda i: (i, 0, 0)),
            col,
            col,
            col,
            pl.BlockSpec((rows, 128), lambda i: (0, 2 * g + i)),
        ]
        + [ANY] * (1 + len(into) + len(pins)),
        input_output_aliases={8 + i: 3 + i for i in range(len(into))},
        out_specs=[col] * 3 + [spec] * 2,
        out_shape=in_hbm([SHAPE((rows, 256), bf16)] * 3) + [out, out],
        scratch_shapes=[pltpu.VMEM((2, rows, 128), bf16)] * 3
        + [
            pltpu.VMEM((rows, 128), f32),
            pltpu.VMEM((width, 384), bf16),
            pltpu.VMEM((width, rows), bf16),
            pltpu.SemaphoreType.DMA((1,)),
        ],
        compiler_params=params(VMEM_MIB),
        cost_estimate=cost(14, 8),
        name=f"attn_bwd_{g}",
    )(bucket, me, *far(qe, k, v, att, gatt, n1t), *into, *pins)


def tail_kernel(n_pins, x_ref, *refs):
    ds = refs[:9]
    w_ref, gmid_ref, norm_ref = refs[9:12]
    tg_ref, gg_ref = refs[12 + n_pins :]

    @pl.when(pl.program_id(0) == 0)
    def _():
        gg_ref[...] = jnp.zeros_like(gg_ref)

    d = jnp.concatenate([ds[3 * g + j][...] for j in range(3) for g in range(3)], axis=1)
    dx, dg, db = ln_back(nt(d, w_ref[...]), x_ref[...].astype(f32), norm_ref[0:1, :])
    tg_ref[...] = (gmid_ref[...] + dx).astype(bf16)
    gg_ref[0:1, :] += dg
    gg_ref[1:2, :] += db


def tail_bwd(x, ds, w, gmid, norms, pins, rb=256):
    rows, width = x.shape
    row = lambda n: pl.BlockSpec((rb, n), lambda i: (i, 0))
    full = lambda *s: pl.BlockSpec(s, lambda i: (0,) * len(s))
    once = lambda *s: pl.BlockSpec(s, lambda i: (0,) * len(s), pipeline_mode=pl.Buffered(1))
    return pl.pallas_call(
        functools.partial(tail_kernel, len(pins)),
        grid=(rows // rb,),
        in_specs=[row(width)] + [row(256)] * 9 + [VMEM, row(width), full(16, width)] + [ANY] * len(pins),
        out_specs=[row(width), full(8, width)],
        out_shape=in_hbm([SHAPE((rows, width), bf16), SHAPE((8, width), f32)]),
        compiler_params=params(VMEM_MIB),
        cost_estimate=cost(5, 16),
        name="tail_bwd",
    )(*far(x, *ds), w, *far(gmid, norms), *pins)


def mixed_kernel(n_pins, mid_ref, act_ref, wd_ref, *refs):
    refs[n_pins][...] = (mid_ref[...] + nn(act_ref[...], wd_ref[...])).astype(bf16)


def mixed_out(mid, act, wd, pins, rb=256):
    rows, width = mid.shape
    hidden = act.shape[1]
    row = lambda n: pl.BlockSpec((rb, n), lambda i: (i, 0))
    once = pl.BlockSpec((hidden, width), lambda i: (0, 0), pipeline_mode=pl.Buffered(1))
    return pl.pallas_call(
        functools.partial(mixed_kernel, len(pins)),
        grid=(rows // rb,),
        in_specs=[row(width), row(hidden), VMEM] + [ANY] * len(pins),
        out_specs=row(width),
        out_shape=in_hbm([SHAPE((rows, width), bf16)])[0],
        compiler_params=params(VMEM_MIB),
        cost_estimate=cost(5, 16),
        name="mixed_out",
    )(*far(mid, act), wd, *pins)


def packet_kernel(n_in, *refs):
    ins, out_ref = refs[:n_in], refs[-1]
    col = 0
    for v in ins:
        out_ref[:, col : col + v.shape[1]] = v[...]
        col += v.shape[1]


def packet(arrays, pins, name):
    rows, cols = arrays[0].shape[0], sum(a.shape[1] for a in arrays)
    full = lambda *s: pl.BlockSpec(s, lambda i: (0,) * len(s))
    return pl.pallas_call(
        functools.partial(packet_kernel, len(arrays)),
        grid=(1,),
        in_specs=[full(*a.shape) for a in arrays] + [ANY] * len(pins),
        out_specs=full(rows, cols),
        out_shape=SHAPE((rows, cols), bf16),
        compiler_params=params(8),
        cost_estimate=cost(0, 2),
        name=name,
    )(*arrays, *pins)


def gate(arrays, pins):
    n = len(arrays)
    if not pins:
        return list(arrays)
    return list(pl.pallas_call(
        lambda *refs: None,
        in_specs=[ANY] * (n + len(pins)),
        out_specs=[ANY] * n,
        out_shape=[SHAPE(a.shape, a.dtype) for a in arrays],
        input_output_aliases={i: i for i in range(n)},
        compiler_params=params(1),
        cost_estimate=cost(0, 0),
        name="gate",
    )(*arrays, *pins))


def total(*vs):
    out = vs[0].astype(f32)
    for v in vs[1:]:
        out = out + v.astype(f32)
    return out.astype(bf16)


def combine_kernel(plan, n_in, n_pins, odd_ref, *refs):
    outs = refs[n_in + n_pins :]
    odd = odd_ref[0] == 1
    at = 0
    for f, spots, n_out in plan:
        values = f(odd, *[refs[i] for i in spots])
        for v in values:
            outs[at][...] = v.astype(outs[at].dtype)
            at += 1


def combine(jobs, odd, pins, name, grid=1):
    arrays, shapes, plan = [], [], []
    for f, ins, outs in jobs:
        spots = []
        for a in ins:
            known = [i for i, b in enumerate(arrays) if b is a]
            spots.append(known[0] if known else len(arrays))
            if not known:
                arrays.append(a)
        plan.append((f, spots, len(outs)))
        shapes += [o if isinstance(o, SHAPE) else SHAPE(o, bf16) for o in outs]
    block = lambda s: pl.BlockSpec(s[:-1] + (s[-1] // grid,), lambda i: (0,) * (len(s) - 1) + (i,))
    sums = pl.pallas_call(
        functools.partial(combine_kernel, plan, len(arrays), len(pins)),
        grid=(grid,),
        in_specs=[SMEM] + [block(a.shape) for a in arrays] + [ANY] * len(pins),
        out_specs=[block(s.shape) for s in shapes],
        out_shape=shapes,
        compiler_params=params(24),
        cost_estimate=cost(0, 4),
        name=name,
    )(odd, *arrays, *pins)
    return list(sums)


def swap(v, axis, size, m):
    return lax.ppermute(v, axis, [(i, i ^ m) for i in range(size)])


def part_plan(cut):
    return [(0, 0), (1, 0), (2, 0), (4, 0), (6, 0), (6, cut), (3, 0), (5, 0), (7, 0), (7, cut)]


class Gather:
    def __init__(self, own, cut, size):
        self.own, self.cut, self.size = own, cut, size

    def near(self):
        self.rx, self.ry = (swap(self.own, "fsdp", self.size, m) for m in (2, 4))
        return [self.rx, self.ry]

    def halves(self):
        n, cols = self.own.shape
        return (
            lambda odd, x, y: (y[: self.cut, :], x[self.cut :, :]),
            [self.rx, self.ry],
            [(self.cut, cols), (n - self.cut, cols)],
        )

    def opposite(self, to_x, to_y):
        self.da, self.db = swap(to_x, "fsdp", self.size, 2), swap(to_y, "fsdp", self.size, 4)
        return [self.da, self.db]

    def core_near(self):
        self.rc, *self.near_c = [swap(v, "fsdp", self.size, 1) for v in (self.own, self.rx, self.ry)]

    def parts(self):
        opp = [self.da, self.db]
        return [self.own, self.rc, self.rx, self.ry] + opp + self.near_c + [swap(v, "fsdp", self.size, 1) for v in opp]


class Chain:
    def __init__(self, packets, plan, n_fsdp, n_rep):
        self.mine, self.got = [], []
        self.plan = ("core",) + plan
        self.at = 0
        self.f = lambda v, m: swap(v, "fsdp", n_fsdp, m)
        self.z = lambda v, m: swap(v, "rep", n_rep, m)
        self.join(packets)

    def join(self, packets):
        keep, send = packets
        self.mine.append(keep)
        self.got.append(self.f(send, 1))
        self.shape = (keep.shape[1], sum(k.shape[2] for k in self.mine))

    def job(self):
        done = self.plan[self.at]
        then = self.plan[self.at + 1] if self.at + 1 < len(self.plan) else None
        rows, cols = self.shape
        h = rows // 2
        whole, half = (rows, cols), (h, cols)
        if done == "core" and then == "xy":

            def f(odd, *vs):
                n = len(vs) // 2
                pairs = list(zip(vs[:n], vs[n:]))
                return tuple(jnp.concatenate([total(k[s], g[s]) for k, g in pairs], axis=1) for s in range(4))

            return f, self.mine + self.got, [whole] * 4
        if done == "core":

            def f(odd, k, g):
                part = lambda s, t, lo: jnp.stack([total(k[i, lo : lo + h, :], g[i, lo : lo + h, :]) for i in (s, t)])
                return part(0, 2, 0), part(0, 1, h), part(1, 3, 0), part(2, 3, h)

            return f, self.mine + self.got, [(2,) + half] * 4
        if done == "a":
            f = lambda odd, a, b, ra, rb: (total(a[0], ra[0]), total(b[0], rb[0]), total(a[1], ra[1]), total(b[1], rb[1]))
            return f, self.mine + self.got, [half] * 4
        if done in ("b", "xy"):

            def f(odd, *vs):
                if done == "b":
                    a, b, ra, rb = vs
                    lo, hi = total(a[...], ra[...]), total(b[...], rb[...])
                else:
                    lo, hi = (total(*[v[r, :] for v in vs]) for r in (slice(0, h), slice(h, rows)))
                if then == "p1":
                    return (jnp.concatenate([lo, hi], axis=0),)
                return jnp.where(odd, hi, lo), jnp.where(odd, lo, hi)

            return f, self.mine + self.got, [whole] if then == "p1" else [half] * 2
        if done == "h3":

            def f(odd, p, o):
                p, o = p[...], o[...]
                return (jnp.concatenate([jnp.where(odd, o, p), jnp.where(odd, p, o)], axis=0),)

            return f, self.mine + self.got, [SHAPE(whole, f32)]
        out = half if done[0] == "h" else whole
        return (lambda odd, a, b: (total(a[...], b[...]),)), self.mine + self.got, [out if then else SHAPE(out, f32)]

    def go(self, sums):
        self.at += 1
        step = self.plan[self.at] if self.at < len(self.plan) else None
        if step == "xy":
            self.mine, out = sums[:1], sums[1:]
            self.got = [self.f(v, m) for v, m in zip(out, (2, 4, 6))]
        elif step in ("a", "b"):
            self.mine, out = sums[:2], sums[2:]
            self.got = [self.f(v, m) for v, m in zip(out, (2, 4) if step == "a" else (4, 2))]
        elif step == "h1":
            self.mine, self.got = sums[:1], [self.z(sums[1], 1)]
        else:
            self.mine = sums
            self.got = [self.z(sums[0], 2 if step in ("h2", "p2") else 1)] if step else []


def advance(chains, extra, odd, pins, name, grid=1):
    jobs = [c.job() for c in chains] + extra
    sums = combine(jobs, odd, pins, name, grid)
    at = 0
    for c, job in zip(chains, jobs):
        c.go(sums[at : at + len(job[2])])
        at += len(job[2])
    return sums, sums[at:]


def natural(v, width):
    pairs = width // LANES
    return jnp.concatenate([v[:, LANES * (3 * p + j) :][:, :LANES] for j in range(3) for p in range(pairs)], axis=1)


def last_job(cq, cr):
    rows, cols = cq.shape
    width = cr.shape[1]

    def f(odd, p, o, a, b):
        p, o = p[...], o[...]
        q = jnp.concatenate([jnp.where(odd, o, p), jnp.where(odd, p, o)], axis=0)
        return q[:, :width], natural(jnp.concatenate([q[:, width:], total(a[...], b[...])], axis=1), width)

    return f, cq.mine + cq.got + cr.mine + cr.got, [SHAPE((rows, width), f32), SHAPE((rows, cols), f32)]


def sum_chips(v, size):
    x, y, d = (swap(v, "fsdp", size, m) for m in (2, 4, 6))
    return (v + x) + (y + d)


def sum_replicas(v, size):
    a, b, c = (swap(v, "rep", size, m) for m in (1, 2, 3))
    return (v + a) + (b + c)


def whole(keep, send):
    return jnp.stack([keep, send], axis=1).reshape(-1, keep.shape[2])


def shards(
    n_fsdp, n_rep, tokens, bucket, ln1_gain, ln1_bias, w_qkv, w_out, ln2_gain, ln2_bias, w_up, w_down, cotangent
):
    width = tokens.shape[1]
    fast = n_fsdp == 8 and n_rep == 4
    index = lax.axis_index("fsdp")
    vectors = jnp.stack([ln1_gain, ln1_bias, ln2_gain, ln2_bias])
    if fast:
        me = jnp.reshape(index, (1,)).astype(jnp.int32)
        owner = lax.broadcasted_iota(jnp.int32, (4, width), 1) // (width // 8)
        spread = jnp.where(owner == index, jnp.tile(vectors, (1, 8)), 0)
    else:
        me = jnp.zeros((1,), jnp.int32)
        spread = lax.all_gather(vectors, "fsdp", axis=1, tiled=True)
        w_qkv, w_out, w_up, w_down = (
            lax.all_gather(w, "fsdp", axis=0, tiled=True) for w in (w_qkv, w_out, w_up, w_down)
        )
    local = w_qkv.shape[0]
    norm_rows = jnp.pad(spread, ((0, 12), (0, w_qkv.shape[1] - width)))
    packet_q = jnp.concatenate([w_qkv, norm_rows], axis=0)
    cut, cut_d = local // 2, w_down.shape[0] // 2
    none = [(0, 0)]
    odd = jnp.reshape(lax.axis_index("rep") & 1, (1,)).astype(jnp.int32)

    if fast:
        gq = Gather(packet_q, cut, n_fsdp)
        gq.near()
        far_q = gq.opposite(gq.ry[:cut], gq.rx[cut:])
        gq.core_near()
        (own_u,) = gate([packet([w_out, w_up], [], "packet_up")], far_q + [gq.rc] + gq.near_c)
        gu = Gather(own_u, cut, n_fsdp)
        near_u = gu.near()
        gd = Gather(None, cut_d, n_fsdp)
        plan, plan_d = part_plan(cut), part_plan(cut_d)
        parts_q = gq.parts()
    else:
        plan, plan_d = none, none
        parts_q = [packet_q]

    def pin(v):
        return list(v) if fast else []

    n1, n1t, norms, w_full, *heads0 = forward_first(
        bucket, me, tokens, parts_q, plan, local, pin([own_u] if fast else [])
    )
    sums = []
    if fast:
        sums, (to_x, to_y, own_d) = advance(
            [], [gu.halves(), (lambda o, w: (w[...],), [w_down], [w_down.shape])], odd, far(n1t), "after_a"
        )
        gu.opposite(to_x, to_y)
        gu.rx, gu.ry = gate([gu.rx, gu.ry], far(n1t))
        (gu.own,) = gate([gu.own], far(n1t))
        gu.core_near()
    heads1 = forward_next(1, bucket, n1, w_full, pin(sums))
    sums = []
    if fast:
        gu.da, gu.db, gd.own, gu.rc, *gu.near_c = gate([gu.da, gu.db, own_d, gu.rc] + gu.near_c, far(heads1[3]))
        sums = [gd.own]
        gd.near()
        parts_u = gu.parts()
    heads2 = forward_next(2, bucket, n1, w_full, pin(sums))
    heads = [heads0, heads1, heads2]
    atts = [h[3] for h in heads]
    if fast:
        sums, (to_x, to_y) = advance([], [gd.halves()], odd, far(heads2[3]), "after_c")
        gd.opposite(to_x, to_y)
        gd.core_near()
    else:
        parts_u = [packet([w_out, w_up], [], "packet_up")]
    mid, n2t, act, gp, w_ou = up_proj(me, tokens, atts, norms, parts_u, plan, local, pin(sums))
    if fast:
        gd.da, gd.db = gate([gd.da, gd.db], far(n2t))
        parts_d = gd.parts()
    else:
        parts_d = [w_down]
    pk_d = wdown_grad(me, act, cotangent, pin([gd.da, gd.db] if fast else []))
    halves, direct = ("a", "b", "h1", "h2", "h3"), ("xy", "p1", "p2")
    chain = lambda pk, plan: Chain(pk, plan, n_fsdp, n_rep) if fast else None

    def step(chains, after, name):
        return advance(chains, [], odd, after, name)[0][-1:] if fast else []

    if fast:
        pk_d = [pk_d[0]] + gate([pk_d[1]], parts_d)
    cd = chain(pk_d, halves)
    sums = step([cd], [], "after_wdown")
    gup, *pk_u, w_dn = hidden_bwd(me, cotangent, gp, n2t, parts_d, plan_d, w_down.shape[0], pin(sums))
    sums = step([cd], far(gup), "after_hidden")
    if fast:
        pk_u = [pk_u[0]] + gate([pk_u[1]], sums)
    cu = chain(pk_u, halves)
    gmid, gatt, g_norm2, *pk_q = mid_bwd(me, cotangent, gup, mid, norms, w_ou, atts, pin(sums))
    sums = step([cd, cu], far(g_norm2), "after_mid")
    *d0, k, s = attn_bwd(0, bucket, me, heads[0], gatt, n1t, pk_q, 2, pin(sums))
    sums = step([cd, cu], far(d0[0]), "after_bwd0")
    pk_q = [k] + (gate([s], sums) if fast else [s])
    cq = chain(pk_q, ("xy", "h1", "h2", "h3"))
    *d1, k, s = attn_bwd(1, bucket, me, heads[1], gatt, n1t, None, 0, pin(sums))
    s0 = step([cd, cu], far(d1[0]), "after_bwd1")
    pk_1 = [k] + (gate([s], s0) if fast else [s])
    if fast:
        cq.join(pk_1)
    sums = step([cq], s0, "after_bwd1_q")
    *d2, k, s = attn_bwd(2, bucket, me, heads[2], gatt, n1t, None, 0, pin(s0 + sums))
    s0 = step([cd, cu, cq], far(d2[0]), "after_bwd2")
    pk_r = [k] + (gate([s], s0) if fast else [s])
    cr = chain(pk_r, direct)
    sums = step([cr], s0, "after_bwd2_r")
    tokens_grad, g_norm1 = tail_bwd(tokens, d0 + d1 + d2, w_full, gmid, norms, pin(s0 + sums))
    sums = step([cu, cq, cr], far(g_norm1), "after_tail")
    g_norms = jnp.concatenate([g_norm1[:2], g_norm2[:2]], axis=0)
    if fast:
        (g_norms,) = gate([g_norms], sums)
        g_norms_c = swap(g_norms, "fsdp", n_fsdp, 1)
    mixed = mixed_out(mid, act, w_dn, pin(sums))
    sums = step([cu, cq, cr], far(mixed), "after_mixed")
    if fast:
        (g_norms,) = gate([g_norms], sums)
        g_norms = sum_chips(g_norms + g_norms_c, n_fsdp)
    if fast:
        (g_norms,) = gate([g_norms], cq.got)
        g_norms = sum_replicas(g_norms, n_rep)
    if fast:
        gw_out, gw_q = combine([last_job(cq, cr)], odd, [], "last")

    if fast:
        (rows_d,), (rows_u,) = (c.mine for c in (cd, cu))
    else:
        g_norms = lax.psum(g_norms, ("fsdp", "rep"))
        rows_q, rows_1, rows_r, rows_u, rows_d = (whole(*pk) for pk in (pk_q, pk_1, pk_r, pk_u, pk_d))
        rows_q = jnp.concatenate([rows_q, rows_1], axis=1)
        gw_out = rows_q[:, :width]
        gw_q = natural(jnp.concatenate([rows_q[:, width:], rows_r], axis=1), width)
    g_norms = lax.dynamic_slice_in_dim(g_norms, index * (width // n_fsdp), width // n_fsdp, axis=1)
    grads = (gw_q, gw_out, rows_u, rows_d)
    if not fast:
        grads = tuple(
            lax.psum(lax.psum_scatter(g, "fsdp", scatter_dimension=0, tiled=True), "rep") for g in grads
        )
    gw_qkv, gw_out, gw_up, gw_down = (g.astype(f32) for g in grads)
    return (
        mixed,
        tokens_grad,
        g_norms[0],
        g_norms[1],
        gw_qkv,
        gw_out,
        g_norms[2],
        g_norms[3],
        gw_up,
        gw_down,
    )


def solution(mesh):
    return jax.shard_map(
        functools.partial(shards, mesh.shape["fsdp"], mesh.shape["rep"]),
        mesh=mesh,
        in_specs=(
            P(("rep", "fsdp"), None),
            P(("rep", "fsdp")),
            P("fsdp"),
            P("fsdp"),
            P("fsdp", None),
            P("fsdp", None),
            P("fsdp"),
            P("fsdp"),
            P("fsdp", None),
            P("fsdp", None),
            P(("rep", "fsdp"), None),
        ),
        out_specs=(
            P(("rep", "fsdp"), None),
            P(("rep", "fsdp"), None),
            P("fsdp"),
            P("fsdp"),
            P("fsdp", None),
            P("fsdp", None),
            P("fsdp"),
            P("fsdp"),
            P("fsdp", None),
            P("fsdp", None),
        ),
        check_vma=False,
    )
```

```python
import functools

import jax
import jax.numpy as jnp
from jax import lax
from jax.experimental import pallas as pl
from jax.experimental.pallas import tpu as pltpu
from jax.sharding import PartitionSpec as P

HEAD_DIM = 64
SHORT = 256
LN_EPS = 1e-6
LANES = 128
f32 = jnp.float32
bf16 = jnp.bfloat16

LOG2E = 1.4426950408889634
ROOT_2PI = (2 * 3.141592653589793) ** -0.5


def nt(a, b):
    return lax.dot_general(a, b, (((1,), (1,)), ((), ())), preferred_element_type=f32)


def nn(a, b):
    return lax.dot_general(a, b, (((1,), (0,)), ((), ())), preferred_element_type=f32)


def tn(a, b):
    return lax.dot_general(a, b, (((0,), (0,)), ((), ())), preferred_element_type=f32)


def ln_rows(x, gain, bias):
    centred = x - jnp.mean(x, axis=-1, keepdims=True)
    var = jnp.mean(centred * centred, axis=-1, keepdims=True)
    return centred * lax.rsqrt(var + LN_EPS) * gain + bias


def ln_back(grad, v, gain):
    centred = v - jnp.mean(v, axis=-1, keepdims=True)
    r = lax.rsqrt(jnp.mean(centred * centred, axis=-1, keepdims=True) + LN_EPS)
    xh = centred * r
    gg = grad * gain
    dx = r * (gg - jnp.mean(gg, axis=-1, keepdims=True) - xh * jnp.mean(gg * xh, axis=-1, keepdims=True))
    return dx, jnp.sum(grad * xh, axis=0, keepdims=True), jnp.sum(grad, axis=0, keepdims=True)


def gelu_pair(u):
    cdf = 0.5 + 0.5 * lax.erf(u * 2**-0.5)
    density = jnp.exp2((u * u) * (-0.5 * LOG2E))
    return u * cdf, cdf + (u * ROOT_2PI) * density


def terms(v):
    hi = v.astype(bf16).astype(f32)
    r = v - hi
    mid = r.astype(bf16).astype(f32)
    return hi, mid, r - mid


def spread(v, lane):
    hi, mid, lo = terms(-v)
    pos = lane & 63
    return jnp.where(pos == 0, hi, jnp.where(pos == 1, mid, jnp.where(pos == 2, lo, 0.0))).astype(bf16)


def unpack(refs, plan, me, shard_rows, jobs, sem):
    copies = []
    for ref, (r, lo) in zip(refs, plan):
        hi = lo + ref.shape[0]
        for (first, last), cols, dst, step in jobs(shard_rows):
            a, b = max(lo, first), min(hi, last)
            if a >= b:
                continue
            row = pl.multiple_of((me ^ r) * step, 16) + (a - first)
            copies.append(
                pltpu.make_async_copy(
                    ref.at[pl.ds(a - lo, b - a), cols], dst.at[pl.ds(row, b - a), :], sem.at[len(copies)]
                )
            )
    return copies


def run(copies):
    for c in copies:
        c.start()
    for c in copies:
        c.wait()


def put_slots(src_ref, outs, me, cols):
    keep, send = outs
    rows = src_ref.shape[0] // 8
    for r in range(8):
        row = pl.multiple_of((me ^ r) * rows, 16)
        (send if r & 1 else keep)[r >> 1, :, cols] = src_ref[pl.ds(row, rows), :]


def params(mib):
    return pltpu.CompilerParams(vmem_limit_bytes=mib << 20)


def cost(gflops, mib):
    return pl.CostEstimate(flops=1000, bytes_accessed=1024, transcendentals=0)


VMEM_MIB = 44
SMEM = pl.BlockSpec(memory_space=pltpu.SMEM)
VMEM = pl.BlockSpec(memory_space=pltpu.VMEM)
ANY = pl.BlockSpec(memory_space=pl.ANY)
SHAPE = jax.ShapeDtypeStruct


def far(*arrays):
    return [pltpu.with_memory_space_constraint(a, pltpu.HBM) for a in arrays]


def in_hbm(shapes):
    return [pltpu.HBM(s.shape, s.dtype) for s in shapes]


def attend(bucket_ref, qb, n1, wq, wk, wv, qe_ref, k_ref, v_ref, att_ref, vx_ref):
    rows = k_ref.shape[0]
    low = lax.broadcasted_iota(jnp.int32, (rows, 128), 1) < 64
    q = nn(n1, wq)
    k_ref[...] = nn(n1, wk).astype(bf16)
    v = nn(n1, wv)
    v_ref[...] = v.astype(bf16)
    q = q * HEAD_DIM**-0.5
    for p in range(2):
        qp = q[:, 128 * p : 128 * p + 128]
        vp = v[:, 128 * p : 128 * p + 128]
        qe_ref[2 * p] = jnp.where(low, qp, 0.0).astype(bf16)
        qe_ref[2 * p + 1] = jnp.where(low, 0.0, qp).astype(bf16)
        vx_ref[2 * p] = jnp.where(low, vp, 1.0).astype(bf16)
        vx_ref[2 * p + 1] = jnp.where(low, 1.0, vp).astype(bf16)

    def block(r, kr):
        lane = lax.broadcasted_iota(jnp.int32, (r.size, 128), 1)
        lowq = lane < 64
        ss = [nt(qe_ref[h, r, :], k_ref[kr, 128 * (h // 2) : 128 * (h // 2) + 128]) for h in range(4)]
        for p in range(2):
            os, tops = [], []
            for h in (2 * p, 2 * p + 1):
                top = jnp.max(ss[h], axis=-1, keepdims=True)
                e = jnp.exp(ss[h] - top).astype(bf16)
                os.append(nn(e, vx_ref[h, kr, :]))
                tops.append(top)
            sums = jnp.where(lowq, os[1], os[0])
            lse = jnp.where(lowq, tops[1], tops[0]) + jnp.log(sums)
            rest = spread(lse, lane)
            q0, q1 = qe_ref[2 * p, r, :], qe_ref[2 * p + 1, r, :]
            qe_ref[2 * p, r, :] = jnp.where(lowq, q0, rest)
            qe_ref[2 * p + 1, r, :] = jnp.where(lowq, rest, q1)
            att = jnp.where(lowq, os[0], os[1]) / pltpu.roll(sums, 64, 1)
            att_ref[r, 128 * p : 128 * p + 128] = att.astype(bf16)

    is_long = bucket_ref[0] == 1

    @pl.when(is_long)
    def _():
        def body(i, _):
            block(pl.ds(i * qb, qb), slice(None))
            return 0

        lax.fori_loop(0, rows // qb, body, 0)

    @pl.when(jnp.logical_not(is_long))
    def _():
        def body(i, _):
            r = pl.ds(i * SHORT, SHORT)
            block(r, r)
            return 0

        lax.fori_loop(0, rows // SHORT, body, 0)


def q_jobs(w_ref, raw_ref):
    width = w_ref.shape[0]
    return lambda shard: [
        ((0, shard), slice(None), w_ref, shard),
        ((shard, shard + 16), slice(0, width), raw_ref, 16),
    ]


def fwd_first_kernel(plan, shard, n_parts, bucket_ref, me_ref, x_ref, *refs):
    parts = refs[:n_parts]
    n1_ref, n1t_ref, norm_ref, whbm_ref, qe_ref, k_ref, v_ref, att_ref, w_ref, raw_ref, vx_ref, sem = refs[n_parts:]
    rows, width = x_ref.shape
    run(unpack(parts, plan, me_ref[0], shard, q_jobs(w_ref, raw_ref), sem))
    keep = pltpu.make_async_copy(w_ref, whbm_ref, sem.at[0])
    keep.start()
    total = raw_ref[0:16, :].astype(f32)
    for i in range(1, raw_ref.shape[0] // 16):
        total = total + raw_ref[16 * i : 16 * i + 16, :].astype(f32)
    norm_ref[...] = total

    def body(i, _):
        r = pl.ds(i * 128, 128)
        n1_ref[r, :] = ln_rows(x_ref[r, :].astype(f32), norm_ref[0:1, :], norm_ref[1:2, :]).astype(bf16)
        return 0

    lax.fori_loop(0, rows // 128, body, 0)
    n1t_ref[...] = n1_ref[...].T
    w = [w_ref[:, width * i : width * i + 256] for i in range(3)]
    attend(bucket_ref, 256, n1_ref[...], *w, qe_ref, k_ref, v_ref, att_ref, vx_ref)
    keep.wait()


def fwd_next_kernel(n_pins, bucket_ref, n1_ref, wq_ref, wk_ref, wv_ref, *refs):
    attend(bucket_ref, 256, n1_ref[...], wq_ref[...], wk_ref[...], wv_ref[...], *refs[n_pins:])


def head_shapes(rows):
    return [SHAPE((4, rows, 128), bf16)] + [SHAPE((rows, 256), bf16)] * 3


def forward_first(bucket, me, x, parts, plan, shard, pins):
    rows, width = x.shape
    full = lambda *s: pl.BlockSpec(s, lambda i: (0,) * len(s))
    shapes = [
        SHAPE((rows, width), bf16),
        SHAPE((width, rows), bf16),
        SHAPE((16, width), f32),
        SHAPE((width, 3 * width), bf16),
    ] + head_shapes(rows)
    return pl.pallas_call(
        lambda b, m, xr, *refs: fwd_first_kernel(
            plan, shard, len(parts), b, m, xr, *refs[: len(parts)], *refs[len(parts) + len(pins) :]
        ),
        grid=(1,),
        in_specs=[SMEM, SMEM, full(rows, width)] + [ANY] * (len(parts) + len(pins)),
        out_specs=[full(*s.shape) for s in shapes[:3]] + [ANY] + [full(*s.shape) for s in shapes[4:]],
        out_shape=in_hbm(shapes),
        scratch_shapes=[
            pltpu.VMEM((width, 3 * width), bf16),
            pltpu.VMEM((width // shard * 16, width), bf16),
            pltpu.VMEM((4, rows, 128), bf16),
            pltpu.SemaphoreType.DMA((32,)),
        ],
        compiler_params=params(VMEM_MIB),
        cost_estimate=cost(8, 12),
        name="fwd_a",
    )(bucket, me, *far(x, *parts), *pins)


def forward_next(g, bucket, n1, w, pins):
    rows, width = n1.shape
    groups = width // 256
    col = lambda j: pl.BlockSpec((width, 256), lambda i: (0, j * groups + g))
    full = lambda *s: pl.BlockSpec(s, lambda i: (0,) * len(s))
    shapes = head_shapes(rows)
    return pl.pallas_call(
        functools.partial(fwd_next_kernel, len(pins)),
        grid=(1,),
        in_specs=[SMEM, full(rows, width), col(0), col(1), col(2)] + [ANY] * len(pins),
        out_specs=[full(*s.shape) for s in shapes],
        out_shape=in_hbm(shapes),
        scratch_shapes=[pltpu.VMEM((4, rows, 128), bf16)],
        compiler_params=params(VMEM_MIB),
        cost_estimate=cost(8, 8),
        name=f"attn_{g}",
    )(bucket, *far(n1, w, w, w), *pins)


UPN = 512
HIDN = 512


def up_kernel(plan, shard, n_parts, me_ref, x_ref, a0, a1, a2, norm_ref, *refs):
    parts = refs[:n_parts]
    mid_ref, n2t_ref, act_ref, gp_ref, wou_hbm, wo_ref, wu_ref, sem, sem2 = refs[n_parts:]
    width = x_ref.shape[1]
    saves = [
        pltpu.make_async_copy(wo_ref, wou_hbm.at[:, :width], sem2.at[0]),
        pltpu.make_async_copy(wu_ref, wou_hbm.at[:, width:], sem2.at[1]),
    ]

    @pl.when(pl.program_id(0) == 0)
    def _():
        jobs = lambda s: [
            ((0, s), slice(0, width), wo_ref, s),
            ((0, s), slice(width, None), wu_ref, s),
        ]
        run(unpack(parts, plan, me_ref[0], shard, jobs, sem))
        for c in saves:
            c.start()

    att = jnp.concatenate([a0[...], a1[...], a2[...]], axis=1)
    mid = x_ref[...].astype(f32) + nn(att, wo_ref[...])
    mid_ref[...] = mid
    n2 = ln_rows(mid, norm_ref[2:3, :], norm_ref[3:4, :]).astype(bf16)
    n2t_ref[...] = n2.T
    for b in range(wu_ref.shape[1] // UPN):
        c = slice(UPN * b, UPN * b + UPN)
        act, gp = gelu_pair(nn(n2, wu_ref[:, c]))
        act_ref[:, c] = act.astype(bf16)
        gp_ref[:, c] = gp.astype(bf16)

    @pl.when(pl.program_id(0) == pl.num_programs(0) - 1)
    def _():
        for c in saves:
            c.wait()


def up_proj(me, x, atts, norms, parts, plan, shard, pins, rb=256):
    rows, width = x.shape
    hidden = parts[0].shape[1] - width
    row = lambda n: pl.BlockSpec((rb, n), lambda i: (i, 0))
    full = lambda *s: pl.BlockSpec(s, lambda i: (0,) * len(s))
    n = len(parts)
    return pl.pallas_call(
        lambda m, xr, a0, a1, a2, nr, *refs: up_kernel(
            plan, shard, n, m, xr, a0, a1, a2, nr, *refs[:n], *refs[n + len(pins) :]
        ),
        grid=(rows // rb,),
        in_specs=[SMEM, row(width)] + [row(256)] * 3 + [full(16, width)] + [ANY] * (n + len(pins)),
        out_specs=[row(width), pl.BlockSpec((width, rb), lambda i: (0, i)), row(hidden), row(hidden), ANY],
        out_shape=in_hbm([
            SHAPE((rows, width), f32),
            SHAPE((width, rows), bf16),
            SHAPE((rows, hidden), bf16),
            SHAPE((rows, hidden), bf16),
            SHAPE((width, width + hidden), bf16),
        ]),
        scratch_shapes=[
            pltpu.VMEM((width, width), bf16),
            pltpu.VMEM((width, hidden), bf16),
            pltpu.SemaphoreType.DMA((32,)),
            pltpu.SemaphoreType.DMA((2,)),
        ],
        compiler_params=params(VMEM_MIB),
        cost_estimate=cost(9, 20),
        name="up_proj",
    )(me, *far(x, *atts, norms), *parts, *pins)


def wdown_kernel(n_pins, me_ref, act_ref, dy_ref, *refs):
    refs[n_pins][0] = tn(act_ref[...], dy_ref[...]).astype(bf16)


def wdown_grad(me, act, dy, core, pins):
    rows, width = dy.shape
    shard = act.shape[1] // 8
    return pl.pallas_call(
        functools.partial(wdown_kernel, len(pins)),
        grid_spec=pltpu.PrefetchScalarGridSpec(
            num_scalar_prefetch=1,
            grid=(4,),
            in_specs=[
                pl.BlockSpec((rows, shard), lambda i, m: (0, m[0] ^ (2 * i + core))),
                pl.BlockSpec((rows, width), lambda i, m: (0, 0)),
            ]
            + [ANY] * len(pins),
            out_specs=pl.BlockSpec((1, shard, width), lambda i, m: (i, 0, 0)),
        ),
        out_shape=SHAPE((4, shard, width), bf16),
        compiler_params=params(VMEM_MIB),
        cost_estimate=cost(5, 13),
        name=f"wdown_{core}",
    )(me, *far(act, dy), *pins)


def hidden_kernel(plan, shard, n_parts, me_ref, dy_ref, gp_ref, n2t_ref, *refs):
    parts = refs[:n_parts]
    gup_ref, keep_ref, send_ref, wd_hbm, wd_ref, g_ref, sem, sem2 = refs[n_parts:]
    i = pl.program_id(0)
    save = pltpu.make_async_copy(wd_ref, wd_hbm, sem2.at[0])

    @pl.when(i == 0)
    def _():
        run(unpack(parts, plan, me_ref[0], shard, lambda s: [((0, s), slice(None), wd_ref, s)], sem))
        save.start()

    fb = gp_ref.shape[1]
    for b in range(fb // HIDN):
        c = slice(HIDN * b, HIDN * b + HIDN)
        w = wd_ref[pl.ds(pl.multiple_of(i * fb, 256) + HIDN * b, HIDN), :]
        gup_ref[:, c] = (nt(dy_ref[...], w) * gp_ref[:, c].astype(f32)).astype(bf16)
        g_ref[:, c] = nn(n2t_ref[...], gup_ref[:, c]).astype(bf16)
    put_slots(g_ref, (keep_ref, send_ref), me_ref[0], slice(None))

    @pl.when(i == pl.num_programs(0) - 1)
    def _():
        save.wait()


def hidden_bwd(me, dy, gp, n2t, parts, plan, shard, pins, fb=512):
    rows, width = dy.shape
    hidden = gp.shape[1]
    full = lambda *s: pl.BlockSpec(s, lambda i: (0,) * len(s))
    col = pl.BlockSpec((rows, fb), lambda i: (0, i))
    out = SHAPE((4, width // 8, hidden), bf16)
    spec = pl.BlockSpec((4, width // 8, fb), lambda i: (0, 0, i))
    n = len(parts)
    return pl.pallas_call(
        lambda m, a, b, c, *refs: hidden_kernel(plan, shard, n, m, a, b, c, *refs[:n], *refs[n + len(pins) :]),
        grid=(hidden // fb,),
        in_specs=[SMEM, full(rows, width), col, full(width, rows)] + [ANY] * (n + len(pins)),
        out_specs=[col, spec, spec, ANY],
        out_shape=in_hbm([SHAPE((rows, hidden), bf16)]) + [out, out] + in_hbm([SHAPE((hidden, width), bf16)]),
        scratch_shapes=[
            pltpu.VMEM((hidden, width), bf16),
            pltpu.VMEM((width, fb), bf16),
            pltpu.SemaphoreType.DMA((32,)),
            pltpu.SemaphoreType.DMA((1,)),
        ],
        compiler_params=params(VMEM_MIB),
        cost_estimate=cost(10, 26),
        name="hidden_bwd",
    )(me, *far(dy, gp, n2t), *parts, *pins)


def mid_kernel(n_pins, me_ref, dy_ref, gup_ref, mid_ref, norm_ref, wou_ref, a0, a1, a2, *refs):
    gmid_ref, gatt_ref, gg_ref, keep_ref, send_ref, gmb_ref, g_ref = refs[n_pins:]
    rb, width = dy_ref.shape
    i = pl.program_id(0)

    @pl.when(i == 0)
    def _():
        gg_ref[...] = jnp.zeros_like(gg_ref)

    gn2 = nt(gup_ref[...], wou_ref[:, width:])
    dx, dg, db = ln_back(gn2, mid_ref[...], norm_ref[2:3, :])
    gm = dy_ref[...].astype(f32) + dx
    gmid_ref[...] = gm
    gmb = gm.astype(bf16)
    gmb_ref[pl.ds(pl.multiple_of(i * rb, rb), rb), :] = gmb
    gg_ref[0:1, :] += dg
    gg_ref[1:2, :] += db
    gatt_ref[...] = nt(gmb, wou_ref[:, :width]).astype(bf16)

    @pl.when(i == pl.num_programs(0) - 1)
    def _():
        for j, a in enumerate((a0, a1, a2)):
            g_ref[256 * j : 256 * j + 256, :] = tn(a[...], gmb_ref[...]).astype(bf16)
        put_slots(g_ref, (keep_ref, send_ref), me_ref[0], slice(None))


def mid_bwd(me, dy, gup, mid, norms, wou, atts, pins, rb=256):
    rows, width = dy.shape
    hidden = gup.shape[1]
    row = lambda n: pl.BlockSpec((rb, n), lambda i: (i, 0))
    full = lambda *s: pl.BlockSpec(s, lambda i: (0,) * len(s))
    once = lambda *s: pl.BlockSpec(s, lambda i: (0,) * len(s), pipeline_mode=pl.Buffered(1))
    out = SHAPE((4, width // 8, 2 * width), bf16)
    spec = pl.BlockSpec((4, width // 8, width), lambda i: (0, 0, 0))
    return pl.pallas_call(
        functools.partial(mid_kernel, len(pins)),
        grid=(rows // rb,),
        in_specs=[SMEM, row(width), row(hidden), row(width), full(16, width), VMEM]
        + [full(rows, 256)] * 3
        + [ANY] * len(pins),
        out_specs=[row(width), row(width), full(8, width), spec, spec],
        out_shape=in_hbm([SHAPE((rows, width), f32), SHAPE((rows, width), bf16), SHAPE((8, width), f32)]) + [out, out],
        scratch_shapes=[pltpu.VMEM((rows, width), bf16), pltpu.VMEM((width, width), bf16)],
        compiler_params=params(VMEM_MIB),
        cost_estimate=cost(8, 24),
        name="mid_bwd",
    )(me, *far(dy, gup, mid, norms), wou, *far(*atts), *pins)


def bwd_kernel(kb, n_pins, bucket_ref, me_ref, qe_ref, k_ref, v_ref, att_ref, do_ref, n1t_hbm, *refs):
    dq_ref, dk_ref, dv_ref, keep_ref, send_ref, doe_ref, ke_ref, ve_ref, dqa_ref, g_ref, n1t_ref, sem = refs[n_pins:]
    rows = k_ref.shape[0]
    load = pltpu.make_async_copy(n1t_hbm, n1t_ref, sem.at[0])

    @pl.when(pl.program_id(0) == 0)
    def _():
        load.start()

    lane = lax.broadcasted_iota(jnp.int32, (rows, 128), 1)
    low = lane < 64
    do, k, v = do_ref[...], k_ref[...], v_ref[...]
    across = lambda i: lax.broadcasted_iota(jnp.int32, (128, 128), i) // 64
    other = jnp.where(across(0) + across(1) == 1, 1.0, 0.0).astype(bf16)
    d = sum(nn(t.astype(bf16), other) for t in terms(do.astype(f32) * att_ref[...].astype(f32)))
    rest = spread(d, lane)
    ones = jnp.where((lane & 63) < 3, 1.0, 0.0).astype(bf16)
    for j in range(2):
        own = low if j == 0 else ~low
        doe_ref[j] = jnp.where(own, do, rest)
        ke_ref[j] = jnp.where(own, k, ones)
        ve_ref[j] = jnp.where(own, v, ones)

    def block(kr, qr):
        lowk = lax.broadcasted_iota(jnp.int32, (kr.size, 128), 1) < 64
        dks, dvs, dqs = [], [], []
        sts = [nt(ke_ref[j, kr, :], qe_ref[j, qr, :]) for j in range(2)]
        dpts = [nt(ve_ref[j, kr, :], doe_ref[j, qr, :]) for j in range(2)]
        for j in range(2):
            pt = jnp.exp(sts[j])
            ds = (pt * dpts[j]).astype(bf16)
            dvs.append(nn(pt.astype(bf16), do_ref[qr, :]))
            dks.append(nn(ds, qe_ref[j, qr, :]))
            dqs.append(tn(k_ref[kr, :], ds).T)
        dk_ref[kr, :] = jnp.where(lowk, dks[0], dks[1]).astype(bf16)
        dv_ref[kr, :] = jnp.where(lowk, dvs[0], dvs[1]).astype(bf16)
        return dqs

    is_long = bucket_ref[0] == 1

    @pl.when(is_long)
    def _():
        if kb == rows:
            dqs = block(pl.ds(0, rows), slice(None))
            dq_ref[...] = (jnp.where(low, dqs[0], dqs[1]) * HEAD_DIM**-0.5).astype(bf16)
            return
        dqa_ref[...] = jnp.zeros_like(dqa_ref)

        def body(i, _):
            dqs = block(pl.ds(i * kb, kb), slice(None))
            dqa_ref[...] += jnp.where(low, dqs[0], dqs[1])
            return 0

        lax.fori_loop(0, rows // kb, body, 0)
        dq_ref[...] = (dqa_ref[...] * HEAD_DIM**-0.5).astype(bf16)

    @pl.when(jnp.logical_not(is_long))
    def _():
        lows = lax.broadcasted_iota(jnp.int32, (SHORT, 128), 1) < 64

        def body(i, _):
            r = pl.ds(i * SHORT, SHORT)
            dqs = block(r, r)
            dq_ref[r, :] = (jnp.where(lows, dqs[0], dqs[1]) * HEAD_DIM**-0.5).astype(bf16)
            return 0

        lax.fori_loop(0, rows // SHORT, body, 0)

    @pl.when(pl.program_id(0) == 0)
    def _():
        load.wait()

    g_ref[...] = nn(n1t_ref[...], jnp.concatenate([dq_ref[...], dk_ref[...], dv_ref[...]], axis=1)).astype(bf16)
    put_slots(g_ref, (keep_ref, send_ref), me_ref[0], slice(None))


def attn_bwd(g, bucket, me, heads, gatt, n1t, into, first, pins):
    qe, k, v, att = heads
    rows = k.shape[0]
    width = n1t.shape[0]
    col = pl.BlockSpec((rows, 128), lambda i: (0, i))
    out = SHAPE(into[0].shape if into else (4, width // 8, 768), bf16)
    spec = pl.BlockSpec((4, width // 8, 384), lambda i: (0, 0, first + i))
    into = list(into or [])
    return pl.pallas_call(
        functools.partial(bwd_kernel, 512, len(into) + len(pins)),
        grid=(2,),
        in_specs=[
            SMEM,
            SMEM,
            pl.BlockSpec((2, rows, 128), lambda i: (i, 0, 0)),
            col,
            col,
            col,
            pl.BlockSpec((rows, 128), lambda i: (0, 2 * g + i)),
        ]
        + [ANY] * (1 + len(into) + len(pins)),
        input_output_aliases={8 + i: 3 + i for i in range(len(into))},
        out_specs=[col] * 3 + [spec] * 2,
        out_shape=in_hbm([SHAPE((rows, 256), bf16)] * 3) + [out, out],
        scratch_shapes=[pltpu.VMEM((2, rows, 128), bf16)] * 3
        + [
            pltpu.VMEM((rows, 128), f32),
            pltpu.VMEM((width, 384), bf16),
            pltpu.VMEM((width, rows), bf16),
            pltpu.SemaphoreType.DMA((1,)),
        ],
        compiler_params=params(VMEM_MIB),
        cost_estimate=cost(14, 8),
        name=f"attn_bwd_{g}",
    )(bucket, me, *far(qe, k, v, att, gatt, n1t), *into, *pins)


def tail_kernel(n_pins, x_ref, *refs):
    ds = refs[:9]
    w_ref, gmid_ref, norm_ref = refs[9:12]
    tg_ref, gg_ref = refs[12 + n_pins :]

    @pl.when(pl.program_id(0) == 0)
    def _():
        gg_ref[...] = jnp.zeros_like(gg_ref)

    d = jnp.concatenate([ds[3 * g + j][...] for j in range(3) for g in range(3)], axis=1)
    dx, dg, db = ln_back(nt(d, w_ref[...]), x_ref[...].astype(f32), norm_ref[0:1, :])
    tg_ref[...] = (gmid_ref[...] + dx).astype(bf16)
    gg_ref[0:1, :] += dg
    gg_ref[1:2, :] += db


def tail_bwd(x, ds, w, gmid, norms, pins, rb=256):
    rows, width = x.shape
    row = lambda n: pl.BlockSpec((rb, n), lambda i: (i, 0))
    full = lambda *s: pl.BlockSpec(s, lambda i: (0,) * len(s))
    once = lambda *s: pl.BlockSpec(s, lambda i: (0,) * len(s), pipeline_mode=pl.Buffered(1))
    return pl.pallas_call(
        functools.partial(tail_kernel, len(pins)),
        grid=(rows // rb,),
        in_specs=[row(width)] + [row(256)] * 9 + [VMEM, row(width), full(16, width)] + [ANY] * len(pins),
        out_specs=[row(width), full(8, width)],
        out_shape=in_hbm([SHAPE((rows, width), bf16), SHAPE((8, width), f32)]),
        compiler_params=params(VMEM_MIB),
        cost_estimate=cost(5, 16),
        name="tail_bwd",
    )(*far(x, *ds), w, *far(gmid, norms), *pins)


def mixed_kernel(n_pins, mid_ref, act_ref, wd_ref, *refs):
    refs[n_pins][...] = (mid_ref[...] + nn(act_ref[...], wd_ref[...])).astype(bf16)


def mixed_out(mid, act, wd, pins, rb=256):
    rows, width = mid.shape
    hidden = act.shape[1]
    row = lambda n: pl.BlockSpec((rb, n), lambda i: (i, 0))
    once = pl.BlockSpec((hidden, width), lambda i: (0, 0), pipeline_mode=pl.Buffered(1))
    return pl.pallas_call(
        functools.partial(mixed_kernel, len(pins)),
        grid=(rows // rb,),
        in_specs=[row(width), row(hidden), VMEM] + [ANY] * len(pins),
        out_specs=row(width),
        out_shape=in_hbm([SHAPE((rows, width), bf16)])[0],
        compiler_params=params(VMEM_MIB),
        cost_estimate=cost(5, 16),
        name="mixed_out",
    )(*far(mid, act), wd, *pins)


def packet_kernel(n_in, *refs):
    ins, out_ref = refs[:n_in], refs[-1]
    col = 0
    for v in ins:
        out_ref[:, col : col + v.shape[1]] = v[...]
        col += v.shape[1]


def packet(arrays, pins, name):
    rows, cols = arrays[0].shape[0], sum(a.shape[1] for a in arrays)
    full = lambda *s: pl.BlockSpec(s, lambda i: (0,) * len(s))
    return pl.pallas_call(
        functools.partial(packet_kernel, len(arrays)),
        grid=(1,),
        in_specs=[full(*a.shape) for a in arrays] + [ANY] * len(pins),
        out_specs=full(rows, cols),
        out_shape=SHAPE((rows, cols), bf16),
        compiler_params=params(8),
        cost_estimate=cost(0, 2),
        name=name,
    )(*arrays, *pins)


def gate(arrays, pins):
    n = len(arrays)
    if not pins:
        return list(arrays)
    return list(pl.pallas_call(
        lambda *refs: None,
        in_specs=[ANY] * (n + len(pins)),
        out_specs=[ANY] * n,
        out_shape=[SHAPE(a.shape, a.dtype) for a in arrays],
        input_output_aliases={i: i for i in range(n)},
        compiler_params=params(1),
        cost_estimate=cost(0, 0),
        name="gate",
    )(*arrays, *pins))


def total(*vs):
    out = vs[0].astype(f32)
    for v in vs[1:]:
        out = out + v.astype(f32)
    return out.astype(bf16)


def combine_kernel(plan, n_in, n_pins, odd_ref, *refs):
    outs = refs[n_in + n_pins :]
    odd = odd_ref[0] == 1
    at = 0
    for f, spots, n_out in plan:
        values = f(odd, *[refs[i] for i in spots])
        for v in values:
            outs[at][...] = v.astype(outs[at].dtype)
            at += 1


def combine(jobs, odd, pins, name, grid=1):
    arrays, shapes, plan = [], [], []
    for f, ins, outs in jobs:
        spots = []
        for a in ins:
            known = [i for i, b in enumerate(arrays) if b is a]
            spots.append(known[0] if known else len(arrays))
            if not known:
                arrays.append(a)
        plan.append((f, spots, len(outs)))
        shapes += [o if isinstance(o, SHAPE) else SHAPE(o, bf16) for o in outs]
    block = lambda s: pl.BlockSpec(s[:-1] + (s[-1] // grid,), lambda i: (0,) * (len(s) - 1) + (i,))
    sums = pl.pallas_call(
        functools.partial(combine_kernel, plan, len(arrays), len(pins)),
        grid=(grid,),
        in_specs=[SMEM] + [block(a.shape) for a in arrays] + [ANY] * len(pins),
        out_specs=[block(s.shape) for s in shapes],
        out_shape=shapes,
        compiler_params=params(24),
        cost_estimate=cost(0, 4),
        name=name,
    )(odd, *arrays, *pins)
    return list(sums)


def swap(v, axis, size, m):
    return lax.ppermute(v, axis, [(i, i ^ m) for i in range(size)])


def part_plan(cut):
    return [(0, 0), (1, 0), (2, 0), (4, 0), (6, 0), (6, cut), (3, 0), (5, 0), (7, 0), (7, cut)]


class Gather:
    def __init__(self, own, cut, size):
        self.own, self.cut, self.size = own, cut, size

    def near(self):
        self.rx, self.ry = (swap(self.own, "fsdp", self.size, m) for m in (2, 4))
        return [self.rx, self.ry]

    def halves(self):
        n, cols = self.own.shape
        return (
            lambda odd, x, y: (y[: self.cut, :], x[self.cut :, :]),
            [self.rx, self.ry],
            [(self.cut, cols), (n - self.cut, cols)],
        )

    def opposite(self, to_x, to_y):
        self.da, self.db = swap(to_x, "fsdp", self.size, 2), swap(to_y, "fsdp", self.size, 4)
        return [self.da, self.db]

    def core_near(self):
        self.rc, *self.near_c = [swap(v, "fsdp", self.size, 1) for v in (self.own, self.rx, self.ry)]

    def parts(self):
        opp = [self.da, self.db]
        return [self.own, self.rc, self.rx, self.ry] + opp + self.near_c + [swap(v, "fsdp", self.size, 1) for v in opp]


class Chain:
    def __init__(self, packets, plan, n_fsdp, n_rep):
        self.mine, self.got = [], []
        self.plan = ("core",) + plan
        self.at = 0
        self.f = lambda v, m: swap(v, "fsdp", n_fsdp, m)
        self.z = lambda v, m: swap(v, "rep", n_rep, m)
        self.join(packets)

    def join(self, packets):
        keep, send = packets
        self.mine.append(keep)
        self.got.append(self.f(send, 1))
        self.shape = (keep.shape[1], sum(k.shape[2] for k in self.mine))

    def job(self):
        done = self.plan[self.at]
        then = self.plan[self.at + 1] if self.at + 1 < len(self.plan) else None
        rows, cols = self.shape
        h = rows // 2
        whole, half = (rows, cols), (h, cols)
        if done == "core" and then == "xy":

            def f(odd, *vs):
                n = len(vs) // 2
                pairs = list(zip(vs[:n], vs[n:]))
                return tuple(jnp.concatenate([total(k[s], g[s]) for k, g in pairs], axis=1) for s in range(4))

            return f, self.mine + self.got, [whole] * 4
        if done == "core":

            def f(odd, k, g):
                part = lambda s, t, lo: jnp.stack([total(k[i, lo : lo + h, :], g[i, lo : lo + h, :]) for i in (s, t)])
                return part(0, 2, 0), part(0, 1, h), part(1, 3, 0), part(2, 3, h)

            return f, self.mine + self.got, [(2,) + half] * 4
        if done == "a":
            f = lambda odd, a, b, ra, rb: (total(a[0], ra[0]), total(b[0], rb[0]), total(a[1], ra[1]), total(b[1], rb[1]))
            return f, self.mine + self.got, [half] * 4
        if done in ("b", "xy"):

            def f(odd, *vs):
                if done == "b":
                    a, b, ra, rb = vs
                    lo, hi = total(a[...], ra[...]), total(b[...], rb[...])
                else:
                    lo, hi = (total(*[v[r, :] for v in vs]) for r in (slice(0, h), slice(h, rows)))
                if then == "p1":
                    return (jnp.concatenate([lo, hi], axis=0),)
                return jnp.where(odd, hi, lo), jnp.where(odd, lo, hi)

            return f, self.mine + self.got, [whole] if then == "p1" else [half] * 2
        if done == "h3":

            def f(odd, p, o):
                p, o = p[...], o[...]
                return (jnp.concatenate([jnp.where(odd, o, p), jnp.where(odd, p, o)], axis=0),)

            return f, self.mine + self.got, [SHAPE(whole, f32)]
        out = half if done[0] == "h" else whole
        return (lambda odd, a, b: (total(a[...], b[...]),)), self.mine + self.got, [out if then else SHAPE(out, f32)]

    def go(self, sums):
        self.at += 1
        step = self.plan[self.at] if self.at < len(self.plan) else None
        if step == "xy":
            self.mine, out = sums[:1], sums[1:]
            self.got = [self.f(v, m) for v, m in zip(out, (2, 4, 6))]
        elif step in ("a", "b"):
            self.mine, out = sums[:2], sums[2:]
            self.got = [self.f(v, m) for v, m in zip(out, (2, 4) if step == "a" else (4, 2))]
        elif step == "h1":
            self.mine, self.got = sums[:1], [self.z(sums[1], 1)]
        else:
            self.mine = sums
            self.got = [self.z(sums[0], 2 if step in ("h2", "p2") else 1)] if step else []


def advance(chains, extra, odd, pins, name, grid=1):
    jobs = [c.job() for c in chains] + extra
    sums = combine(jobs, odd, pins, name, grid)
    at = 0
    for c, job in zip(chains, jobs):
        c.go(sums[at : at + len(job[2])])
        at += len(job[2])
    return sums, sums[at:]


def natural(v, width):
    pairs = width // LANES
    return jnp.concatenate([v[:, LANES * (3 * p + j) :][:, :LANES] for j in range(3) for p in range(pairs)], axis=1)


def last_job(cq, cr):
    rows, cols = cq.shape
    width = cr.shape[1]

    def f(odd, p, o, a, b):
        p, o = p[...], o[...]
        q = jnp.concatenate([jnp.where(odd, o, p), jnp.where(odd, p, o)], axis=0)
        return q[:, :width], natural(jnp.concatenate([q[:, width:], total(a[...], b[...])], axis=1), width)

    return f, cq.mine + cq.got + cr.mine + cr.got, [SHAPE((rows, width), f32), SHAPE((rows, cols), f32)]


def sum_chips(v, size):
    x, y, d = (swap(v, "fsdp", size, m) for m in (2, 4, 6))
    return (v + x) + (y + d)


def sum_replicas(v, size):
    a, b, c = (swap(v, "rep", size, m) for m in (1, 2, 3))
    return (v + a) + (b + c)


def whole(keep, send):
    return jnp.stack([keep, send], axis=1).reshape(-1, keep.shape[2])


def shards(
    n_fsdp, n_rep, tokens, bucket, ln1_gain, ln1_bias, w_qkv, w_out, ln2_gain, ln2_bias, w_up, w_down, cotangent
):
    width = tokens.shape[1]
    fast = n_fsdp == 8 and n_rep == 4
    index = lax.axis_index("fsdp")
    vectors = jnp.stack([ln1_gain, ln1_bias, ln2_gain, ln2_bias])
    if fast:
        me = jnp.reshape(index, (1,)).astype(jnp.int32)
        owner = lax.broadcasted_iota(jnp.int32, (4, width), 1) // (width // 8)
        spread = jnp.where(owner == index, jnp.tile(vectors, (1, 8)), 0)
    else:
        me = jnp.zeros((1,), jnp.int32)
        spread = lax.all_gather(vectors, "fsdp", axis=1, tiled=True)
        w_qkv, w_out, w_up, w_down = (
            lax.all_gather(w, "fsdp", axis=0, tiled=True) for w in (w_qkv, w_out, w_up, w_down)
        )
    local = w_qkv.shape[0]
    norm_rows = jnp.pad(spread, ((0, 12), (0, w_qkv.shape[1] - width)))
    packet_q = jnp.concatenate([w_qkv, norm_rows], axis=0)
    cut, cut_d = local // 2, w_down.shape[0] // 2
    none = [(0, 0)]
    odd = jnp.reshape(lax.axis_index("rep") & 1, (1,)).astype(jnp.int32)

    if fast:
        gq = Gather(packet_q, cut, n_fsdp)
        gq.near()
        far_q = gq.opposite(gq.ry[:cut], gq.rx[cut:])
        gq.core_near()
        (own_u,) = gate([packet([w_out, w_up], [], "packet_up")], far_q + [gq.rc] + gq.near_c)
        gu = Gather(own_u, cut, n_fsdp)
        near_u = gu.near()
        gd = Gather(None, cut_d, n_fsdp)
        plan, plan_d = part_plan(cut), part_plan(cut_d)
        parts_q = gq.parts()
    else:
        plan, plan_d = none, none
        parts_q = [packet_q]

    def pin(v):
        return list(v) if fast else []

    n1, n1t, norms, w_full, *heads0 = forward_first(
        bucket, me, tokens, parts_q, plan, local, pin([own_u] if fast else [])
    )
    sums = []
    if fast:
        sums, (to_x, to_y, own_d) = advance(
            [], [gu.halves(), (lambda o, w: (w[...],), [w_down], [w_down.shape])], odd, far(n1t), "after_a"
        )
        gu.opposite(to_x, to_y)
        gu.rx, gu.ry = gate([gu.rx, gu.ry], far(n1t))
        (gu.own,) = gate([gu.own], far(n1t))
        gu.core_near()
    heads1 = forward_next(1, bucket, n1, w_full, pin(sums))
    sums = []
    if fast:
        gu.da, gu.db, gd.own, gu.rc, *gu.near_c = gate([gu.da, gu.db, own_d, gu.rc] + gu.near_c, far(heads1[3]))
        sums = [gd.own]
        gd.near()
        parts_u = gu.parts()
    heads2 = forward_next(2, bucket, n1, w_full, pin(sums))
    heads = [heads0, heads1, heads2]
    atts = [h[3] for h in heads]
    if fast:
        sums, (to_x, to_y) = advance([], [gd.halves()], odd, far(heads2[3]), "after_c")
        gd.opposite(to_x, to_y)
        gd.core_near()
    else:
        parts_u = [packet([w_out, w_up], [], "packet_up")]
    mid, n2t, act, gp, w_ou = up_proj(me, tokens, atts, norms, parts_u, plan, local, pin(sums))
    if fast:
        gd.da, gd.db = gate([gd.da, gd.db], far(n2t))
        parts_d = gd.parts()
    else:
        parts_d = [w_down]
    send_d = wdown_grad(me, act, cotangent, 1, pin([gd.da, gd.db] if fast else []))
    halves, direct = ("a", "b", "h1", "h2", "h3"), ("xy", "p1", "p2")
    chain = lambda pk, plan: Chain(pk, plan, n_fsdp, n_rep) if fast else None

    def step(chains, after, name):
        return advance(chains, [], odd, after, name)[0][-1:] if fast else []

    if fast:
        (send_d,) = gate([send_d], parts_d)
    pk_d = [wdown_grad(me, act, cotangent, 0, pin([send_d])), send_d]
    cd = chain(pk_d, halves)
    sums = step([cd], [], "after_wdown")
    gup, *pk_u, w_dn = hidden_bwd(me, cotangent, gp, n2t, parts_d, plan_d, w_down.shape[0], pin(sums))
    sums = step([cd], far(gup), "after_hidden")
    if fast:
        pk_u = [pk_u[0]] + gate([pk_u[1]], sums)
    cu = chain(pk_u, halves)
    gmid, gatt, g_norm2, *pk_q = mid_bwd(me, cotangent, gup, mid, norms, w_ou, atts, pin(sums))
    sums = step([cd, cu], far(g_norm2), "after_mid")
    *d0, k, s = attn_bwd(0, bucket, me, heads[0], gatt, n1t, pk_q, 2, pin(sums))
    sums = step([cd, cu], far(d0[0]), "after_bwd0")
    pk_q = [k] + (gate([s], sums) if fast else [s])
    cq = chain(pk_q, ("xy", "h1", "h2", "h3"))
    *d1, k, s = attn_bwd(1, bucket, me, heads[1], gatt, n1t, None, 0, pin(sums))
    s0 = step([cd, cu], far(d1[0]), "after_bwd1")
    pk_1 = [k] + (gate([s], s0) if fast else [s])
    if fast:
        cq.join(pk_1)
    sums = step([cq], s0, "after_bwd1_q")
    *d2, k, s = attn_bwd(2, bucket, me, heads[2], gatt, n1t, None, 0, pin(s0 + sums))
    s0 = step([cd, cu, cq], far(d2[0]), "after_bwd2")
    pk_r = [k] + (gate([s], s0) if fast else [s])
    cr = chain(pk_r, direct)
    sums = step([cr], s0, "after_bwd2_r")
    tokens_grad, g_norm1 = tail_bwd(tokens, d0 + d1 + d2, w_full, gmid, norms, pin(s0 + sums))
    sums = step([cu, cq, cr], far(g_norm1), "after_tail")
    g_norms = jnp.concatenate([g_norm1[:2], g_norm2[:2]], axis=0)
    if fast:
        (g_norms,) = gate([g_norms], sums)
        g_norms_c = swap(g_norms, "fsdp", n_fsdp, 1)
    mixed = mixed_out(mid, act, w_dn, pin(sums))
    sums = step([cu, cq, cr], far(mixed), "after_mixed")
    if fast:
        (g_norms,) = gate([g_norms], sums)
        g_norms = sum_chips(g_norms + g_norms_c, n_fsdp)
    if fast:
        (g_norms,) = gate([g_norms], cq.got)
        g_norms = sum_replicas(g_norms, n_rep)
    if fast:
        gw_out, gw_q = combine([last_job(cq, cr)], odd, [], "last")

    if fast:
        (rows_d,), (rows_u,) = (c.mine for c in (cd, cu))
    else:
        g_norms = lax.psum(g_norms, ("fsdp", "rep"))
        rows_q, rows_1, rows_r, rows_u, rows_d = (whole(*pk) for pk in (pk_q, pk_1, pk_r, pk_u, pk_d))
        rows_q = jnp.concatenate([rows_q, rows_1], axis=1)
        gw_out = rows_q[:, :width]
        gw_q = natural(jnp.concatenate([rows_q[:, width:], rows_r], axis=1), width)
    g_norms = lax.dynamic_slice_in_dim(g_norms, index * (width // n_fsdp), width // n_fsdp, axis=1)
    grads = (gw_q, gw_out, rows_u, rows_d)
    if not fast:
        grads = tuple(
            lax.psum(lax.psum_scatter(g, "fsdp", scatter_dimension=0, tiled=True), "rep") for g in grads
        )
    gw_qkv, gw_out, gw_up, gw_down = (g.astype(f32) for g in grads)
    return (
        mixed,
        tokens_grad,
        g_norms[0],
        g_norms[1],
        gw_qkv,
        gw_out,
        g_norms[2],
        g_norms[3],
        gw_up,
        gw_down,
    )


def solution(mesh):
    return jax.shard_map(
        functools.partial(shards, mesh.shape["fsdp"], mesh.shape["rep"]),
        mesh=mesh,
        in_specs=(
            P(("rep", "fsdp"), None),
            P(("rep", "fsdp")),
            P("fsdp"),
            P("fsdp"),
            P("fsdp", None),
            P("fsdp", None),
            P("fsdp"),
            P("fsdp"),
            P("fsdp", None),
            P("fsdp", None),
            P(("rep", "fsdp"), None),
        ),
        out_specs=(
            P(("rep", "fsdp"), None),
            P(("rep", "fsdp"), None),
            P("fsdp"),
            P("fsdp"),
            P("fsdp", None),
            P("fsdp", None),
            P("fsdp"),
            P("fsdp"),
            P("fsdp", None),
            P("fsdp", None),
        ),
        check_vma=False,
    )
```

```python
import functools

import jax
import jax.numpy as jnp
from jax import lax
from jax.experimental import pallas as pl
from jax.experimental.pallas import tpu as pltpu
from jax.sharding import PartitionSpec as P

HEAD_DIM = 64
SHORT = 256
LN_EPS = 1e-6
LANES = 128
f32 = jnp.float32
bf16 = jnp.bfloat16

LOG2E = 1.4426950408889634
ROOT_2PI = (2 * 3.141592653589793) ** -0.5


def nt(a, b):
    return lax.dot_general(a, b, (((1,), (1,)), ((), ())), preferred_element_type=f32)


def nn(a, b):
    return lax.dot_general(a, b, (((1,), (0,)), ((), ())), preferred_element_type=f32)


def tn(a, b):
    return lax.dot_general(a, b, (((0,), (0,)), ((), ())), preferred_element_type=f32)


def ln_rows(x, gain, bias):
    centred = x - jnp.mean(x, axis=-1, keepdims=True)
    var = jnp.mean(centred * centred, axis=-1, keepdims=True)
    return centred * lax.rsqrt(var + LN_EPS) * gain + bias


def ln_back(grad, v, gain):
    centred = v - jnp.mean(v, axis=-1, keepdims=True)
    r = lax.rsqrt(jnp.mean(centred * centred, axis=-1, keepdims=True) + LN_EPS)
    xh = centred * r
    gg = grad * gain
    dx = r * (gg - jnp.mean(gg, axis=-1, keepdims=True) - xh * jnp.mean(gg * xh, axis=-1, keepdims=True))
    return dx, jnp.sum(grad * xh, axis=0, keepdims=True), jnp.sum(grad, axis=0, keepdims=True)


def gelu_pair(u):
    cdf = 0.5 + 0.5 * lax.erf(u * 2**-0.5)
    density = jnp.exp2((u * u) * (-0.5 * LOG2E))
    return u * cdf, cdf + (u * ROOT_2PI) * density


def terms(v):
    hi = v.astype(bf16).astype(f32)
    r = v - hi
    mid = r.astype(bf16).astype(f32)
    return hi, mid, r - mid


def spread(v, lane):
    hi, mid, lo = terms(-v)
    pos = lane & 63
    return jnp.where(pos == 0, hi, jnp.where(pos == 1, mid, jnp.where(pos == 2, lo, 0.0))).astype(bf16)


def unpack(refs, plan, me, shard_rows, jobs, sem):
    copies = []
    for ref, (r, lo) in zip(refs, plan):
        hi = lo + ref.shape[0]
        for (first, last), cols, dst, step in jobs(shard_rows):
            a, b = max(lo, first), min(hi, last)
            if a >= b:
                continue
            row = pl.multiple_of((me ^ r) * step, 16) + (a - first)
            copies.append(
                pltpu.make_async_copy(
                    ref.at[pl.ds(a - lo, b - a), cols], dst.at[pl.ds(row, b - a), :], sem.at[len(copies)]
                )
            )
    return copies


def run(copies):
    for c in copies:
        c.start()
    for c in copies:
        c.wait()


def put_slots(src_ref, outs, me, cols):
    keep, send = outs
    rows = src_ref.shape[0] // 8
    for r in range(8):
        row = pl.multiple_of((me ^ r) * rows, 16)
        (send if r & 1 else keep)[r >> 1, :, cols] = src_ref[pl.ds(row, rows), :]


def params(mib):
    return pltpu.CompilerParams(vmem_limit_bytes=mib << 20)


def cost(gflops, mib):
    return pl.CostEstimate(flops=1000, bytes_accessed=1024, transcendentals=0)


VMEM_MIB = 44
SMEM = pl.BlockSpec(memory_space=pltpu.SMEM)
VMEM = pl.BlockSpec(memory_space=pltpu.VMEM)
ANY = pl.BlockSpec(memory_space=pl.ANY)
SHAPE = jax.ShapeDtypeStruct


def far(*arrays):
    return [pltpu.with_memory_space_constraint(a, pltpu.HBM) for a in arrays]


def in_hbm(shapes):
    return [pltpu.HBM(s.shape, s.dtype) for s in shapes]


def attend(bucket_ref, qb, n1, wq, wk, wv, qe_ref, k_ref, v_ref, att_ref, vx_ref):
    rows = k_ref.shape[0]
    low = lax.broadcasted_iota(jnp.int32, (rows, 128), 1) < 64
    q = nn(n1, wq)
    k_ref[...] = nn(n1, wk).astype(bf16)
    v = nn(n1, wv)
    v_ref[...] = v.astype(bf16)
    q = q * HEAD_DIM**-0.5
    for p in range(2):
        qp = q[:, 128 * p : 128 * p + 128]
        vp = v[:, 128 * p : 128 * p + 128]
        qe_ref[2 * p] = jnp.where(low, qp, 0.0).astype(bf16)
        qe_ref[2 * p + 1] = jnp.where(low, 0.0, qp).astype(bf16)
        vx_ref[2 * p] = jnp.where(low, vp, 1.0).astype(bf16)
        vx_ref[2 * p + 1] = jnp.where(low, 1.0, vp).astype(bf16)

    def block(r, kr):
        lane = lax.broadcasted_iota(jnp.int32, (r.size, 128), 1)
        lowq = lane < 64
        ss = [nt(qe_ref[h, r, :], k_ref[kr, 128 * (h // 2) : 128 * (h // 2) + 128]) for h in range(4)]
        for p in range(2):
            os, tops = [], []
            for h in (2 * p, 2 * p + 1):
                top = jnp.max(ss[h], axis=-1, keepdims=True)
                e = jnp.exp(ss[h] - top).astype(bf16)
                os.append(nn(e, vx_ref[h, kr, :]))
                tops.append(top)
            sums = jnp.where(lowq, os[1], os[0])
            lse = jnp.where(lowq, tops[1], tops[0]) + jnp.log(sums)
            rest = spread(lse, lane)
            q0, q1 = qe_ref[2 * p, r, :], qe_ref[2 * p + 1, r, :]
            qe_ref[2 * p, r, :] = jnp.where(lowq, q0, rest)
            qe_ref[2 * p + 1, r, :] = jnp.where(lowq, rest, q1)
            att = jnp.where(lowq, os[0], os[1]) / pltpu.roll(sums, 64, 1)
            att_ref[r, 128 * p : 128 * p + 128] = att.astype(bf16)

    is_long = bucket_ref[0] == 1

    @pl.when(is_long)
    def _():
        def body(i, _):
            block(pl.ds(i * qb, qb), slice(None))
            return 0

        lax.fori_loop(0, rows // qb, body, 0)

    @pl.when(jnp.logical_not(is_long))
    def _():
        def body(i, _):
            r = pl.ds(i * SHORT, SHORT)
            block(r, r)
            return 0

        lax.fori_loop(0, rows // SHORT, body, 0)


def q_jobs(w_ref, raw_ref):
    width = w_ref.shape[0]
    return lambda shard: [
        ((0, shard), slice(None), w_ref, shard),
        ((shard, shard + 16), slice(0, width), raw_ref, 16),
    ]


def fwd_first_kernel(plan, shard, n_parts, bucket_ref, me_ref, x_ref, *refs):
    parts = refs[:n_parts]
    n1_ref, n1t_ref, norm_ref, whbm_ref, qe_ref, k_ref, v_ref, att_ref, w_ref, raw_ref, vx_ref, sem = refs[n_parts:]
    rows, width = x_ref.shape
    run(unpack(parts, plan, me_ref[0], shard, q_jobs(w_ref, raw_ref), sem))
    keep = pltpu.make_async_copy(w_ref, whbm_ref, sem.at[0])
    keep.start()
    total = raw_ref[0:16, :].astype(f32)
    for i in range(1, raw_ref.shape[0] // 16):
        total = total + raw_ref[16 * i : 16 * i + 16, :].astype(f32)
    norm_ref[...] = total

    def body(i, _):
        r = pl.ds(i * 128, 128)
        n1_ref[r, :] = ln_rows(x_ref[r, :].astype(f32), norm_ref[0:1, :], norm_ref[1:2, :]).astype(bf16)
        return 0

    lax.fori_loop(0, rows // 128, body, 0)
    n1t_ref[...] = n1_ref[...].T
    w = [w_ref[:, width * i : width * i + 256] for i in range(3)]
    attend(bucket_ref, 256, n1_ref[...], *w, qe_ref, k_ref, v_ref, att_ref, vx_ref)
    keep.wait()


def fwd_next_kernel(n_pins, bucket_ref, n1_ref, wq_ref, wk_ref, wv_ref, *refs):
    attend(bucket_ref, 256, n1_ref[...], wq_ref[...], wk_ref[...], wv_ref[...], *refs[n_pins:])


def head_shapes(rows):
    return [SHAPE((4, rows, 128), bf16)] + [SHAPE((rows, 256), bf16)] * 3


def forward_first(bucket, me, x, parts, plan, shard, pins):
    rows, width = x.shape
    full = lambda *s: pl.BlockSpec(s, lambda i: (0,) * len(s))
    shapes = [
        SHAPE((rows, width), bf16),
        SHAPE((width, rows), bf16),
        SHAPE((16, width), f32),
        SHAPE((width, 3 * width), bf16),
    ] + head_shapes(rows)
    return pl.pallas_call(
        lambda b, m, xr, *refs: fwd_first_kernel(
            plan, shard, len(parts), b, m, xr, *refs[: len(parts)], *refs[len(parts) + len(pins) :]
        ),
        grid=(1,),
        in_specs=[SMEM, SMEM, full(rows, width)] + [ANY] * (len(parts) + len(pins)),
        out_specs=[full(*s.shape) for s in shapes[:3]] + [ANY] + [full(*s.shape) for s in shapes[4:]],
        out_shape=in_hbm(shapes),
        scratch_shapes=[
            pltpu.VMEM((width, 3 * width), bf16),
            pltpu.VMEM((width // shard * 16, width), bf16),
            pltpu.VMEM((4, rows, 128), bf16),
            pltpu.SemaphoreType.DMA((32,)),
        ],
        compiler_params=params(VMEM_MIB),
        cost_estimate=cost(8, 12),
        name="fwd_a",
    )(bucket, me, *far(x, *parts), *pins)


def forward_next(g, bucket, n1, w, pins):
    rows, width = n1.shape
    groups = width // 256
    col = lambda j: pl.BlockSpec((width, 256), lambda i: (0, j * groups + g))
    full = lambda *s: pl.BlockSpec(s, lambda i: (0,) * len(s))
    shapes = head_shapes(rows)
    return pl.pallas_call(
        functools.partial(fwd_next_kernel, len(pins)),
        grid=(1,),
        in_specs=[SMEM, full(rows, width), col(0), col(1), col(2)] + [ANY] * len(pins),
        out_specs=[full(*s.shape) for s in shapes],
        out_shape=in_hbm(shapes),
        scratch_shapes=[pltpu.VMEM((4, rows, 128), bf16)],
        compiler_params=params(VMEM_MIB),
        cost_estimate=cost(8, 8),
        name=f"attn_{g}",
    )(bucket, *far(n1, w, w, w), *pins)


UPN = 512
HIDN = 512


def up_kernel(plan, shard, n_parts, me_ref, x_ref, a0, a1, a2, norm_ref, *refs):
    parts = refs[:n_parts]
    mid_ref, n2t_ref, act_ref, gp_ref, wou_hbm, wo_ref, wu_ref, sem, sem2 = refs[n_parts:]
    width = x_ref.shape[1]
    saves = [
        pltpu.make_async_copy(wo_ref, wou_hbm.at[:, :width], sem2.at[0]),
        pltpu.make_async_copy(wu_ref, wou_hbm.at[:, width:], sem2.at[1]),
    ]

    @pl.when(pl.program_id(0) == 0)
    def _():
        jobs = lambda s: [
            ((0, s), slice(0, width), wo_ref, s),
            ((0, s), slice(width, None), wu_ref, s),
        ]
        run(unpack(parts, plan, me_ref[0], shard, jobs, sem))
        for c in saves:
            c.start()

    att = jnp.concatenate([a0[...], a1[...], a2[...]], axis=1)
    mid = x_ref[...].astype(f32) + nn(att, wo_ref[...])
    mid_ref[...] = mid
    n2 = ln_rows(mid, norm_ref[2:3, :], norm_ref[3:4, :]).astype(bf16)
    n2t_ref[...] = n2.T
    for b in range(wu_ref.shape[1] // UPN):
        c = slice(UPN * b, UPN * b + UPN)
        act, gp = gelu_pair(nn(n2, wu_ref[:, c]))
        act_ref[:, c] = act.astype(bf16)
        gp_ref[:, c] = gp.astype(bf16)

    @pl.when(pl.program_id(0) == pl.num_programs(0) - 1)
    def _():
        for c in saves:
            c.wait()


def up_proj(me, x, atts, norms, parts, plan, shard, pins, rb=256):
    rows, width = x.shape
    hidden = parts[0].shape[1] - width
    row = lambda n: pl.BlockSpec((rb, n), lambda i: (i, 0))
    full = lambda *s: pl.BlockSpec(s, lambda i: (0,) * len(s))
    n = len(parts)
    return pl.pallas_call(
        lambda m, xr, a0, a1, a2, nr, *refs: up_kernel(
            plan, shard, n, m, xr, a0, a1, a2, nr, *refs[:n], *refs[n + len(pins) :]
        ),
        grid=(rows // rb,),
        in_specs=[SMEM, row(width)] + [row(256)] * 3 + [full(16, width)] + [ANY] * (n + len(pins)),
        out_specs=[row(width), pl.BlockSpec((width, rb), lambda i: (0, i)), row(hidden), row(hidden), ANY],
        out_shape=in_hbm([
            SHAPE((rows, width), f32),
            SHAPE((width, rows), bf16),
            SHAPE((rows, hidden), bf16),
            SHAPE((rows, hidden), bf16),
            SHAPE((width, width + hidden), bf16),
        ]),
        scratch_shapes=[
            pltpu.VMEM((width, width), bf16),
            pltpu.VMEM((width, hidden), bf16),
            pltpu.SemaphoreType.DMA((32,)),
            pltpu.SemaphoreType.DMA((2,)),
        ],
        compiler_params=params(VMEM_MIB),
        cost_estimate=cost(9, 20),
        name="up_proj",
    )(me, *far(x, *atts, norms), *parts, *pins)


def wdown_kernel(n_pins, me_ref, act_ref, dy_ref, *refs):
    refs[n_pins][0] = tn(act_ref[...], dy_ref[...]).astype(bf16)


def wdown_grad(me, act, dy, core, pins):
    rows, width = dy.shape
    shard = act.shape[1] // 8
    return pl.pallas_call(
        functools.partial(wdown_kernel, len(pins)),
        grid_spec=pltpu.PrefetchScalarGridSpec(
            num_scalar_prefetch=1,
            grid=(4,),
            in_specs=[
                pl.BlockSpec((rows, shard), lambda i, m: (0, m[0] ^ (2 * i + core))),
                pl.BlockSpec((rows, width), lambda i, m: (0, 0)),
            ]
            + [ANY] * len(pins),
            out_specs=pl.BlockSpec((1, shard, width), lambda i, m: (i, 0, 0)),
        ),
        out_shape=SHAPE((4, shard, width), bf16),
        compiler_params=params(VMEM_MIB),
        cost_estimate=cost(5, 13),
        name=f"wdown_{core}",
    )(me, *far(act, dy), *pins)


def hidden_kernel(plan, shard, n_parts, me_ref, dy_ref, gp_ref, n2t_ref, *refs):
    parts = refs[:n_parts]
    gup_ref, keep_ref, send_ref, wd_hbm, wd_ref, g_ref, sem, sem2 = refs[n_parts:]
    i = pl.program_id(0)
    save = pltpu.make_async_copy(wd_ref, wd_hbm, sem2.at[0])

    @pl.when(i == 0)
    def _():
        run(unpack(parts, plan, me_ref[0], shard, lambda s: [((0, s), slice(None), wd_ref, s)], sem))
        save.start()

    fb = gp_ref.shape[1]
    for b in range(fb // HIDN):
        c = slice(HIDN * b, HIDN * b + HIDN)
        w = wd_ref[pl.ds(pl.multiple_of(i * fb, 256) + HIDN * b, HIDN), :]
        gup_ref[:, c] = (nt(dy_ref[...], w) * gp_ref[:, c].astype(f32)).astype(bf16)
        g_ref[:, c] = nn(n2t_ref[...], gup_ref[:, c]).astype(bf16)
    put_slots(g_ref, (keep_ref, send_ref), me_ref[0], slice(None))

    @pl.when(i == pl.num_programs(0) - 1)
    def _():
        save.wait()


def hidden_bwd(me, dy, gp, n2t, parts, plan, shard, pins, fb=512):
    rows, width = dy.shape
    hidden = gp.shape[1]
    full = lambda *s: pl.BlockSpec(s, lambda i: (0,) * len(s))
    col = pl.BlockSpec((rows, fb), lambda i: (0, i))
    out = SHAPE((4, width // 8, hidden), bf16)
    spec = pl.BlockSpec((4, width // 8, fb), lambda i: (0, 0, i))
    n = len(parts)
    return pl.pallas_call(
        lambda m, a, b, c, *refs: hidden_kernel(plan, shard, n, m, a, b, c, *refs[:n], *refs[n + len(pins) :]),
        grid=(hidden // fb,),
        in_specs=[SMEM, full(rows, width), col, full(width, rows)] + [ANY] * (n + len(pins)),
        out_specs=[col, spec, spec, ANY],
        out_shape=in_hbm([SHAPE((rows, hidden), bf16)]) + [out, out] + in_hbm([SHAPE((hidden, width), bf16)]),
        scratch_shapes=[
            pltpu.VMEM((hidden, width), bf16),
            pltpu.VMEM((width, fb), bf16),
            pltpu.SemaphoreType.DMA((32,)),
            pltpu.SemaphoreType.DMA((1,)),
        ],
        compiler_params=params(VMEM_MIB),
        cost_estimate=cost(10, 26),
        name="hidden_bwd",
    )(me, *far(dy, gp, n2t), *parts, *pins)


def mid_kernel(n_pins, me_ref, dy_ref, gup_ref, mid_ref, norm_ref, wou_ref, a0, a1, a2, *refs):
    gmid_ref, gatt_ref, gg_ref, keep_ref, send_ref, gmb_ref, g_ref = refs[n_pins:]
    rb, width = dy_ref.shape
    i = pl.program_id(0)

    @pl.when(i == 0)
    def _():
        gg_ref[...] = jnp.zeros_like(gg_ref)

    gn2 = nt(gup_ref[...], wou_ref[:, width:])
    dx, dg, db = ln_back(gn2, mid_ref[...], norm_ref[2:3, :])
    gm = dy_ref[...].astype(f32) + dx
    gmid_ref[...] = gm
    gmb = gm.astype(bf16)
    gmb_ref[pl.ds(pl.multiple_of(i * rb, rb), rb), :] = gmb
    gg_ref[0:1, :] += dg
    gg_ref[1:2, :] += db
    gatt_ref[...] = nt(gmb, wou_ref[:, :width]).astype(bf16)

    @pl.when(i == pl.num_programs(0) - 1)
    def _():
        for j, a in enumerate((a0, a1, a2)):
            g_ref[256 * j : 256 * j + 256, :] = tn(a[...], gmb_ref[...]).astype(bf16)
        put_slots(g_ref, (keep_ref, send_ref), me_ref[0], slice(None))


def mid_bwd(me, dy, gup, mid, norms, wou, atts, pins, rb=256):
    rows, width = dy.shape
    hidden = gup.shape[1]
    row = lambda n: pl.BlockSpec((rb, n), lambda i: (i, 0))
    full = lambda *s: pl.BlockSpec(s, lambda i: (0,) * len(s))
    once = lambda *s: pl.BlockSpec(s, lambda i: (0,) * len(s), pipeline_mode=pl.Buffered(1))
    out = SHAPE((4, width // 8, 2 * width), bf16)
    spec = pl.BlockSpec((4, width // 8, width), lambda i: (0, 0, 0))
    return pl.pallas_call(
        functools.partial(mid_kernel, len(pins)),
        grid=(rows // rb,),
        in_specs=[SMEM, row(width), row(hidden), row(width), full(16, width), VMEM]
        + [full(rows, 256)] * 3
        + [ANY] * len(pins),
        out_specs=[row(width), row(width), full(8, width), spec, spec],
        out_shape=in_hbm([SHAPE((rows, width), f32), SHAPE((rows, width), bf16), SHAPE((8, width), f32)]) + [out, out],
        scratch_shapes=[pltpu.VMEM((rows, width), bf16), pltpu.VMEM((width, width), bf16)],
        compiler_params=params(VMEM_MIB),
        cost_estimate=cost(8, 24),
        name="mid_bwd",
    )(me, *far(dy, gup, mid, norms), wou, *far(*atts), *pins)


def bwd_kernel(kb, n_pins, bucket_ref, me_ref, qe_ref, k_ref, v_ref, att_ref, do_ref, n1t_hbm, *refs):
    dq_ref, dk_ref, dv_ref, keep_ref, send_ref, doe_ref, ke_ref, ve_ref, dqa_ref, g_ref, n1t_ref, sem = refs[n_pins:]
    rows = k_ref.shape[0]
    load = pltpu.make_async_copy(n1t_hbm, n1t_ref, sem.at[0])

    @pl.when(pl.program_id(0) == 0)
    def _():
        load.start()

    lane = lax.broadcasted_iota(jnp.int32, (rows, 128), 1)
    low = lane < 64
    do, k, v = do_ref[...], k_ref[...], v_ref[...]
    across = lambda i: lax.broadcasted_iota(jnp.int32, (128, 128), i) // 64
    other = jnp.where(across(0) + across(1) == 1, 1.0, 0.0).astype(bf16)
    d = sum(nn(t.astype(bf16), other) for t in terms(do.astype(f32) * att_ref[...].astype(f32)))
    rest = spread(d, lane)
    ones = jnp.where((lane & 63) < 3, 1.0, 0.0).astype(bf16)
    for j in range(2):
        own = low if j == 0 else ~low
        doe_ref[j] = jnp.where(own, do, rest)
        ke_ref[j] = jnp.where(own, k, ones)
        ve_ref[j] = jnp.where(own, v, ones)

    def block(kr, qr):
        lowk = lax.broadcasted_iota(jnp.int32, (kr.size, 128), 1) < 64
        dks, dvs, dqs = [], [], []
        sts = [nt(ke_ref[j, kr, :], qe_ref[j, qr, :]) for j in range(2)]
        dpts = [nt(ve_ref[j, kr, :], doe_ref[j, qr, :]) for j in range(2)]
        for j in range(2):
            pt = jnp.exp(sts[j])
            ds = (pt * dpts[j]).astype(bf16)
            dvs.append(nn(pt.astype(bf16), do_ref[qr, :]))
            dks.append(nn(ds, qe_ref[j, qr, :]))
            dqs.append(tn(k_ref[kr, :], ds).T)
        dk_ref[kr, :] = jnp.where(lowk, dks[0], dks[1]).astype(bf16)
        dv_ref[kr, :] = jnp.where(lowk, dvs[0], dvs[1]).astype(bf16)
        return dqs

    is_long = bucket_ref[0] == 1

    @pl.when(is_long)
    def _():
        if kb == rows:
            dqs = block(pl.ds(0, rows), slice(None))
            dq_ref[...] = (jnp.where(low, dqs[0], dqs[1]) * HEAD_DIM**-0.5).astype(bf16)
            return
        dqa_ref[...] = jnp.zeros_like(dqa_ref)

        def body(i, _):
            dqs = block(pl.ds(i * kb, kb), slice(None))
            dqa_ref[...] += jnp.where(low, dqs[0], dqs[1])
            return 0

        lax.fori_loop(0, rows // kb, body, 0)
        dq_ref[...] = (dqa_ref[...] * HEAD_DIM**-0.5).astype(bf16)

    @pl.when(jnp.logical_not(is_long))
    def _():
        lows = lax.broadcasted_iota(jnp.int32, (SHORT, 128), 1) < 64

        def body(i, _):
            r = pl.ds(i * SHORT, SHORT)
            dqs = block(r, r)
            dq_ref[r, :] = (jnp.where(lows, dqs[0], dqs[1]) * HEAD_DIM**-0.5).astype(bf16)
            return 0

        lax.fori_loop(0, rows // SHORT, body, 0)

    @pl.when(pl.program_id(0) == 0)
    def _():
        load.wait()

    g_ref[...] = nn(n1t_ref[...], jnp.concatenate([dq_ref[...], dk_ref[...], dv_ref[...]], axis=1)).astype(bf16)
    put_slots(g_ref, (keep_ref, send_ref), me_ref[0], slice(None))


def attn_bwd(g, bucket, me, heads, gatt, n1t, into, first, pins):
    qe, k, v, att = heads
    rows = k.shape[0]
    width = n1t.shape[0]
    col = pl.BlockSpec((rows, 128), lambda i: (0, i))
    out = SHAPE(into[0].shape if into else (4, width // 8, 768), bf16)
    spec = pl.BlockSpec((4, width // 8, 384), lambda i: (0, 0, first + i))
    into = list(into or [])
    return pl.pallas_call(
        functools.partial(bwd_kernel, 512, len(into) + len(pins)),
        grid=(2,),
        in_specs=[
            SMEM,
            SMEM,
            pl.BlockSpec((2, rows, 128), lambda i: (i, 0, 0)),
            col,
            col,
            col,
            pl.BlockSpec((rows, 128), lambda i: (0, 2 * g + i)),
        ]
        + [ANY] * (1 + len(into) + len(pins)),
        input_output_aliases={8 + i: 3 + i for i in range(len(into))},
        out_specs=[col] * 3 + [spec] * 2,
        out_shape=in_hbm([SHAPE((rows, 256), bf16)] * 3) + [out, out],
        scratch_shapes=[pltpu.VMEM((2, rows, 128), bf16)] * 3
        + [
            pltpu.VMEM((rows, 128), f32),
            pltpu.VMEM((width, 384), bf16),
            pltpu.VMEM((width, rows), bf16),
            pltpu.SemaphoreType.DMA((1,)),
        ],
        compiler_params=params(VMEM_MIB),
        cost_estimate=cost(14, 8),
        name=f"attn_bwd_{g}",
    )(bucket, me, *far(qe, k, v, att, gatt, n1t), *into, *pins)


def tail_kernel(n_pins, x_ref, *refs):
    ds = refs[:9]
    w_ref, gmid_ref, norm_ref, g2_ref = refs[9:13]
    tg_ref, gg_ref = refs[13 + n_pins :]

    @pl.when(pl.program_id(0) == 0)
    def _():
        gg_ref[...] = jnp.zeros_like(gg_ref)
        gg_ref[2:4, :] = g2_ref[0:2, :]

    d = jnp.concatenate([ds[3 * g + j][...] for j in range(3) for g in range(3)], axis=1)
    dx, dg, db = ln_back(nt(d, w_ref[...]), x_ref[...].astype(f32), norm_ref[0:1, :])
    tg_ref[...] = (gmid_ref[...] + dx).astype(bf16)
    gg_ref[0:1, :] += dg
    gg_ref[1:2, :] += db


def tail_bwd(x, ds, w, gmid, norms, g2, pins, rb=256):
    rows, width = x.shape
    row = lambda n: pl.BlockSpec((rb, n), lambda i: (i, 0))
    full = lambda *s: pl.BlockSpec(s, lambda i: (0,) * len(s))
    once = lambda *s: pl.BlockSpec(s, lambda i: (0,) * len(s), pipeline_mode=pl.Buffered(1))
    return pl.pallas_call(
        functools.partial(tail_kernel, len(pins)),
        grid=(rows // rb,),
        in_specs=[row(width)] + [row(256)] * 9 + [VMEM, row(width), full(16, width), full(8, width)] + [ANY] * len(pins),
        out_specs=[row(width), full(8, width)],
        out_shape=in_hbm([SHAPE((rows, width), bf16), SHAPE((8, width), f32)]),
        compiler_params=params(VMEM_MIB),
        cost_estimate=cost(5, 16),
        name="tail_bwd",
    )(*far(x, *ds), w, *far(gmid, norms, g2), *pins)


def mixed_kernel(n_pins, mid_ref, act_ref, wd_ref, *refs):
    refs[n_pins][...] = (mid_ref[...] + nn(act_ref[...], wd_ref[...])).astype(bf16)


def mixed_out(mid, act, wd, pins, rb=256):
    rows, width = mid.shape
    hidden = act.shape[1]
    row = lambda n: pl.BlockSpec((rb, n), lambda i: (i, 0))
    once = pl.BlockSpec((hidden, width), lambda i: (0, 0), pipeline_mode=pl.Buffered(1))
    return pl.pallas_call(
        functools.partial(mixed_kernel, len(pins)),
        grid=(rows // rb,),
        in_specs=[row(width), row(hidden), VMEM] + [ANY] * len(pins),
        out_specs=row(width),
        out_shape=in_hbm([SHAPE((rows, width), bf16)])[0],
        compiler_params=params(VMEM_MIB),
        cost_estimate=cost(5, 16),
        name="mixed_out",
    )(*far(mid, act), wd, *pins)


def packet_kernel(n_in, *refs):
    ins, out_ref = refs[:n_in], refs[-1]
    col = 0
    for v in ins:
        out_ref[:, col : col + v.shape[1]] = v[...]
        col += v.shape[1]


def packet(arrays, pins, name):
    rows, cols = arrays[0].shape[0], sum(a.shape[1] for a in arrays)
    full = lambda *s: pl.BlockSpec(s, lambda i: (0,) * len(s))
    return pl.pallas_call(
        functools.partial(packet_kernel, len(arrays)),
        grid=(1,),
        in_specs=[full(*a.shape) for a in arrays] + [ANY] * len(pins),
        out_specs=full(rows, cols),
        out_shape=SHAPE((rows, cols), bf16),
        compiler_params=params(8),
        cost_estimate=cost(0, 2),
        name=name,
    )(*arrays, *pins)


def gate(arrays, pins):
    n = len(arrays)
    if not pins:
        return list(arrays)
    return list(pl.pallas_call(
        lambda *refs: None,
        in_specs=[ANY] * (n + len(pins)),
        out_specs=[ANY] * n,
        out_shape=[SHAPE(a.shape, a.dtype) for a in arrays],
        input_output_aliases={i: i for i in range(n)},
        compiler_params=params(1),
        cost_estimate=cost(0, 0),
        name="gate",
    )(*arrays, *pins))


def total(*vs):
    out = vs[0].astype(f32)
    for v in vs[1:]:
        out = out + v.astype(f32)
    return out.astype(bf16)


def combine_kernel(plan, n_in, n_pins, odd_ref, *refs):
    outs = refs[n_in + n_pins :]
    odd = odd_ref[0] == 1
    at = 0
    for f, spots, n_out in plan:
        values = f(odd, *[refs[i] for i in spots])
        for v in values:
            outs[at][...] = v.astype(outs[at].dtype)
            at += 1


def combine(jobs, odd, pins, name, grid=1):
    arrays, shapes, plan = [], [], []
    for f, ins, outs in jobs:
        spots = []
        for a in ins:
            known = [i for i, b in enumerate(arrays) if b is a]
            spots.append(known[0] if known else len(arrays))
            if not known:
                arrays.append(a)
        plan.append((f, spots, len(outs)))
        shapes += [o if isinstance(o, SHAPE) else SHAPE(o, bf16) for o in outs]
    block = lambda s: pl.BlockSpec(s[:-1] + (s[-1] // grid,), lambda i: (0,) * (len(s) - 1) + (i,))
    sums = pl.pallas_call(
        functools.partial(combine_kernel, plan, len(arrays), len(pins)),
        grid=(grid,),
        in_specs=[SMEM] + [block(a.shape) for a in arrays] + [ANY] * len(pins),
        out_specs=[block(s.shape) for s in shapes],
        out_shape=shapes,
        compiler_params=params(24),
        cost_estimate=cost(0, 4),
        name=name,
    )(odd, *arrays, *pins)
    return list(sums)


def swap(v, axis, size, m):
    return lax.ppermute(v, axis, [(i, i ^ m) for i in range(size)])


def part_plan(cut):
    return [(0, 0), (1, 0), (2, 0), (4, 0), (6, 0), (6, cut), (3, 0), (5, 0), (7, 0), (7, cut)]


class Gather:
    def __init__(self, own, cut, size):
        self.own, self.cut, self.size = own, cut, size

    def near(self):
        self.rx, self.ry = (swap(self.own, "fsdp", self.size, m) for m in (2, 4))
        return [self.rx, self.ry]

    def halves(self):
        n, cols = self.own.shape
        return (
            lambda odd, x, y: (y[: self.cut, :], x[self.cut :, :]),
            [self.rx, self.ry],
            [(self.cut, cols), (n - self.cut, cols)],
        )

    def opposite(self, to_x, to_y):
        self.da, self.db = swap(to_x, "fsdp", self.size, 2), swap(to_y, "fsdp", self.size, 4)
        return [self.da, self.db]

    def core_near(self):
        self.rc, *self.near_c = [swap(v, "fsdp", self.size, 1) for v in (self.own, self.rx, self.ry)]

    def parts(self):
        opp = [self.da, self.db]
        return [self.own, self.rc, self.rx, self.ry] + opp + self.near_c + [swap(v, "fsdp", self.size, 1) for v in opp]


class Chain:
    def __init__(self, packets, plan, n_fsdp, n_rep):
        self.mine, self.got = [], []
        self.plan = ("core",) + plan
        self.at = 0
        self.f = lambda v, m: swap(v, "fsdp", n_fsdp, m)
        self.z = lambda v, m: swap(v, "rep", n_rep, m)
        self.join(packets)

    def join(self, packets):
        keep, send = packets
        self.mine.append(keep)
        self.got.append(self.f(send, 1))
        self.shape = (keep.shape[1], sum(k.shape[2] for k in self.mine))

    def job(self):
        done = self.plan[self.at]
        then = self.plan[self.at + 1] if self.at + 1 < len(self.plan) else None
        rows, cols = self.shape
        h = rows // 2
        whole, half = (rows, cols), (h, cols)
        if done == "core" and then == "xy":

            def f(odd, *vs):
                n = len(vs) // 2
                pairs = list(zip(vs[:n], vs[n:]))
                return tuple(jnp.concatenate([total(k[s], g[s]) for k, g in pairs], axis=1) for s in range(4))

            return f, self.mine + self.got, [whole] * 4
        if done == "core":

            def f(odd, k, g):
                part = lambda s, t, lo: jnp.stack([total(k[i, lo : lo + h, :], g[i, lo : lo + h, :]) for i in (s, t)])
                return part(0, 2, 0), part(0, 1, h), part(1, 3, 0), part(2, 3, h)

            return f, self.mine + self.got, [(2,) + half] * 4
        if done == "a":
            f = lambda odd, a, b, ra, rb: (total(a[0], ra[0]), total(b[0], rb[0]), total(a[1], ra[1]), total(b[1], rb[1]))
            return f, self.mine + self.got, [half] * 4
        if done in ("b", "xy"):

            def f(odd, *vs):
                if done == "b":
                    a, b, ra, rb = vs
                    lo, hi = total(a[...], ra[...]), total(b[...], rb[...])
                else:
                    lo, hi = (total(*[v[r, :] for v in vs]) for r in (slice(0, h), slice(h, rows)))
                if then == "p1":
                    return (jnp.concatenate([lo, hi], axis=0),)
                return jnp.where(odd, hi, lo), jnp.where(odd, lo, hi)

            return f, self.mine + self.got, [whole] if then == "p1" else [half] * 2
        if done == "h3":

            def f(odd, p, o):
                p, o = p[...], o[...]
                return (jnp.concatenate([jnp.where(odd, o, p), jnp.where(odd, p, o)], axis=0),)

            return f, self.mine + self.got, [SHAPE(whole, f32)]
        out = half if done[0] == "h" else whole
        return (lambda odd, a, b: (total(a[...], b[...]),)), self.mine + self.got, [out if then else SHAPE(out, f32)]

    def go(self, sums):
        self.at += 1
        step = self.plan[self.at] if self.at < len(self.plan) else None
        if step == "xy":
            self.mine, out = sums[:1], sums[1:]
            self.got = [self.f(v, m) for v, m in zip(out, (2, 4, 6))]
        elif step in ("a", "b"):
            self.mine, out = sums[:2], sums[2:]
            self.got = [self.f(v, m) for v, m in zip(out, (2, 4) if step == "a" else (4, 2))]
        elif step == "h1":
            self.mine, self.got = sums[:1], [self.z(sums[1], 1)]
        else:
            self.mine = sums
            self.got = [self.z(sums[0], 2 if step in ("h2", "p2") else 1)] if step else []


def advance(chains, extra, odd, pins, name, grid=1):
    jobs = [c.job() for c in chains] + extra
    sums = combine(jobs, odd, pins, name, grid)
    at = 0
    for c, job in zip(chains, jobs):
        c.go(sums[at : at + len(job[2])])
        at += len(job[2])
    return sums, sums[at:]


def natural(v, width):
    pairs = width // LANES
    return jnp.concatenate([v[:, LANES * (3 * p + j) :][:, :LANES] for j in range(3) for p in range(pairs)], axis=1)


def last_job(cq, cr):
    rows, cols = cq.shape
    width = cr.shape[1]

    def f(odd, p, o, a, b):
        p, o = p[...], o[...]
        q = jnp.concatenate([jnp.where(odd, o, p), jnp.where(odd, p, o)], axis=0)
        return q[:, :width], natural(jnp.concatenate([q[:, width:], total(a[...], b[...])], axis=1), width)

    return f, cq.mine + cq.got + cr.mine + cr.got, [SHAPE((rows, width), f32), SHAPE((rows, cols), f32)]


def sum_chips(v, size):
    x, y, d = (swap(v, "fsdp", size, m) for m in (2, 4, 6))
    return (v + x) + (y + d)


def sum_replicas(v, size):
    a, b, c = (swap(v, "rep", size, m) for m in (1, 2, 3))
    return (v + a) + (b + c)


def whole(keep, send):
    return jnp.stack([keep, send], axis=1).reshape(-1, keep.shape[2])


def shards(
    n_fsdp, n_rep, tokens, bucket, ln1_gain, ln1_bias, w_qkv, w_out, ln2_gain, ln2_bias, w_up, w_down, cotangent
):
    width = tokens.shape[1]
    fast = n_fsdp == 8 and n_rep == 4
    index = lax.axis_index("fsdp")
    vectors = jnp.stack([ln1_gain, ln1_bias, ln2_gain, ln2_bias])
    if fast:
        me = jnp.reshape(index, (1,)).astype(jnp.int32)
        owner = lax.broadcasted_iota(jnp.int32, (4, width), 1) // (width // 8)
        spread = jnp.where(owner == index, jnp.tile(vectors, (1, 8)), 0)
    else:
        me = jnp.zeros((1,), jnp.int32)
        spread = lax.all_gather(vectors, "fsdp", axis=1, tiled=True)
        w_qkv, w_out, w_up, w_down = (
            lax.all_gather(w, "fsdp", axis=0, tiled=True) for w in (w_qkv, w_out, w_up, w_down)
        )
    local = w_qkv.shape[0]
    norm_rows = jnp.pad(spread, ((0, 12), (0, w_qkv.shape[1] - width)))
    packet_q = jnp.concatenate([w_qkv, norm_rows], axis=0)
    cut, cut_d = local // 2, w_down.shape[0] // 2
    none = [(0, 0)]
    odd = jnp.reshape(lax.axis_index("rep") & 1, (1,)).astype(jnp.int32)

    if fast:
        gq = Gather(packet_q, cut, n_fsdp)
        gq.near()
        far_q = gq.opposite(gq.ry[:cut], gq.rx[cut:])
        gq.core_near()
        (own_u,) = gate([packet([w_out, w_up], [], "packet_up")], far_q + [gq.rc] + gq.near_c)
        gu = Gather(own_u, cut, n_fsdp)
        near_u = gu.near()
        gd = Gather(None, cut_d, n_fsdp)
        plan, plan_d = part_plan(cut), part_plan(cut_d)
        parts_q = gq.parts()
    else:
        plan, plan_d = none, none
        parts_q = [packet_q]

    def pin(v):
        return list(v) if fast else []

    n1, n1t, norms, w_full, *heads0 = forward_first(
        bucket, me, tokens, parts_q, plan, local, pin([own_u] if fast else [])
    )
    sums = []
    if fast:
        sums, (to_x, to_y, own_d) = advance(
            [], [gu.halves(), (lambda o, w: (w[...],), far(w_down), [w_down.shape])], odd, far(n1t), "after_a"
        )
        gu.opposite(to_x, to_y)
        gu.rx, gu.ry = gate([gu.rx, gu.ry], far(n1t))
        (gu.own,) = gate([gu.own], far(n1t))
        gu.core_near()
    heads1 = forward_next(1, bucket, n1, w_full, pin(sums))
    sums = []
    if fast:
        gu.da, gu.db, gd.own, gu.rc, *gu.near_c = gate([gu.da, gu.db, own_d, gu.rc] + gu.near_c, far(heads1[3]))
        sums = [gd.own]
        gd.near()
        parts_u = gu.parts()
    heads2 = forward_next(2, bucket, n1, w_full, pin(sums))
    heads = [heads0, heads1, heads2]
    atts = [h[3] for h in heads]
    if fast:
        sums, (to_x, to_y) = advance([], [gd.halves()], odd, far(heads2[3]), "after_c")
        gd.opposite(to_x, to_y)
        gd.core_near()
    else:
        parts_u = [packet([w_out, w_up], [], "packet_up")]
    mid, n2t, act, gp, w_ou = up_proj(me, tokens, atts, norms, parts_u, plan, local, pin(sums))
    if fast:
        gd.da, gd.db = gate([gd.da, gd.db], far(n2t))
        parts_d = gd.parts()
    else:
        parts_d = [w_down]
    send_d = wdown_grad(me, act, cotangent, 1, pin([gd.da, gd.db] if fast else []))
    halves, direct = ("a", "b", "h1", "h2", "h3"), ("xy", "p1", "p2")
    chain = lambda pk, plan: Chain(pk, plan, n_fsdp, n_rep) if fast else None

    def step(chains, after, name):
        return advance(chains, [], odd, after, name)[0][-1:] if fast else []

    if fast:
        (send_d,) = gate([send_d], parts_d)
    pk_d = [wdown_grad(me, act, cotangent, 0, pin([send_d])), send_d]
    cd = chain(pk_d, halves)
    sums = step([cd], [], "after_wdown")
    gup, *pk_u, w_dn = hidden_bwd(me, cotangent, gp, n2t, parts_d, plan_d, w_down.shape[0], pin(sums))
    sums = step([cd], far(gup), "after_hidden")
    if fast:
        pk_u = [pk_u[0]] + gate([pk_u[1]], sums)
    cu = chain(pk_u, halves)
    gmid, gatt, g_norm2, *pk_q = mid_bwd(me, cotangent, gup, mid, norms, w_ou, atts, pin(sums))
    sums = step([cd, cu], far(g_norm2), "after_mid")
    *d0, k, s = attn_bwd(0, bucket, me, heads[0], gatt, n1t, pk_q, 2, pin(sums))
    sums = step([cd, cu], far(d0[0]), "after_bwd0")
    pk_q = [k] + (gate([s], sums) if fast else [s])
    cq = chain(pk_q, ("xy", "h1", "h2", "h3"))
    *d1, k, s = attn_bwd(1, bucket, me, heads[1], gatt, n1t, None, 0, pin(sums))
    s0 = step([cd, cu], far(d1[0]), "after_bwd1")
    pk_1 = [k] + (gate([s], s0) if fast else [s])
    if fast:
        cq.join(pk_1)
    sums = step([cq], s0, "after_bwd1_q")
    *d2, k, s = attn_bwd(2, bucket, me, heads[2], gatt, n1t, None, 0, pin(s0 + sums))
    s0 = step([cd, cu, cq], far(d2[0]), "after_bwd2")
    pk_r = [k] + (gate([s], s0) if fast else [s])
    cr = chain(pk_r, direct)
    sums = step([cr], s0, "after_bwd2_r")
    tokens_grad, g_norm1 = tail_bwd(tokens, d0 + d1 + d2, w_full, gmid, norms, g_norm2, pin(s0 + sums))
    sums = step([cu, cq, cr], far(g_norm1), "after_tail")
    g_norms = g_norm1
    if fast:
        (g_norms,) = gate([g_norms], sums)
        g_norms_c = swap(g_norms, "fsdp", n_fsdp, 1)
    mixed = mixed_out(mid, act, w_dn, pin(sums))
    sums = step([cu, cq, cr], far(mixed), "after_mixed")
    if fast:
        (g_norms,) = gate([g_norms], sums)
        g_norms = sum_chips(g_norms + g_norms_c, n_fsdp)
    if fast:
        (g_norms,) = gate([g_norms], cq.got)
        g_norms = sum_replicas(g_norms, n_rep)
    if fast:
        gw_out, gw_q = combine([last_job(cq, cr)], odd, [], "last")

    if fast:
        (rows_d,), (rows_u,) = (c.mine for c in (cd, cu))
    else:
        g_norms = lax.psum(g_norms, ("fsdp", "rep"))
        rows_q, rows_1, rows_r, rows_u, rows_d = (whole(*pk) for pk in (pk_q, pk_1, pk_r, pk_u, pk_d))
        rows_q = jnp.concatenate([rows_q, rows_1], axis=1)
        gw_out = rows_q[:, :width]
        gw_q = natural(jnp.concatenate([rows_q[:, width:], rows_r], axis=1), width)
    g_norms = lax.dynamic_slice_in_dim(g_norms, index * (width // n_fsdp), width // n_fsdp, axis=1)
    grads = (gw_q, gw_out, rows_u, rows_d)
    if not fast:
        grads = tuple(
            lax.psum(lax.psum_scatter(g, "fsdp", scatter_dimension=0, tiled=True), "rep") for g in grads
        )
    gw_qkv, gw_out, gw_up, gw_down = (g.astype(f32) for g in grads)
    return (
        mixed,
        tokens_grad,
        g_norms[0],
        g_norms[1],
        gw_qkv,
        gw_out,
        g_norms[2],
        g_norms[3],
        gw_up,
        gw_down,
    )


def solution(mesh):
    return jax.shard_map(
        functools.partial(shards, mesh.shape["fsdp"], mesh.shape["rep"]),
        mesh=mesh,
        in_specs=(
            P(("rep", "fsdp"), None),
            P(("rep", "fsdp")),
            P("fsdp"),
            P("fsdp"),
            P("fsdp", None),
            P("fsdp", None),
            P("fsdp"),
            P("fsdp"),
            P("fsdp", None),
            P("fsdp", None),
            P(("rep", "fsdp"), None),
        ),
        out_specs=(
            P(("rep", "fsdp"), None),
            P(("rep", "fsdp"), None),
            P("fsdp"),
            P("fsdp"),
            P("fsdp", None),
            P("fsdp", None),
            P("fsdp"),
            P("fsdp"),
            P("fsdp", None),
            P("fsdp", None),
        ),
        check_vma=False,
    )
```

```python
import functools

import jax
import jax.numpy as jnp
from jax import lax
from jax.experimental import pallas as pl
from jax.experimental.pallas import tpu as pltpu
from jax.sharding import PartitionSpec as P

HEAD_DIM = 64
SHORT = 256
LN_EPS = 1e-6
LANES = 128
f32 = jnp.float32
bf16 = jnp.bfloat16

LOG2E = 1.4426950408889634
ROOT_2PI = (2 * 3.141592653589793) ** -0.5


def nt(a, b):
    return lax.dot_general(a, b, (((1,), (1,)), ((), ())), preferred_element_type=f32)


def nn(a, b):
    return lax.dot_general(a, b, (((1,), (0,)), ((), ())), preferred_element_type=f32)


def tn(a, b):
    return lax.dot_general(a, b, (((0,), (0,)), ((), ())), preferred_element_type=f32)


def ln_rows(x, gain, bias):
    centred = x - jnp.mean(x, axis=-1, keepdims=True)
    var = jnp.mean(centred * centred, axis=-1, keepdims=True)
    return centred * lax.rsqrt(var + LN_EPS) * gain + bias


def ln_back(grad, v, gain):
    centred = v - jnp.mean(v, axis=-1, keepdims=True)
    r = lax.rsqrt(jnp.mean(centred * centred, axis=-1, keepdims=True) + LN_EPS)
    xh = centred * r
    gg = grad * gain
    dx = r * (gg - jnp.mean(gg, axis=-1, keepdims=True) - xh * jnp.mean(gg * xh, axis=-1, keepdims=True))
    return dx, jnp.sum(grad * xh, axis=0, keepdims=True), jnp.sum(grad, axis=0, keepdims=True)


def gelu_pair(u):
    cdf = 0.5 + 0.5 * lax.erf(u * 2**-0.5)
    density = jnp.exp2((u * u) * (-0.5 * LOG2E))
    return u * cdf, cdf + (u * ROOT_2PI) * density


def terms(v):
    hi = v.astype(bf16).astype(f32)
    r = v - hi
    mid = r.astype(bf16).astype(f32)
    return hi, mid, r - mid


def spread(v, lane):
    hi, mid, lo = terms(-v)
    pos = lane & 63
    return jnp.where(pos == 0, hi, jnp.where(pos == 1, mid, jnp.where(pos == 2, lo, 0.0))).astype(bf16)


def unpack(refs, plan, me, shard_rows, jobs, sem):
    copies = []
    for ref, (r, lo) in zip(refs, plan):
        hi = lo + ref.shape[0]
        for (first, last), cols, dst, step in jobs(shard_rows):
            a, b = max(lo, first), min(hi, last)
            if a >= b:
                continue
            row = pl.multiple_of((me ^ r) * step, 16) + (a - first)
            copies.append(
                pltpu.make_async_copy(
                    ref.at[pl.ds(a - lo, b - a), cols], dst.at[pl.ds(row, b - a), :], sem.at[len(copies)]
                )
            )
    return copies


def run(copies):
    for c in copies:
        c.start()
    for c in copies:
        c.wait()


def put_slots(src_ref, outs, me, cols):
    keep, send = outs
    rows = src_ref.shape[0] // 8
    for r in range(8):
        row = pl.multiple_of((me ^ r) * rows, 16)
        (send if r & 1 else keep)[r >> 1, :, cols] = src_ref[pl.ds(row, rows), :]


def params(mib):
    return pltpu.CompilerParams(vmem_limit_bytes=mib << 20)


def cost(gflops, mib):
    return pl.CostEstimate(flops=1000, bytes_accessed=1024, transcendentals=0)


VMEM_MIB = 44
SMEM = pl.BlockSpec(memory_space=pltpu.SMEM)
VMEM = pl.BlockSpec(memory_space=pltpu.VMEM)
ANY = pl.BlockSpec(memory_space=pl.ANY)
SHAPE = jax.ShapeDtypeStruct


def far(*arrays):
    return [pltpu.with_memory_space_constraint(a, pltpu.HBM) for a in arrays]


def in_hbm(shapes):
    return [pltpu.HBM(s.shape, s.dtype) for s in shapes]


def attend(bucket_ref, qb, n1, wq, wk, wv, qe_ref, k_ref, v_ref, att_ref, vx_ref):
    rows = k_ref.shape[0]
    low = lax.broadcasted_iota(jnp.int32, (rows, 128), 1) < 64
    q = nn(n1, wq)
    k_ref[...] = nn(n1, wk).astype(bf16)
    v = nn(n1, wv)
    v_ref[...] = v.astype(bf16)
    q = q * HEAD_DIM**-0.5
    for p in range(2):
        qp = q[:, 128 * p : 128 * p + 128]
        vp = v[:, 128 * p : 128 * p + 128]
        qe_ref[2 * p] = jnp.where(low, qp, 0.0).astype(bf16)
        qe_ref[2 * p + 1] = jnp.where(low, 0.0, qp).astype(bf16)
        vx_ref[2 * p] = jnp.where(low, vp, 1.0).astype(bf16)
        vx_ref[2 * p + 1] = jnp.where(low, 1.0, vp).astype(bf16)

    def block(r, kr):
        lane = lax.broadcasted_iota(jnp.int32, (r.size, 128), 1)
        lowq = lane < 64
        ss = [nt(qe_ref[h, r, :], k_ref[kr, 128 * (h // 2) : 128 * (h // 2) + 128]) for h in range(4)]
        for p in range(2):
            os, tops = [], []
            for h in (2 * p, 2 * p + 1):
                top = jnp.max(ss[h], axis=-1, keepdims=True)
                e = jnp.exp(ss[h] - top).astype(bf16)
                os.append(nn(e, vx_ref[h, kr, :]))
                tops.append(top)
            sums = jnp.where(lowq, os[1], os[0])
            lse = jnp.where(lowq, tops[1], tops[0]) + jnp.log(sums)
            rest = spread(lse, lane)
            q0, q1 = qe_ref[2 * p, r, :], qe_ref[2 * p + 1, r, :]
            qe_ref[2 * p, r, :] = jnp.where(lowq, q0, rest)
            qe_ref[2 * p + 1, r, :] = jnp.where(lowq, rest, q1)
            att = jnp.where(lowq, os[0], os[1]) / pltpu.roll(sums, 64, 1)
            att_ref[r, 128 * p : 128 * p + 128] = att.astype(bf16)

    is_long = bucket_ref[0] == 1

    @pl.when(is_long)
    def _():
        def body(i, _):
            block(pl.ds(i * qb, qb), slice(None))
            return 0

        lax.fori_loop(0, rows // qb, body, 0)

    @pl.when(jnp.logical_not(is_long))
    def _():
        def body(i, _):
            r = pl.ds(i * SHORT, SHORT)
            block(r, r)
            return 0

        lax.fori_loop(0, rows // SHORT, body, 0)


def q_jobs(w_ref, raw_ref):
    width = w_ref.shape[0]
    return lambda shard: [
        ((0, shard), slice(None), w_ref, shard),
        ((shard, shard + 16), slice(0, width), raw_ref, 16),
    ]


def fwd_first_kernel(plan, shard, n_parts, bucket_ref, me_ref, x_ref, *refs):
    parts = refs[:n_parts]
    n1_ref, n1t_ref, norm_ref, whbm_ref, qe_ref, k_ref, v_ref, att_ref, w_ref, raw_ref, vx_ref, sem = refs[n_parts:]
    rows, width = x_ref.shape
    run(unpack(parts, plan, me_ref[0], shard, q_jobs(w_ref, raw_ref), sem))
    keep = pltpu.make_async_copy(w_ref, whbm_ref, sem.at[0])
    keep.start()
    total = raw_ref[0:16, :].astype(f32)
    for i in range(1, raw_ref.shape[0] // 16):
        total = total + raw_ref[16 * i : 16 * i + 16, :].astype(f32)
    norm_ref[...] = total

    def body(i, _):
        r = pl.ds(i * 128, 128)
        n1_ref[r, :] = ln_rows(x_ref[r, :].astype(f32), norm_ref[0:1, :], norm_ref[1:2, :]).astype(bf16)
        return 0

    lax.fori_loop(0, rows // 128, body, 0)
    n1t_ref[...] = n1_ref[...].T
    w = [w_ref[:, width * i : width * i + 256] for i in range(3)]
    attend(bucket_ref, 256, n1_ref[...], *w, qe_ref, k_ref, v_ref, att_ref, vx_ref)
    keep.wait()


def fwd_next_kernel(n_pins, bucket_ref, n1_ref, wq_ref, wk_ref, wv_ref, *refs):
    attend(bucket_ref, 256, n1_ref[...], wq_ref[...], wk_ref[...], wv_ref[...], *refs[n_pins:])


def head_shapes(rows):
    return [SHAPE((4, rows, 128), bf16)] + [SHAPE((rows, 256), bf16)] * 3


def forward_first(bucket, me, x, parts, plan, shard, pins):
    rows, width = x.shape
    full = lambda *s: pl.BlockSpec(s, lambda i: (0,) * len(s))
    shapes = [
        SHAPE((rows, width), bf16),
        SHAPE((width, rows), bf16),
        SHAPE((16, width), f32),
        SHAPE((width, 3 * width), bf16),
    ] + head_shapes(rows)
    return pl.pallas_call(
        lambda b, m, xr, *refs: fwd_first_kernel(
            plan, shard, len(parts), b, m, xr, *refs[: len(parts)], *refs[len(parts) + len(pins) :]
        ),
        grid=(1,),
        in_specs=[SMEM, SMEM, full(rows, width)] + [ANY] * (len(parts) + len(pins)),
        out_specs=[full(*s.shape) for s in shapes[:3]] + [ANY] + [full(*s.shape) for s in shapes[4:]],
        out_shape=in_hbm(shapes),
        scratch_shapes=[
            pltpu.VMEM((width, 3 * width), bf16),
            pltpu.VMEM((width // shard * 16, width), bf16),
            pltpu.VMEM((4, rows, 128), bf16),
            pltpu.SemaphoreType.DMA((32,)),
        ],
        compiler_params=params(VMEM_MIB),
        cost_estimate=cost(8, 12),
        name="fwd_a",
    )(bucket, me, *far(x, *parts), *pins)


def forward_next(g, bucket, n1, w, pins):
    rows, width = n1.shape
    groups = width // 256
    col = lambda j: pl.BlockSpec((width, 256), lambda i: (0, j * groups + g))
    full = lambda *s: pl.BlockSpec(s, lambda i: (0,) * len(s))
    shapes = head_shapes(rows)
    return pl.pallas_call(
        functools.partial(fwd_next_kernel, len(pins)),
        grid=(1,),
        in_specs=[SMEM, full(rows, width), col(0), col(1), col(2)] + [ANY] * len(pins),
        out_specs=[full(*s.shape) for s in shapes],
        out_shape=in_hbm(shapes),
        scratch_shapes=[pltpu.VMEM((4, rows, 128), bf16)],
        compiler_params=params(VMEM_MIB),
        cost_estimate=cost(8, 8),
        name=f"attn_{g}",
    )(bucket, *far(n1, w, w, w), *pins)


UPN = 512
HIDN = 512


def up_kernel(plan, shard, n_parts, me_ref, x_ref, a0, a1, a2, norm_ref, *refs):
    parts = refs[:n_parts]
    mid_ref, n2t_ref, act_ref, gp_ref, wou_hbm, wo_ref, wu_ref, sem, sem2 = refs[n_parts:]
    width = x_ref.shape[1]
    saves = [
        pltpu.make_async_copy(wo_ref, wou_hbm.at[:, :width], sem2.at[0]),
        pltpu.make_async_copy(wu_ref, wou_hbm.at[:, width:], sem2.at[1]),
    ]

    @pl.when(pl.program_id(0) == 0)
    def _():
        jobs = lambda s: [
            ((0, s), slice(0, width), wo_ref, s),
            ((0, s), slice(width, None), wu_ref, s),
        ]
        run(unpack(parts, plan, me_ref[0], shard, jobs, sem))
        for c in saves:
            c.start()

    att = jnp.concatenate([a0[...], a1[...], a2[...]], axis=1)
    mid = x_ref[...].astype(f32) + nn(att, wo_ref[...])
    mid_ref[...] = mid
    n2 = ln_rows(mid, norm_ref[2:3, :], norm_ref[3:4, :]).astype(bf16)
    n2t_ref[...] = n2.T
    for b in range(wu_ref.shape[1] // UPN):
        c = slice(UPN * b, UPN * b + UPN)
        act, gp = gelu_pair(nn(n2, wu_ref[:, c]))
        act_ref[:, c] = act.astype(bf16)
        gp_ref[:, c] = gp.astype(bf16)

    @pl.when(pl.program_id(0) == pl.num_programs(0) - 1)
    def _():
        for c in saves:
            c.wait()


def up_proj(me, x, atts, norms, parts, plan, shard, pins, rb=256):
    rows, width = x.shape
    hidden = parts[0].shape[1] - width
    row = lambda n: pl.BlockSpec((rb, n), lambda i: (i, 0))
    full = lambda *s: pl.BlockSpec(s, lambda i: (0,) * len(s))
    n = len(parts)
    return pl.pallas_call(
        lambda m, xr, a0, a1, a2, nr, *refs: up_kernel(
            plan, shard, n, m, xr, a0, a1, a2, nr, *refs[:n], *refs[n + len(pins) :]
        ),
        grid=(rows // rb,),
        in_specs=[SMEM, row(width)] + [row(256)] * 3 + [full(16, width)] + [ANY] * (n + len(pins)),
        out_specs=[row(width), pl.BlockSpec((width, rb), lambda i: (0, i)), row(hidden), row(hidden), ANY],
        out_shape=in_hbm([
            SHAPE((rows, width), f32),
            SHAPE((width, rows), bf16),
            SHAPE((rows, hidden), bf16),
            SHAPE((rows, hidden), bf16),
            SHAPE((width, width + hidden), bf16),
        ]),
        scratch_shapes=[
            pltpu.VMEM((width, width), bf16),
            pltpu.VMEM((width, hidden), bf16),
            pltpu.SemaphoreType.DMA((32,)),
            pltpu.SemaphoreType.DMA((2,)),
        ],
        compiler_params=params(VMEM_MIB),
        cost_estimate=cost(9, 20),
        name="up_proj",
    )(me, *far(x, *atts, norms), *parts, *pins)


def wdown_kernel(n_pins, me_ref, act_ref, dy_ref, *refs):
    refs[n_pins][0] = tn(act_ref[...], dy_ref[...]).astype(bf16)


def wdown_grad(me, act, dy, core, pins):
    rows, width = dy.shape
    shard = act.shape[1] // 8
    return pl.pallas_call(
        functools.partial(wdown_kernel, len(pins)),
        grid_spec=pltpu.PrefetchScalarGridSpec(
            num_scalar_prefetch=1,
            grid=(4,),
            in_specs=[
                pl.BlockSpec((rows, shard), lambda i, m: (0, m[0] ^ (2 * i + core))),
                VMEM,
            ]
            + [ANY] * len(pins),
            out_specs=pl.BlockSpec((1, shard, width), lambda i, m: (i, 0, 0)),
        ),
        out_shape=SHAPE((4, shard, width), bf16),
        compiler_params=params(VMEM_MIB),
        cost_estimate=cost(5, 13),
        name=f"wdown_{core}",
    )(me, *far(act), dy, *pins)


def hidden_kernel(plan, shard, n_parts, me_ref, dy_ref, gp_ref, n2t_ref, *refs):
    parts = refs[:n_parts]
    gup_ref, keep_ref, send_ref, wd_hbm, wd_ref, g_ref, sem, sem2 = refs[n_parts:]
    i = pl.program_id(0)
    save = pltpu.make_async_copy(wd_ref, wd_hbm, sem2.at[0])

    @pl.when(i == 0)
    def _():
        run(unpack(parts, plan, me_ref[0], shard, lambda s: [((0, s), slice(None), wd_ref, s)], sem))
        save.start()

    fb = gp_ref.shape[1]
    for b in range(fb // HIDN):
        c = slice(HIDN * b, HIDN * b + HIDN)
        w = wd_ref[pl.ds(pl.multiple_of(i * fb, 256) + HIDN * b, HIDN), :]
        gup_ref[:, c] = (nt(dy_ref[...], w) * gp_ref[:, c].astype(f32)).astype(bf16)
        g_ref[:, c] = nn(n2t_ref[...], gup_ref[:, c]).astype(bf16)
    put_slots(g_ref, (keep_ref, send_ref), me_ref[0], slice(None))

    @pl.when(i == pl.num_programs(0) - 1)
    def _():
        save.wait()


def hidden_bwd(me, dy, gp, n2t, parts, plan, shard, pins, fb=512):
    rows, width = dy.shape
    hidden = gp.shape[1]
    full = lambda *s: pl.BlockSpec(s, lambda i: (0,) * len(s))
    col = pl.BlockSpec((rows, fb), lambda i: (0, i))
    out = SHAPE((4, width // 8, hidden), bf16)
    spec = pl.BlockSpec((4, width // 8, fb), lambda i: (0, 0, i))
    n = len(parts)
    return pl.pallas_call(
        lambda m, a, b, c, *refs: hidden_kernel(plan, shard, n, m, a, b, c, *refs[:n], *refs[n + len(pins) :]),
        grid=(hidden // fb,),
        in_specs=[SMEM, VMEM, col, full(width, rows)] + [ANY] * (n + len(pins)),
        out_specs=[col, spec, spec, ANY],
        out_shape=in_hbm([SHAPE((rows, hidden), bf16)]) + [out, out] + in_hbm([SHAPE((hidden, width), bf16)]),
        scratch_shapes=[
            pltpu.VMEM((hidden, width), bf16),
            pltpu.VMEM((width, fb), bf16),
            pltpu.SemaphoreType.DMA((32,)),
            pltpu.SemaphoreType.DMA((1,)),
        ],
        compiler_params=params(VMEM_MIB),
        cost_estimate=cost(10, 26),
        name="hidden_bwd",
    )(me, dy, *far(gp, n2t), *parts, *pins)


def mid_kernel(n_pins, me_ref, dy_ref, gup_ref, mid_ref, norm_ref, wou_ref, a0, a1, a2, *refs):
    gmid_ref, gatt_ref, gg_ref, keep_ref, send_ref, gmb_ref, g_ref = refs[n_pins:]
    rb, width = dy_ref.shape
    i = pl.program_id(0)

    @pl.when(i == 0)
    def _():
        gg_ref[...] = jnp.zeros_like(gg_ref)

    gn2 = nt(gup_ref[...], wou_ref[:, width:])
    dx, dg, db = ln_back(gn2, mid_ref[...], norm_ref[2:3, :])
    gm = dy_ref[...].astype(f32) + dx
    gmid_ref[...] = gm
    gmb = gm.astype(bf16)
    gmb_ref[pl.ds(pl.multiple_of(i * rb, rb), rb), :] = gmb
    gg_ref[0:1, :] += dg
    gg_ref[1:2, :] += db
    gatt_ref[...] = nt(gmb, wou_ref[:, :width]).astype(bf16)

    @pl.when(i == pl.num_programs(0) - 1)
    def _():
        for j, a in enumerate((a0, a1, a2)):
            g_ref[256 * j : 256 * j + 256, :] = tn(a[...], gmb_ref[...]).astype(bf16)
        put_slots(g_ref, (keep_ref, send_ref), me_ref[0], slice(None))


def mid_bwd(me, dy, gup, mid, norms, wou, atts, pins, rb=256):
    rows, width = dy.shape
    hidden = gup.shape[1]
    row = lambda n: pl.BlockSpec((rb, n), lambda i: (i, 0))
    full = lambda *s: pl.BlockSpec(s, lambda i: (0,) * len(s))
    once = lambda *s: pl.BlockSpec(s, lambda i: (0,) * len(s), pipeline_mode=pl.Buffered(1))
    out = SHAPE((4, width // 8, 2 * width), bf16)
    spec = pl.BlockSpec((4, width // 8, width), lambda i: (0, 0, 0))
    return pl.pallas_call(
        functools.partial(mid_kernel, len(pins)),
        grid=(rows // rb,),
        in_specs=[SMEM, row(width), row(hidden), row(width), full(16, width), VMEM]
        + [full(rows, 256)] * 3
        + [ANY] * len(pins),
        out_specs=[row(width), row(width), full(8, width), spec, spec],
        out_shape=in_hbm([SHAPE((rows, width), f32), SHAPE((rows, width), bf16), SHAPE((8, width), f32)]) + [out, out],
        scratch_shapes=[pltpu.VMEM((rows, width), bf16), pltpu.VMEM((width, width), bf16)],
        compiler_params=params(VMEM_MIB),
        cost_estimate=cost(8, 24),
        name="mid_bwd",
    )(me, *far(dy, gup, mid, norms), wou, *far(*atts), *pins)


def bwd_kernel(kb, n_pins, bucket_ref, me_ref, qe_ref, k_ref, v_ref, att_ref, do_ref, n1t_hbm, *refs):
    dq_ref, dk_ref, dv_ref, keep_ref, send_ref, doe_ref, ke_ref, ve_ref, dqa_ref, g_ref, n1t_ref, sem = refs[n_pins:]
    rows = k_ref.shape[0]
    load = pltpu.make_async_copy(n1t_hbm, n1t_ref, sem.at[0])

    @pl.when(pl.program_id(0) == 0)
    def _():
        load.start()

    lane = lax.broadcasted_iota(jnp.int32, (rows, 128), 1)
    low = lane < 64
    do, k, v = do_ref[...], k_ref[...], v_ref[...]
    across = lambda i: lax.broadcasted_iota(jnp.int32, (128, 128), i) // 64
    other = jnp.where(across(0) + across(1) == 1, 1.0, 0.0).astype(bf16)
    d = sum(nn(t.astype(bf16), other) for t in terms(do.astype(f32) * att_ref[...].astype(f32)))
    rest = spread(d, lane)
    ones = jnp.where((lane & 63) < 3, 1.0, 0.0).astype(bf16)
    for j in range(2):
        own = low if j == 0 else ~low
        doe_ref[j] = jnp.where(own, do, rest)
        ke_ref[j] = jnp.where(own, k, ones)
        ve_ref[j] = jnp.where(own, v, ones)

    def block(kr, qr):
        lowk = lax.broadcasted_iota(jnp.int32, (kr.size, 128), 1) < 64
        dks, dvs, dqs = [], [], []
        sts = [nt(ke_ref[j, kr, :], qe_ref[j, qr, :]) for j in range(2)]
        dpts = [nt(ve_ref[j, kr, :], doe_ref[j, qr, :]) for j in range(2)]
        for j in range(2):
            pt = jnp.exp(sts[j])
            ds = (pt * dpts[j]).astype(bf16)
            dvs.append(nn(pt.astype(bf16), do_ref[qr, :]))
            dks.append(nn(ds, qe_ref[j, qr, :]))
            dqs.append(tn(k_ref[kr, :], ds).T)
        dk_ref[kr, :] = jnp.where(lowk, dks[0], dks[1]).astype(bf16)
        dv_ref[kr, :] = jnp.where(lowk, dvs[0], dvs[1]).astype(bf16)
        return dqs

    is_long = bucket_ref[0] == 1

    @pl.when(is_long)
    def _():
        if kb == rows:
            dqs = block(pl.ds(0, rows), slice(None))
            dq_ref[...] = (jnp.where(low, dqs[0], dqs[1]) * HEAD_DIM**-0.5).astype(bf16)
            return
        dqa_ref[...] = jnp.zeros_like(dqa_ref)

        def body(i, _):
            dqs = block(pl.ds(i * kb, kb), slice(None))
            dqa_ref[...] += jnp.where(low, dqs[0], dqs[1])
            return 0

        lax.fori_loop(0, rows // kb, body, 0)
        dq_ref[...] = (dqa_ref[...] * HEAD_DIM**-0.5).astype(bf16)

    @pl.when(jnp.logical_not(is_long))
    def _():
        lows = lax.broadcasted_iota(jnp.int32, (SHORT, 128), 1) < 64

        def body(i, _):
            r = pl.ds(i * SHORT, SHORT)
            dqs = block(r, r)
            dq_ref[r, :] = (jnp.where(lows, dqs[0], dqs[1]) * HEAD_DIM**-0.5).astype(bf16)
            return 0

        lax.fori_loop(0, rows // SHORT, body, 0)

    @pl.when(pl.program_id(0) == 0)
    def _():
        load.wait()

    g_ref[...] = nn(n1t_ref[...], jnp.concatenate([dq_ref[...], dk_ref[...], dv_ref[...]], axis=1)).astype(bf16)
    put_slots(g_ref, (keep_ref, send_ref), me_ref[0], slice(None))


def attn_bwd(g, bucket, me, heads, gatt, n1t, into, first, pins):
    qe, k, v, att = heads
    rows = k.shape[0]
    width = n1t.shape[0]
    col = pl.BlockSpec((rows, 128), lambda i: (0, i))
    out = SHAPE(into[0].shape if into else (4, width // 8, 768), bf16)
    spec = pl.BlockSpec((4, width // 8, 384), lambda i: (0, 0, first + i))
    into = list(into or [])
    return pl.pallas_call(
        functools.partial(bwd_kernel, 512, len(into) + len(pins)),
        grid=(2,),
        in_specs=[
            SMEM,
            SMEM,
            pl.BlockSpec((2, rows, 128), lambda i: (i, 0, 0)),
            col,
            col,
            col,
            pl.BlockSpec((rows, 128), lambda i: (0, 2 * g + i)),
        ]
        + [ANY] * (1 + len(into) + len(pins)),
        input_output_aliases={8 + i: 3 + i for i in range(len(into))},
        out_specs=[col] * 3 + [spec] * 2,
        out_shape=in_hbm([SHAPE((rows, 256), bf16)] * 3) + [out, out],
        scratch_shapes=[pltpu.VMEM((2, rows, 128), bf16)] * 3
        + [
            pltpu.VMEM((rows, 128), f32),
            pltpu.VMEM((width, 384), bf16),
            pltpu.VMEM((width, rows), bf16),
            pltpu.SemaphoreType.DMA((1,)),
        ],
        compiler_params=params(VMEM_MIB),
        cost_estimate=cost(14, 8),
        name=f"attn_bwd_{g}",
    )(bucket, me, *far(qe, k, v, att, gatt, n1t), *into, *pins)


def tail_kernel(n_pins, x_ref, *refs):
    ds = refs[:9]
    w_ref, gmid_ref, norm_ref = refs[9:12]
    tg_ref, gg_ref = refs[12 + n_pins :]

    @pl.when(pl.program_id(0) == 0)
    def _():
        gg_ref[...] = jnp.zeros_like(gg_ref)

    d = jnp.concatenate([ds[3 * g + j][...] for j in range(3) for g in range(3)], axis=1)
    dx, dg, db = ln_back(nt(d, w_ref[...]), x_ref[...].astype(f32), norm_ref[0:1, :])
    tg_ref[...] = (gmid_ref[...] + dx).astype(bf16)
    gg_ref[0:1, :] += dg
    gg_ref[1:2, :] += db


def tail_bwd(x, ds, w, gmid, norms, pins, rb=256):
    rows, width = x.shape
    row = lambda n: pl.BlockSpec((rb, n), lambda i: (i, 0))
    full = lambda *s: pl.BlockSpec(s, lambda i: (0,) * len(s))
    once = lambda *s: pl.BlockSpec(s, lambda i: (0,) * len(s), pipeline_mode=pl.Buffered(1))
    return pl.pallas_call(
        functools.partial(tail_kernel, len(pins)),
        grid=(rows // rb,),
        in_specs=[row(width)] + [row(256)] * 9 + [VMEM, row(width), full(16, width)] + [ANY] * len(pins),
        out_specs=[row(width), full(8, width)],
        out_shape=in_hbm([SHAPE((rows, width), bf16), SHAPE((8, width), f32)]),
        compiler_params=params(VMEM_MIB),
        cost_estimate=cost(5, 16),
        name="tail_bwd",
    )(*far(x, *ds), w, *far(gmid, norms), *pins)


def mixed_kernel(n_pins, mid_ref, act_ref, wd_ref, *refs):
    refs[n_pins][...] = (mid_ref[...] + nn(act_ref[...], wd_ref[...])).astype(bf16)


def mixed_out(mid, act, wd, pins, rb=256):
    rows, width = mid.shape
    hidden = act.shape[1]
    row = lambda n: pl.BlockSpec((rb, n), lambda i: (i, 0))
    once = pl.BlockSpec((hidden, width), lambda i: (0, 0), pipeline_mode=pl.Buffered(1))
    return pl.pallas_call(
        functools.partial(mixed_kernel, len(pins)),
        grid=(rows // rb,),
        in_specs=[row(width), row(hidden), VMEM] + [ANY] * len(pins),
        out_specs=row(width),
        out_shape=in_hbm([SHAPE((rows, width), bf16)])[0],
        compiler_params=params(VMEM_MIB),
        cost_estimate=cost(5, 16),
        name="mixed_out",
    )(*far(mid, act), wd, *pins)


def packet_kernel(n_in, *refs):
    ins, out_ref = refs[:n_in], refs[-1]
    col = 0
    for v in ins:
        out_ref[:, col : col + v.shape[1]] = v[...]
        col += v.shape[1]


def packet(arrays, pins, name):
    rows, cols = arrays[0].shape[0], sum(a.shape[1] for a in arrays)
    full = lambda *s: pl.BlockSpec(s, lambda i: (0,) * len(s))
    return pl.pallas_call(
        functools.partial(packet_kernel, len(arrays)),
        grid=(1,),
        in_specs=[full(*a.shape) for a in arrays] + [ANY] * len(pins),
        out_specs=full(rows, cols),
        out_shape=SHAPE((rows, cols), bf16),
        compiler_params=params(8),
        cost_estimate=cost(0, 2),
        name=name,
    )(*arrays, *pins)


def gate(arrays, pins):
    n = len(arrays)
    if not pins:
        return list(arrays)
    return list(pl.pallas_call(
        lambda *refs: None,
        in_specs=[ANY] * (n + len(pins)),
        out_specs=[ANY] * n,
        out_shape=[SHAPE(a.shape, a.dtype) for a in arrays],
        input_output_aliases={i: i for i in range(n)},
        compiler_params=params(1),
        cost_estimate=cost(0, 0),
        name="gate",
    )(*arrays, *pins))


def total(*vs):
    out = vs[0].astype(f32)
    for v in vs[1:]:
        out = out + v.astype(f32)
    return out.astype(bf16)


def combine_kernel(plan, n_in, n_pins, odd_ref, *refs):
    outs = refs[n_in + n_pins :]
    odd = odd_ref[0] == 1
    at = 0
    for f, spots, n_out in plan:
        values = f(odd, *[refs[i] for i in spots])
        for v in values:
            outs[at][...] = v.astype(outs[at].dtype)
            at += 1


def combine(jobs, odd, pins, name, grid=1):
    arrays, shapes, plan = [], [], []
    for f, ins, outs in jobs:
        spots = []
        for a in ins:
            known = [i for i, b in enumerate(arrays) if b is a]
            spots.append(known[0] if known else len(arrays))
            if not known:
                arrays.append(a)
        plan.append((f, spots, len(outs)))
        shapes += [o if isinstance(o, SHAPE) else SHAPE(o, bf16) for o in outs]
    block = lambda s: pl.BlockSpec(s[:-1] + (s[-1] // grid,), lambda i: (0,) * (len(s) - 1) + (i,))
    sums = pl.pallas_call(
        functools.partial(combine_kernel, plan, len(arrays), len(pins)),
        grid=(grid,),
        in_specs=[SMEM] + [block(a.shape) for a in arrays] + [ANY] * len(pins),
        out_specs=[block(s.shape) for s in shapes],
        out_shape=shapes,
        compiler_params=params(24),
        cost_estimate=cost(0, 4),
        name=name,
    )(odd, *arrays, *pins)
    return list(sums)


def swap(v, axis, size, m):
    return lax.ppermute(v, axis, [(i, i ^ m) for i in range(size)])


def part_plan(cut):
    return [(0, 0), (1, 0), (2, 0), (4, 0), (6, 0), (6, cut), (3, 0), (5, 0), (7, 0), (7, cut)]


class Gather:
    def __init__(self, own, cut, size):
        self.own, self.cut, self.size = own, cut, size

    def near(self):
        self.rx, self.ry = (swap(self.own, "fsdp", self.size, m) for m in (2, 4))
        return [self.rx, self.ry]

    def halves(self):
        n, cols = self.own.shape
        return (
            lambda odd, x, y: (y[: self.cut, :], x[self.cut :, :]),
            [self.rx, self.ry],
            [(self.cut, cols), (n - self.cut, cols)],
        )

    def opposite(self, to_x, to_y):
        self.da, self.db = swap(to_x, "fsdp", self.size, 2), swap(to_y, "fsdp", self.size, 4)
        return [self.da, self.db]

    def core_near(self):
        self.rc, *self.near_c = [swap(v, "fsdp", self.size, 1) for v in (self.own, self.rx, self.ry)]

    def parts(self):
        opp = [self.da, self.db]
        return [self.own, self.rc, self.rx, self.ry] + opp + self.near_c + [swap(v, "fsdp", self.size, 1) for v in opp]


class Chain:
    def __init__(self, packets, plan, n_fsdp, n_rep):
        self.mine, self.got = [], []
        self.plan = ("core",) + plan
        self.at = 0
        self.f = lambda v, m: swap(v, "fsdp", n_fsdp, m)
        self.z = lambda v, m: swap(v, "rep", n_rep, m)
        self.join(packets)

    def join(self, packets):
        keep, send = packets
        self.mine.append(keep)
        self.got.append(self.f(send, 1))
        self.shape = (keep.shape[1], sum(k.shape[2] for k in self.mine))

    def job(self):
        done = self.plan[self.at]
        then = self.plan[self.at + 1] if self.at + 1 < len(self.plan) else None
        rows, cols = self.shape
        h = rows // 2
        whole, half = (rows, cols), (h, cols)
        if done == "core" and then == "xy":

            def f(odd, *vs):
                n = len(vs) // 2
                pairs = list(zip(vs[:n], vs[n:]))
                return tuple(jnp.concatenate([total(k[s], g[s]) for k, g in pairs], axis=1) for s in range(4))

            return f, self.mine + self.got, [whole] * 4
        if done == "core":

            def f(odd, k, g):
                part = lambda s, t, lo: jnp.stack([total(k[i, lo : lo + h, :], g[i, lo : lo + h, :]) for i in (s, t)])
                return part(0, 2, 0), part(0, 1, h), part(1, 3, 0), part(2, 3, h)

            return f, self.mine + self.got, [(2,) + half] * 4
        if done == "a":
            f = lambda odd, a, b, ra, rb: (total(a[0], ra[0]), total(b[0], rb[0]), total(a[1], ra[1]), total(b[1], rb[1]))
            return f, self.mine + self.got, [half] * 4
        if done in ("b", "xy"):

            def f(odd, *vs):
                if done == "b":
                    a, b, ra, rb = vs
                    lo, hi = total(a[...], ra[...]), total(b[...], rb[...])
                else:
                    lo, hi = (total(*[v[r, :] for v in vs]) for r in (slice(0, h), slice(h, rows)))
                if then == "p1":
                    return (jnp.concatenate([lo, hi], axis=0),)
                return jnp.where(odd, hi, lo), jnp.where(odd, lo, hi)

            return f, self.mine + self.got, [whole] if then == "p1" else [half] * 2
        if done == "h3":

            def f(odd, p, o):
                p, o = p[...], o[...]
                return (jnp.concatenate([jnp.where(odd, o, p), jnp.where(odd, p, o)], axis=0),)

            return f, self.mine + self.got, [SHAPE(whole, f32)]
        out = half if done[0] == "h" else whole
        return (lambda odd, a, b: (total(a[...], b[...]),)), self.mine + self.got, [out if then else SHAPE(out, f32)]

    def go(self, sums):
        self.at += 1
        step = self.plan[self.at] if self.at < len(self.plan) else None
        if step == "xy":
            self.mine, out = sums[:1], sums[1:]
            self.got = [self.f(v, m) for v, m in zip(out, (2, 4, 6))]
        elif step in ("a", "b"):
            self.mine, out = sums[:2], sums[2:]
            self.got = [self.f(v, m) for v, m in zip(out, (2, 4) if step == "a" else (4, 2))]
        elif step == "h1":
            self.mine, self.got = sums[:1], [self.z(sums[1], 1)]
        else:
            self.mine = sums
            self.got = [self.z(sums[0], 2 if step in ("h2", "p2") else 1)] if step else []


def advance(chains, extra, odd, pins, name, grid=1):
    jobs = [c.job() for c in chains] + extra
    sums = combine(jobs, odd, pins, name, grid)
    at = 0
    for c, job in zip(chains, jobs):
        c.go(sums[at : at + len(job[2])])
        at += len(job[2])
    return sums, sums[at:]


def natural(v, width):
    pairs = width // LANES
    return jnp.concatenate([v[:, LANES * (3 * p + j) :][:, :LANES] for j in range(3) for p in range(pairs)], axis=1)


def last_job(cq, cr):
    rows, cols = cq.shape
    width = cr.shape[1]

    def f(odd, p, o, a, b):
        p, o = p[...], o[...]
        q = jnp.concatenate([jnp.where(odd, o, p), jnp.where(odd, p, o)], axis=0)
        return q[:, :width], natural(jnp.concatenate([q[:, width:], total(a[...], b[...])], axis=1), width)

    return f, cq.mine + cq.got + cr.mine + cr.got, [SHAPE((rows, width), f32), SHAPE((rows, cols), f32)]


def sum_chips(v, size):
    x, y, d = (swap(v, "fsdp", size, m) for m in (2, 4, 6))
    return (v + x) + (y + d)


def sum_replicas(v, size):
    a, b, c = (swap(v, "rep", size, m) for m in (1, 2, 3))
    return (v + a) + (b + c)


def whole(keep, send):
    return jnp.stack([keep, send], axis=1).reshape(-1, keep.shape[2])


def shards(
    n_fsdp, n_rep, tokens, bucket, ln1_gain, ln1_bias, w_qkv, w_out, ln2_gain, ln2_bias, w_up, w_down, cotangent
):
    width = tokens.shape[1]
    fast = n_fsdp == 8 and n_rep == 4
    index = lax.axis_index("fsdp")
    vectors = jnp.stack([ln1_gain, ln1_bias, ln2_gain, ln2_bias])
    if fast:
        me = jnp.reshape(index, (1,)).astype(jnp.int32)
        owner = lax.broadcasted_iota(jnp.int32, (4, width), 1) // (width // 8)
        spread = jnp.where(owner == index, jnp.tile(vectors, (1, 8)), 0)
    else:
        me = jnp.zeros((1,), jnp.int32)
        spread = lax.all_gather(vectors, "fsdp", axis=1, tiled=True)
        w_qkv, w_out, w_up, w_down = (
            lax.all_gather(w, "fsdp", axis=0, tiled=True) for w in (w_qkv, w_out, w_up, w_down)
        )
    local = w_qkv.shape[0]
    norm_rows = jnp.pad(spread, ((0, 12), (0, w_qkv.shape[1] - width)))
    packet_q = jnp.concatenate([w_qkv, norm_rows], axis=0)
    cut, cut_d = local // 2, w_down.shape[0] // 2
    none = [(0, 0)]
    odd = jnp.reshape(lax.axis_index("rep") & 1, (1,)).astype(jnp.int32)

    if fast:
        gq = Gather(packet_q, cut, n_fsdp)
        gq.near()
        far_q = gq.opposite(gq.ry[:cut], gq.rx[cut:])
        gq.core_near()
        (own_u,) = gate([packet([w_out, w_up], [], "packet_up")], far_q + [gq.rc] + gq.near_c)
        gu = Gather(own_u, cut, n_fsdp)
        near_u = gu.near()
        gd = Gather(None, cut_d, n_fsdp)
        plan, plan_d = part_plan(cut), part_plan(cut_d)
        parts_q = gq.parts()
    else:
        plan, plan_d = none, none
        parts_q = [packet_q]

    def pin(v):
        return list(v) if fast else []

    n1, n1t, norms, w_full, *heads0 = forward_first(
        bucket, me, tokens, parts_q, plan, local, pin([own_u] if fast else [])
    )
    sums = []
    if fast:
        sums, (to_x, to_y, own_d) = advance(
            [], [gu.halves(), (lambda o, w: (w[...],), [w_down], [w_down.shape])], odd, far(n1t), "after_a"
        )
        gu.opposite(to_x, to_y)
        gu.rx, gu.ry = gate([gu.rx, gu.ry], far(n1t))
        (gu.own,) = gate([gu.own], far(n1t))
        gu.core_near()
    heads1 = forward_next(1, bucket, n1, w_full, pin(sums))
    sums = []
    if fast:
        gu.da, gu.db, gd.own, gu.rc, *gu.near_c = gate([gu.da, gu.db, own_d, gu.rc] + gu.near_c, far(heads1[3]))
        sums = [gd.own]
        gd.near()
        parts_u = gu.parts()
    heads2 = forward_next(2, bucket, n1, w_full, pin(sums))
    heads = [heads0, heads1, heads2]
    atts = [h[3] for h in heads]
    if fast:
        sums, (to_x, to_y) = advance([], [gd.halves()], odd, far(heads2[3]), "after_c")
        gd.opposite(to_x, to_y)
        gd.core_near()
    else:
        parts_u = [packet([w_out, w_up], [], "packet_up")]
    mid, n2t, act, gp, w_ou = up_proj(me, tokens, atts, norms, parts_u, plan, local, pin(sums))
    if fast:
        gd.da, gd.db = gate([gd.da, gd.db], far(n2t))
        parts_d = gd.parts()
    else:
        parts_d = [w_down]
    send_d = wdown_grad(me, act, cotangent, 1, pin([gd.da, gd.db] if fast else []))
    halves, direct = ("a", "b", "h1", "h2", "h3"), ("xy", "p1", "p2")
    chain = lambda pk, plan: Chain(pk, plan, n_fsdp, n_rep) if fast else None

    def step(chains, after, name):
        return advance(chains, [], odd, after, name)[0][-1:] if fast else []

    if fast:
        (send_d,) = gate([send_d], parts_d)
    pk_d = [wdown_grad(me, act, cotangent, 0, pin([send_d])), send_d]
    cd = chain(pk_d, halves)
    sums = step([cd], [], "after_wdown")
    gup, *pk_u, w_dn = hidden_bwd(me, cotangent, gp, n2t, parts_d, plan_d, w_down.shape[0], pin(sums))
    sums = step([cd], far(gup), "after_hidden")
    if fast:
        pk_u = [pk_u[0]] + gate([pk_u[1]], sums)
    cu = chain(pk_u, halves)
    gmid, gatt, g_norm2, *pk_q = mid_bwd(me, cotangent, gup, mid, norms, w_ou, atts, pin(sums))
    sums = step([cd, cu], far(g_norm2), "after_mid")
    *d0, k, s = attn_bwd(0, bucket, me, heads[0], gatt, n1t, pk_q, 2, pin(sums))
    sums = step([cd, cu], far(d0[0]), "after_bwd0")
    pk_q = [k] + (gate([s], sums) if fast else [s])
    cq = chain(pk_q, ("xy", "h1", "h2", "h3"))
    *d1, k, s = attn_bwd(1, bucket, me, heads[1], gatt, n1t, None, 0, pin(sums))
    s0 = step([cd, cu], far(d1[0]), "after_bwd1")
    pk_1 = [k] + (gate([s], s0) if fast else [s])
    if fast:
        cq.join(pk_1)
    sums = step([cq], s0, "after_bwd1_q")
    *d2, k, s = attn_bwd(2, bucket, me, heads[2], gatt, n1t, None, 0, pin(s0 + sums))
    s0 = step([cd, cu, cq], far(d2[0]), "after_bwd2")
    pk_r = [k] + (gate([s], s0) if fast else [s])
    cr = chain(pk_r, direct)
    sums = step([cr], s0, "after_bwd2_r")
    tokens_grad, g_norm1 = tail_bwd(tokens, d0 + d1 + d2, w_full, gmid, norms, pin(s0 + sums))
    sums = step([cu, cq, cr], far(g_norm1), "after_tail")
    g_norms = jnp.concatenate([g_norm1[:2], g_norm2[:2]], axis=0)
    if fast:
        (g_norms,) = gate([g_norms], sums)
        g_norms_c = swap(g_norms, "fsdp", n_fsdp, 1)
    mixed = mixed_out(mid, act, w_dn, pin(sums))
    sums = step([cu, cq, cr], far(mixed), "after_mixed")
    if fast:
        (g_norms,) = gate([g_norms], sums)
        g_norms = sum_chips(g_norms + g_norms_c, n_fsdp)
    if fast:
        (g_norms,) = gate([g_norms], cq.got)
        g_norms = sum_replicas(g_norms, n_rep)
    if fast:
        gw_out, gw_q = combine([last_job(cq, cr)], odd, [], "last")

    if fast:
        (rows_d,), (rows_u,) = (c.mine for c in (cd, cu))
    else:
        g_norms = lax.psum(g_norms, ("fsdp", "rep"))
        rows_q, rows_1, rows_r, rows_u, rows_d = (whole(*pk) for pk in (pk_q, pk_1, pk_r, pk_u, pk_d))
        rows_q = jnp.concatenate([rows_q, rows_1], axis=1)
        gw_out = rows_q[:, :width]
        gw_q = natural(jnp.concatenate([rows_q[:, width:], rows_r], axis=1), width)
    g_norms = lax.dynamic_slice_in_dim(g_norms, index * (width // n_fsdp), width // n_fsdp, axis=1)
    grads = (gw_q, gw_out, rows_u, rows_d)
    if not fast:
        grads = tuple(
            lax.psum(lax.psum_scatter(g, "fsdp", scatter_dimension=0, tiled=True), "rep") for g in grads
        )
    gw_qkv, gw_out, gw_up, gw_down = (g.astype(f32) for g in grads)
    return (
        mixed,
        tokens_grad,
        g_norms[0],
        g_norms[1],
        gw_qkv,
        gw_out,
        g_norms[2],
        g_norms[3],
        gw_up,
        gw_down,
    )


def solution(mesh):
    return jax.shard_map(
        functools.partial(shards, mesh.shape["fsdp"], mesh.shape["rep"]),
        mesh=mesh,
        in_specs=(
            P(("rep", "fsdp"), None),
            P(("rep", "fsdp")),
            P("fsdp"),
            P("fsdp"),
            P("fsdp", None),
            P("fsdp", None),
            P("fsdp"),
            P("fsdp"),
            P("fsdp", None),
            P("fsdp", None),
            P(("rep", "fsdp"), None),
        ),
        out_specs=(
            P(("rep", "fsdp"), None),
            P(("rep", "fsdp"), None),
            P("fsdp"),
            P("fsdp"),
            P("fsdp", None),
            P("fsdp", None),
            P("fsdp"),
            P("fsdp"),
            P("fsdp", None),
            P("fsdp", None),
        ),
        check_vma=False,
    )
```
